256 devices in a mesh: depth: 2 (over core), row: 16 (over x, y), col: 8 (over z).
Axes of the slice: x: 4, y: 4, z: 8, core: 2. Of those that a mesh axis runs over, the one named last changes fastest.
Arguments:
- queries: bfloat16 [16, 256, 8192], P('row', 'depth', 'col'), may hold values from -35 to 35
- key_states: bfloat16 [16, 256, 1024], P('row', 'depth', 'col'), may hold values from -6 to 6
- value_states: bfloat16 [16, 256, 1024], P('row', 'depth', 'col'), may hold values from -8 to 8
- residual: bfloat16 [16, 256, 8192], P('col', 'depth', 'row'), may hold values from -300 to 300
- gain: float32 [8192], P('row'), may hold values from 0.1 to 1.9
- w_out: bfloat16 [8192, 8192], P('col', 'row'), may hold values from -0.0625 to 0.0625
- w_gate: bfloat16 [8192, 14336], P('row', 'col'), may hold values from -0.0625 to 0.0625
- w_up: bfloat16 [8192, 14336], P('row', 'col'), may hold values from -0.0625 to 0.0625
Outputs:
- hidden: bfloat16 [16, 256, 14336], P('row', 'depth', 'col')
- stream: bfloat16 [16, 256, 8192], P('col', 'depth', 'row')
The draws below stay inside these ranges and needn't reach their ends.
All inputs are finite; a program needn't handle non-finite values.
Results may differ from the reference program's by a relative error of at most 0.03.
Values may be sent and summed in bfloat16 or wider, within the bound.
No kernel may reach another device: no remote copies, remote signals or barrier semaphores. Data moves between devices by JAX's collectives and lax.ppermute only.
A program may use at most 64 MiB of HBM per device.

```python
import math
import jax
import jax.numpy as jnp
from jax import lax

D = 8192
H = 64
KVH = 8
DH = 128
FF = 14336
L = 256
SEQS = 16


def common_keys(key):
    base_key = jax.random.fold_in(key, 101)
    first_key = jax.random.fold_in(base_key, 0)
    shape = (SEQS, L, KVH * DH)
    normal_base = jnp.clip(jax.random.normal(first_key, shape, jnp.float32), -6.0, 6.0)
    return normal_base


def draw_key_states(key, part):
    normal_base = common_keys(key)
    return normal_base.astype(jnp.bfloat16)


def draw_queries(key, part):
    key = jax.random.fold_in(key, 7)
    first_key = jax.random.fold_in(key, 0)
    values = jax.random.normal(first_key, (SEQS, L, H * DH), jnp.float32)
    return jnp.clip(values, -6.0, 6.0).astype(jnp.bfloat16)


def draw_residual(key, part):
    key = jax.random.fold_in(key, 11)
    col_key, row_key, cell_key = jax.random.split(key, 3)
    spread = jax.random.uniform(col_key, (D,), jnp.float32)
    along = jnp.arange(D).astype(jnp.float32) / D
    row_level = jax.random.uniform(row_key, (SEQS, L, 1), jnp.float32)
    row_scale = jnp.exp((row_level - 0.5) * math.log(10.0))
    col_scale = 0.15 * jnp.exp(spread * math.log(10.0) + along * math.log(3.0))
    cells = jnp.clip(jax.random.normal(cell_key, (SEQS, L, D), jnp.float32), -6.0, 6.0)
    return (row_scale * col_scale * cells).astype(jnp.bfloat16)


def shard_levels(key, shape, shards, least, high):
    def one(dim, blocks):
        heights = jax.random.uniform(jax.random.fold_in(jax.random.fold_in(key, 6), dim), (blocks,), jnp.float32, least / len(shards), high / len(shards))
        return jnp.repeat(jnp.exp(heights), shape[dim] // blocks).reshape((-1,) + (1,) * (len(shape) - dim - 1))

    loudness = one(*shards[0])
    for cut in shards[1:]:
        loudness = loudness * one(*cut)
    return loudness


def bell_draw(own_key, shape, width, most, pieces=(), held_as=jnp.bfloat16):
    level = shard_levels(own_key, shape, pieces, -0.22, 0.18) if pieces else 1.0
    drawn = jax.random.normal(own_key, shape, jnp.float32) * width * level
    return jnp.minimum(jnp.maximum(drawn, -most), most).astype(held_as)


def setup_inputs(seed: int = 0) -> dict:
    arg_keys = jax.random.split(jax.random.key(seed), 9)
    queries = draw_queries(jax.random.fold_in(arg_keys[8], 71), 0)
    key_states = draw_key_states(jax.random.fold_in(arg_keys[8], 71), 0)
    value_states = bell_draw(arg_keys[2], (SEQS, L, KVH * DH), 2.0, 8.0, ((0, 16), (1, 2), (2, 8)))
    residual = draw_residual(jax.random.fold_in(arg_keys[8], 71), 0)
    gain = jnp.clip(1.0 + 0.18 * jax.random.normal(arg_keys[4], (D,), jnp.float32), 0.1, 1.9)
    w_out = bell_draw(arg_keys[5], (H * DH, D), (H * DH) ** -0.5, 0.0625, ((0, 8), (1, 16)))
    w_gate = bell_draw(arg_keys[6], (D, FF), D ** -0.5, 0.0625, ((0, 16), (1, 8)))
    w_up = bell_draw(arg_keys[7], (D, FF), D ** -0.5, 0.0625, ((0, 16), (1, 8)))
    return {"queries": queries, "key_states": key_states, "value_states": value_states, "residual": residual, "gain": gain, "w_out": w_out, "w_gate": w_gate, "w_up": w_up}


eps_norm = 1e-05
masked_score = -1e+30

def attend(triple):
    queries, keys, values = triple
    length = queries.shape[0]
    grouped = queries.astype(jnp.float32).reshape(length, KVH, H // KVH, DH)
    keyed = keys.astype(jnp.float32).reshape(length, KVH, DH)
    valued = values.astype(jnp.float32).reshape(length, KVH, DH)
    scores = jnp.einsum('tgid,ugd->gitu', grouped, keyed) * DH ** (-0.5)
    allowed = jnp.arange(length)[None, :] <= jnp.arange(length)[:, None]
    scores = jnp.where(allowed, scores, masked_score)
    top = lax.optimization_barrier(jnp.max(scores, axis=-1, keepdims=True))
    expo = jnp.exp(scores - top)
    totals = lax.optimization_barrier(jnp.sum(expo, axis=-1))
    probs = lax.optimization_barrier(expo.astype(jnp.bfloat16)).astype(jnp.float32)
    mixed = jnp.einsum('gitu,ugd->tgid', probs, valued)
    mixed = mixed / jnp.transpose(totals, (2, 0, 1))[..., None]
    return mixed.astype(jnp.bfloat16).reshape(length, H * DH)

def reference(queries, key_states, value_states, residual, gain, w_out, w_gate, w_up):
    seq_count, length, features = queries.shape
    attended = lax.map(attend, (queries, key_states, value_states))
    projected = jnp.dot(attended.reshape(-1, features), w_out, preferred_element_type=jnp.float32)
    stream = (residual.astype(jnp.float32) + projected.reshape(seq_count, length, D)).astype(jnp.bfloat16)
    wide = stream.astype(jnp.float32)
    inverse = lax.rsqrt(lax.optimization_barrier(jnp.sum(wide * wide, axis=-1)) / D + eps_norm)
    scaled = (wide * gain).astype(jnp.bfloat16).reshape(-1, D)
    block = D // SEQS
    gate_sum = jnp.zeros((seq_count * length, FF), jnp.float32)
    up_sum = jnp.zeros((seq_count * length, FF), jnp.float32)
    for block_index in range(SEQS):
        piece = scaled[:, block_index * block:(block_index + 1) * block]
        gate_part = jnp.dot(piece, w_gate[block_index * block:(block_index + 1) * block], preferred_element_type=jnp.float32)
        up_part = jnp.dot(piece, w_up[block_index * block:(block_index + 1) * block], preferred_element_type=jnp.float32)
        gate_sum = gate_sum + lax.optimization_barrier(gate_part.astype(jnp.bfloat16)).astype(jnp.float32)
        up_sum = up_sum + lax.optimization_barrier(up_part.astype(jnp.bfloat16)).astype(jnp.float32)
    factor = inverse.reshape(-1, 1)
    hidden = (jax.nn.silu(gate_sum * factor) * (up_sum * factor)).astype(jnp.bfloat16)
    return (hidden.reshape(seq_count, length, FF), stream)
```

```python
import jax
import jax.numpy as jnp
from jax import lax
from jax.sharding import Mesh, PartitionSpec as P

D = 8192
H = 64
KVH = 8
DH = 128
NX = 4
NY = 4
NZ = 8

eps_norm = 1e-05
masked_score = -1e30
bf16 = jnp.bfloat16
f32 = jnp.float32


def shift(value, axis, size, by):
    return lax.ppermute(value, axis, [(i, (i + by) % size) for i in range(size)])


def attend_local(queries, keys_all, values_all):
    half = queries.shape[1]
    length = keys_all.shape[1]
    kv_local = keys_all.shape[2] // DH
    grouped = queries.reshape(half, kv_local, H // KVH, DH)
    keyed = keys_all.reshape(length, kv_local, DH)
    valued = values_all.reshape(length, kv_local, DH)
    scores = jnp.einsum(
        "tgid,ugd->gitu", grouped, keyed, preferred_element_type=f32
    ) * DH ** (-0.5)
    positions = lax.axis_index("depth") * half + jnp.arange(half)
    allowed = jnp.arange(length)[None, :] <= positions[:, None]
    scores = jnp.where(allowed, scores, masked_score)
    top = jnp.max(scores, axis=-1, keepdims=True)
    expo = jnp.exp(scores - top)
    totals = jnp.sum(expo, axis=-1)
    probs = expo.astype(bf16)
    mixed = jnp.einsum("gitu,ugd->tgid", probs, valued, preferred_element_type=f32)
    mixed = mixed / jnp.transpose(totals, (2, 0, 1))[..., None]
    return mixed.astype(bf16).reshape(half, queries.shape[2])


def reduce_scatter_z(parts):
    z = lax.axis_index("col")
    rows = parts.shape[1]
    cut = rows // 2

    def part(offset, low):
        block = lax.dynamic_slice(
            parts, ((z + offset + NZ) % NZ, low, 0), (1, cut, parts.shape[2])
        )
        return block[0].astype(f32)

    right_a = part(4, 0).astype(bf16)
    left_b = part(-4, cut).astype(bf16)
    right_a = shift(right_a, "col", NZ, 1)
    left_b = shift(left_b, "col", NZ, -1)
    right_b = shift(part(3, cut).astype(bf16), "col", NZ, 1)
    left_a = shift(part(-3, 0).astype(bf16), "col", NZ, -1)
    for step, offset in enumerate((3, 2, 1)):
        right_a = shift((right_a.astype(f32) + part(offset, 0)).astype(bf16), "col", NZ, 1)
        left_b = shift((left_b.astype(f32) + part(-offset, cut)).astype(bf16), "col", NZ, -1)
        if step > 0:
            right_b = shift((right_b.astype(f32) + part(offset, cut)).astype(bf16), "col", NZ, 1)
            left_a = shift((left_a.astype(f32) + part(-offset, 0)).astype(bf16), "col", NZ, -1)
    total_a = part(0, 0) + right_a.astype(f32) + left_a.astype(f32)
    total_b = part(0, cut) + right_b.astype(f32) + left_b.astype(f32)
    return jnp.concatenate([total_a, total_b], axis=0)


def all_gather_z(block):
    cut = block.shape[0] // 2
    right = [block]
    left = [block]
    for _ in range(3):
        right.append(shift(right[-1], "col", NZ, 1))
        left.append(shift(left[-1], "col", NZ, -1))
    far_a = shift(right[3][:cut], "col", NZ, 1)
    far_b = shift(left[3][cut:], "col", NZ, -1)
    far = jnp.concatenate([far_a, far_b], axis=0)
    return [block, left[1], left[2], left[3], far, right[3], right[2], right[1]]


def natural_to_work(h):
    pairs = []
    for x in range(NX):
        for y in range(NY):
            for high in range(2):
                for low in range(4):
                    seq = 4 * x + (y + 2 * high + h) % 4
                    there = (low * NY + y) * NZ + seq // 2
                    here = (x * NY + y) * NZ + high * 4 + low
                    pairs.append((there, here))
    return pairs


def per_device(queries, key_states, value_states, residual, gain, w_out, w_gate, w_up):
    half = queries.shape[1]
    depth = lax.axis_index("depth")
    y = lax.axis_index("y")
    z = lax.axis_index("col")
    odd = (y % 2) == 1

    out_rows = w_out.shape[0] // 2
    wo_half = lax.dynamic_slice_in_dim(w_out, depth * out_rows, out_rows, 0)
    wo_own = lax.all_gather(wo_half, "x", axis=0)
    wo_other = shift(wo_own, "depth", 2, 1)
    units = w_gate.shape[1] // 2
    scaled_gate = lax.dynamic_slice_in_dim(w_gate, depth * units, units, 1).astype(f32) * gain[:, None]
    scaled_up = lax.dynamic_slice_in_dim(w_up, depth * units, units, 1).astype(f32) * gain[:, None]
    w2_half = jnp.concatenate([scaled_gate, scaled_up], axis=1).astype(bf16)
    w2_own = lax.all_gather(w2_half, "x", axis=0, tiled=True)
    w2_other = shift(w2_own, "depth", 2, 1)

    res_first = jnp.where(odd, residual[1], residual[0])
    res_second = jnp.where(odd, residual[0], residual[1])
    axes = ("x", "y", "col")
    res_work = jnp.concatenate(
        [
            lax.ppermute(res_first, axes, natural_to_work(0)),
            lax.ppermute(res_second, axes, natural_to_work(1)),
        ],
        axis=0,
    )

    keys_all = lax.all_gather(key_states, "depth", axis=1, tiled=True)
    values_all = lax.all_gather(value_states, "depth", axis=1, tiled=True)
    attended = attend_local(queries, keys_all, values_all)
    four = jnp.stack(
        [
            attended,
            shift(attended, "y", NY, -1),
            shift(attended, "y", NY, 2),
            shift(attended, "y", NY, 1),
        ]
    )
    flat = four.reshape(NY * half, four.shape[2])
    flat_own = lax.dynamic_slice_in_dim(flat, depth * out_rows, out_rows, 1)
    flat_other = lax.dynamic_slice_in_dim(flat, (1 - depth) * out_rows, out_rows, 1)
    partial = jnp.einsum("tk,xkf->xtf", flat_own, wo_own, preferred_element_type=f32)
    partial = partial + jnp.einsum("tk,xkf->xtf", flat_other, wo_other, preferred_element_type=f32)
    block = w_out.shape[1]
    parts = partial.reshape(NX, 2, 2 * half, block).transpose(1, 0, 2, 3).reshape(NZ, 2 * half, block)
    projected = reduce_scatter_z(parts.astype(bf16))
    stream = (res_work.astype(f32) + projected).astype(bf16)

    work_to_natural = [[(b, a) for a, b in natural_to_work(h)] for h in range(2)]
    back_first = lax.ppermute(stream[:half], axes, work_to_natural[0])
    back_second = lax.ppermute(stream[half:], axes, work_to_natural[1])
    stream_out = jnp.stack(
        [jnp.where(odd, back_second, back_first), jnp.where(odd, back_first, back_second)]
    )

    ring = jnp.stack(all_gather_z(stream))
    ring = jnp.roll(ring, z, axis=0)
    tokens = (
        ring.reshape(2, NX, 2 * half, block).transpose(0, 2, 1, 3).reshape(NY, half, NX * block)
    )
    wide = tokens.astype(f32)
    squares = jnp.sum(wide * wide, axis=-1)
    square_total = (
        squares[0]
        + shift(squares[1], "y", NY, 1)
        + shift(squares[2], "y", NY, 2)
        + shift(squares[3], "y", NY, -1)
    )
    inverse = lax.rsqrt(square_total / D + eps_norm)[:, None]

    def product(k, weights):
        return jnp.dot(tokens[k], weights, preferred_element_type=f32)

    far_own = shift(product(2, w2_own).astype(bf16), "y", NY, 1)
    far_other = shift(product(2, w2_other).astype(bf16), "y", NY, -1)
    right_other = shift(product(1, w2_other).astype(bf16), "y", NY, 1)
    left_own = shift(product(3, w2_own).astype(bf16), "y", NY, -1)
    right_own = shift((product(1, w2_own) + far_own.astype(f32)).astype(bf16), "y", NY, 1)
    left_other = shift((product(3, w2_other) + far_other.astype(f32)).astype(bf16), "y", NY, -1)
    sum_own = product(0, w2_own) + right_own.astype(f32) + left_own.astype(f32)
    sum_other = product(0, w2_other) + right_other.astype(f32) + left_other.astype(f32)

    def activate(total):
        total = total * inverse
        return (jax.nn.silu(total[:, :units]) * total[:, units:]).astype(bf16)

    own = activate(sum_own)
    other = activate(sum_other)
    hidden = jnp.where(
        depth == 0,
        jnp.concatenate([own, other], axis=1),
        jnp.concatenate([other, own], axis=1),
    )
    return (hidden[None], stream_out)


def solution(mesh):
    fine = Mesh(mesh.devices.reshape(2, NX, NY, NZ), ("depth", "x", "y", "col"))
    row = ("x", "y")
    return jax.shard_map(
        per_device,
        mesh=fine,
        in_specs=(
            P(row, "depth", "col"),
            P(row, "depth", "col"),
            P(row, "depth", "col"),
            P("col", "depth", row),
            P(row),
            P("col", row),
            P(row, "col"),
            P(row, "col"),
        ),
        out_specs=(P(row, "depth", "col"), P("col", "depth", row)),
        check_vma=False,
    )
```

```python
import functools
import jax
import jax.numpy as jnp
from jax import lax
from jax.experimental import pallas as pl
from jax.experimental.pallas import tpu as pltpu
from jax.sharding import Mesh, PartitionSpec as P

D = 8192
DH = 128
GROUP = 8
NX = 4
NY = 4
NZ = 8

eps_norm = 1e-05
masked_score = -1e30
bf16 = jnp.bfloat16
f32 = jnp.float32
VMEM_BYTES = 48 * 1024 * 1024


def shift(value, axis, size, by):
    return lax.ppermute(value, axis, [(i, (i + by) % size) for i in range(size)])


def swap(value):
    return shift(value, "depth", 2, 1)


def attend_kernel(where_ref, q_ref, kv_ref, out_ref):
    depth = where_ref[0]
    half = q_ref.shape[0]
    keys = jnp.concatenate([kv_ref[0, :, :DH], kv_ref[1, :, :DH]], axis=0)
    values = jnp.concatenate([kv_ref[0, :, DH:], kv_ref[1, :, DH:]], axis=0)
    rows = jnp.concatenate([q_ref[:, h * DH : (h + 1) * DH] for h in range(GROUP)], axis=0)
    scores = lax.dot_general(
        rows, keys, (((1,), (1,)), ((), ())), preferred_element_type=f32
    ) * DH ** (-0.5)
    shape = scores.shape
    position = lax.broadcasted_iota(jnp.int32, shape, 0) % half + depth * half
    allowed = lax.broadcasted_iota(jnp.int32, shape, 1) <= position
    scores = jnp.where(allowed, scores, masked_score)
    top = jnp.max(scores, axis=-1, keepdims=True)
    expo = jnp.exp(scores - top)
    totals = jnp.sum(expo, axis=-1, keepdims=True)
    mixed = jnp.dot(expo.astype(bf16), values, preferred_element_type=f32) / totals
    mixed = mixed.astype(bf16)
    for h in range(GROUP):
        out_ref[:, h * DH : (h + 1) * DH] = mixed[h * half : (h + 1) * half]


def attend(where, queries, kv):
    half, features = queries.shape
    length = 2 * half
    return pl.pallas_call(
        attend_kernel,
        in_specs=[pl.BlockSpec(memory_space=pltpu.SMEM)]
        + [pl.BlockSpec(memory_space=pltpu.VMEM)] * 2,
        out_specs=pl.BlockSpec(memory_space=pltpu.VMEM),
        out_shape=jax.ShapeDtypeStruct((half, features), bf16),
        compiler_params=pltpu.CompilerParams(vmem_limit_bytes=VMEM_BYTES),
        cost_estimate=pl.CostEstimate(
            flops=4 * half * features * length,
            bytes_accessed=4 * half * features,
            transcendentals=half * GROUP * length,
        ),
    )(where, queries, kv)


def out_kernel(where_ref, *refs):
    att, weights, out_ref = refs[:NY], refs[NY:-1], refs[-1]
    depth, x = where_ref[0], where_ref[1]
    rows, features = att[0].shape
    cut = features // 2
    mine = pl.ds(pl.multiple_of(depth * cut, cut), cut)
    theirs = pl.ds(pl.multiple_of((1 - depth) * cut, cut), cut)
    all_full = jnp.concatenate([ref[...] for ref in att], axis=0)
    all_mine = jnp.concatenate([ref[:, mine] for ref in att], axis=0)
    all_theirs = jnp.concatenate([ref[:, theirs] for ref in att], axis=0)
    for j in range(NX):
        if j == 0:
            total = jnp.dot(all_full, weights[0][...], preferred_element_type=f32)
        else:
            total = jnp.dot(all_mine, weights[j][...], preferred_element_type=f32)
            total += jnp.dot(all_theirs, weights[j + NX - 1][...], preferred_element_type=f32)
        total = total.astype(bf16)
        place = (x + j) % NX
        out_ref[place] = total[: 2 * rows]
        out_ref[place + NX] = total[2 * rows :]


def out_project(where, attended, w_out, own, other):
    rows, features = attended[0].shape
    width = w_out.shape[1]
    operands = [*attended, w_out, *own, *other]
    return pl.pallas_call(
        out_kernel,
        in_specs=[pl.BlockSpec(memory_space=pltpu.SMEM)]
        + [pl.BlockSpec(memory_space=pltpu.VMEM)] * len(operands),
        out_specs=pl.BlockSpec(memory_space=pltpu.VMEM),
        out_shape=jax.ShapeDtypeStruct((2 * NX, 2 * rows, width), bf16),
        compiler_params=pltpu.CompilerParams(vmem_limit_bytes=VMEM_BYTES),
        cost_estimate=pl.CostEstimate(
            flops=2 * NY * rows * features * NX * width,
            bytes_accessed=2 * (NY * rows * features + NX * features * width + 4 * NX * rows * width),
            transcendentals=0,
        ),
    )(where, *operands)


def gate_kernel(seqs, where_ref, *refs):
    own, other = refs[:NZ], refs[NZ : 2 * NZ]
    weight_ref = refs[2 * NZ]
    outs, total_ref = refs[2 * NZ + 1 : -1], refs[-1]
    step = pl.program_id(0)
    z = where_ref[2]
    rows = own[0].shape[0]
    for j in range(NX):

        @pl.when(step == j)
        def _():
            near_is_first = (z + j) % NZ < NX
            for i, k in enumerate(seqs):
                use_near = near_is_first if k < 2 else jnp.logical_not(near_is_first)
                own_rows = jnp.where(use_near, own[j][...], own[j + NX][...])
                other_rows = jnp.where(use_near, other[j][...], other[j + NX][...])
                both = jnp.concatenate([own_rows, other_rows], axis=0)
                add = jnp.dot(both, weight_ref[...], preferred_element_type=f32)
                if j > 0:
                    add = total_ref[i] + add
                if j < NX - 1:
                    total_ref[i] = add
                else:
                    outs[2 * i][...] = add[:rows].astype(bf16)
                    outs[2 * i + 1][...] = add[rows:].astype(bf16)


def gate_products(seqs, where, own, other, weights):
    rows = own[0].shape[0] // 2
    block = own[0].shape[1]
    width = weights.shape[1]
    place = seqs[0] % 2
    spec = pl.BlockSpec((rows, block), lambda j, where: (place, 0))
    return pl.pallas_call(
        functools.partial(gate_kernel, seqs),
        grid_spec=pltpu.PrefetchScalarGridSpec(
            num_scalar_prefetch=1,
            grid=(NX,),
            in_specs=[spec] * (2 * NZ)
            + [pl.BlockSpec((block, width), lambda j, where: ((where[2] + j) % NX, 0))],
            out_specs=[pl.BlockSpec((rows, width), lambda j, where: (0, 0))] * (2 * len(seqs)),
            scratch_shapes=[pltpu.VMEM((len(seqs), 2 * rows, width), f32)],
        ),
        out_shape=[jax.ShapeDtypeStruct((rows, width), bf16)] * (2 * len(seqs)),
        compiler_params=pltpu.CompilerParams(vmem_limit_bytes=VMEM_BYTES),
        cost_estimate=pl.CostEstimate(
            flops=4 * len(seqs) * rows * NX * block * width,
            bytes_accessed=2 * NX * block * width + 4 * NZ * rows * block,
            transcendentals=0,
        ),
    )(where, *own, *other, weights)


def reduce_scatter_z(parts):
    z = lax.axis_index("col")
    rows = parts.shape[1]
    cut = rows // 2

    def part(offset):
        return lax.dynamic_index_in_dim(parts, (z + offset + NZ) % NZ, 0, keepdims=False)

    right = shift(part(4)[:cut], "col", NZ, 1)
    left = shift(part(-4)[cut:], "col", NZ, -1)
    first, second = part(3), part(-3)
    right = jnp.concatenate(
        [(right.astype(f32) + first[:cut].astype(f32)).astype(bf16), first[cut:]], axis=0
    )
    left = jnp.concatenate(
        [second[:cut], (left.astype(f32) + second[cut:].astype(f32)).astype(bf16)], axis=0
    )
    right = shift(right, "col", NZ, 1)
    left = shift(left, "col", NZ, -1)
    for offset in (2, 1):
        right = shift((right.astype(f32) + part(offset).astype(f32)).astype(bf16), "col", NZ, 1)
        left = shift((left.astype(f32) + part(-offset).astype(f32)).astype(bf16), "col", NZ, -1)
    return part(0).astype(f32) + right.astype(f32) + left.astype(f32)


def all_gather_z(block):
    cut = block.shape[0] // 2
    right = [block]
    left = [block]
    for _ in range(3):
        right.append(shift(right[-1], "col", NZ, 1))
        left.append(shift(left[-1], "col", NZ, -1))
    far_a = shift(right[3][:cut], "col", NZ, 1)
    far_b = shift(left[3][cut:], "col", NZ, -1)
    far = jnp.concatenate([far_a, far_b], axis=0)
    return [block, left[1], left[2], left[3], far, right[3], right[2], right[1]]


def natural_to_work(h):
    pairs = []
    for x in range(NX):
        for y in range(NY):
            for high in range(2):
                for low in range(4):
                    seq = 4 * x + (y + 2 * high + h) % 4
                    there = (low * NY + y) * NZ + seq // 2
                    here = (x * NY + y) * NZ + high * 4 + low
                    pairs.append((there, here))
    return pairs


def square_sums(blocks, z):
    sums = []
    for block in blocks:
        wide = block.astype(f32)
        sums.append(jnp.sum(wide * wide, axis=-1))
    low = sums[0]
    sums = jnp.roll(jnp.stack(sums), z, axis=0)
    return jnp.sum(sums.reshape(2, NX, low.shape[0]), axis=1).reshape(NY, low.shape[0] // 2)


def per_device(queries, key_states, value_states, residual, gain, w_out, w_gate, w_up):
    half = queries.shape[1]
    depth = lax.axis_index("depth")
    x = lax.axis_index("x")
    y = lax.axis_index("y")
    z = lax.axis_index("col")
    odd = (y % 2) == 1
    where = jnp.stack([depth, x, z]).astype(jnp.int32)

    out_rows = w_out.shape[0] // 2
    wo_half = lax.dynamic_slice_in_dim(w_out, depth * out_rows, out_rows, 0)
    wo_own = [shift(wo_half, "x", NX, -1), shift(wo_half, "x", NX, 2), shift(wo_half, "x", NX, 1)]
    wo_other = [swap(block) for block in wo_own]

    kv = jnp.concatenate([key_states[0], value_states[0]], axis=1)
    kv = lax.all_gather(kv, "depth", axis=0)
    attended = attend(where, queries[0], kv)

    units = w_gate.shape[1] // 2
    scaled_gate = lax.dynamic_slice_in_dim(w_gate, depth * units, units, 1).astype(f32) * gain[:, None]
    scaled_up = lax.dynamic_slice_in_dim(w_up, depth * units, units, 1).astype(f32) * gain[:, None]
    w2_half = jnp.concatenate([scaled_gate.astype(bf16), scaled_up.astype(bf16)], axis=1)
    w2_half, _ = lax.optimization_barrier((w2_half, attended))
    w2 = lax.all_gather(w2_half, "x", axis=0, tiled=True)

    four = [
        attended,
        shift(attended, "y", NY, -1),
        shift(attended, "y", NY, 2),
        shift(attended, "y", NY, 1),
    ]

    res_first = jnp.where(odd, residual[1], residual[0])
    res_second = jnp.where(odd, residual[0], residual[1])
    axes = ("x", "y", "col")
    res_work = jnp.concatenate(
        [
            lax.ppermute(res_first, axes, natural_to_work(0)),
            lax.ppermute(res_second, axes, natural_to_work(1)),
        ],
        axis=0,
    )

    parts = out_project(where, four, w_out, wo_own, wo_other)
    projected = reduce_scatter_z(parts)
    stream = (res_work.astype(f32) + projected).astype(bf16)

    work_to_natural = [[(b, a) for a, b in natural_to_work(h)] for h in range(2)]
    back_first = lax.ppermute(stream[:half], axes, work_to_natural[0])
    back_second = lax.ppermute(stream[half:], axes, work_to_natural[1])
    stream_out = jnp.stack(
        [jnp.where(odd, back_second, back_first), jnp.where(odd, back_first, back_second)]
    )

    own = all_gather_z(stream)
    other = [swap(block) for block in own]
    squares = jnp.concatenate([square_sums(own, z), square_sums(other, z)], axis=1)
    square_total = (
        squares[0]
        + shift(squares[1], "y", NY, 1)
        + shift(squares[2], "y", NY, 2)
        + shift(squares[3], "y", NY, -1)
    )
    inverse = lax.rsqrt(square_total / D + eps_norm)[:, None]

    def add(a, b):
        return (a.astype(f32) + b.astype(f32)).astype(bf16)

    far_own, far_other = gate_products((2,), where, own, other, w2)
    far_own = shift(far_own, "y", NY, 1)
    far_other = shift(far_other, "y", NY, -1)
    near = gate_products((1, 3), where, own, other, w2)
    right_other = shift(near[1], "y", NY, 1)
    left_own = shift(near[2], "y", NY, -1)
    right_own = shift(add(near[0], far_own), "y", NY, 1)
    left_other = shift(add(near[3], far_other), "y", NY, -1)
    mine_own, mine_other = gate_products((0,), where, own, other, w2)

    def activate(mine, right, left, factor):
        total = (mine.astype(f32) + right.astype(f32) + left.astype(f32)) * factor
        return (jax.nn.silu(total[:, :units]) * total[:, units:]).astype(bf16)

    hidden_other = swap(activate(mine_other, right_other, left_other, inverse[half:]))
    hidden_own = activate(mine_own, right_own, left_own, inverse[:half])
    hidden = jnp.where(
        depth == 0,
        jnp.concatenate([hidden_own, hidden_other], axis=1),
        jnp.concatenate([hidden_other, hidden_own], axis=1),
    )
    return (hidden[None], stream_out)


def solution(mesh):
    fine = Mesh(mesh.devices.reshape(2, NX, NY, NZ), ("depth", "x", "y", "col"))
    row = ("x", "y")
    return jax.shard_map(
        per_device,
        mesh=fine,
        in_specs=(
            P(row, "depth", "col"),
            P(row, "depth", "col"),
            P(row, "depth", "col"),
            P("col", "depth", row),
            P(row),
            P("col", row),
            P(row, "col"),
            P(row, "col"),
        ),
        out_specs=(P(row, "depth", "col"), P("col", "depth", row)),
        check_vma=False,
    )
```

```python
import functools
import jax
import jax.numpy as jnp
from jax import lax
from jax.experimental import pallas as pl
from jax.experimental.pallas import tpu as pltpu
from jax.sharding import Mesh, PartitionSpec as P

D = 8192
DH = 128
GROUP = 8
NX = 4
NY = 4
NZ = 8

eps_norm = 1e-05
masked_score = -1e30
bf16 = jnp.bfloat16
f32 = jnp.float32
VMEM_BYTES = 20 * 1024 * 1024


def shift(value, axis, size, by):
    return lax.ppermute(value, axis, [(i, (i + by) % size) for i in range(size)])


def swap(value):
    return shift(value, "depth", 2, 1)


def attend_kernel(where_ref, q_ref, kv_ref, out_ref):
    depth = where_ref[0]
    half = q_ref.shape[0]
    keys = jnp.concatenate([kv_ref[0, :, :DH], kv_ref[1, :, :DH]], axis=0)
    values = jnp.concatenate([kv_ref[0, :, DH:], kv_ref[1, :, DH:]], axis=0)
    rows = jnp.concatenate([q_ref[:, h * DH : (h + 1) * DH] for h in range(GROUP)], axis=0)
    scores = lax.dot_general(
        rows, keys, (((1,), (1,)), ((), ())), preferred_element_type=f32
    ) * DH ** (-0.5)
    shape = scores.shape
    position = lax.broadcasted_iota(jnp.int32, shape, 0) % half + depth * half
    allowed = lax.broadcasted_iota(jnp.int32, shape, 1) <= position
    scores = jnp.where(allowed, scores, masked_score)
    top = jnp.max(scores, axis=-1, keepdims=True)
    expo = jnp.exp(scores - top)
    totals = jnp.sum(expo, axis=-1, keepdims=True)
    mixed = jnp.dot(expo.astype(bf16), values, preferred_element_type=f32) / totals
    mixed = mixed.astype(bf16)
    for h in range(GROUP):
        out_ref[:, h * DH : (h + 1) * DH] = mixed[h * half : (h + 1) * half]


def attend(where, queries, kv):
    half, features = queries.shape
    length = 2 * half
    return pl.pallas_call(
        attend_kernel,
        in_specs=[pl.BlockSpec(memory_space=pltpu.SMEM)]
        + [pl.BlockSpec(memory_space=pltpu.VMEM)] * 2,
        out_specs=pl.BlockSpec(memory_space=pltpu.VMEM),
        out_shape=jax.ShapeDtypeStruct((half, features), bf16),
        compiler_params=pltpu.CompilerParams(vmem_limit_bytes=VMEM_BYTES),
        cost_estimate=pl.CostEstimate(
            flops=4 * half * features * length,
            bytes_accessed=4 * half * features,
            transcendentals=half * GROUP * length,
        ),
    )(where, queries, kv)


def out_kernel(where_ref, *refs):
    att, weights, out_ref = refs[:NY], refs[NY:-1], refs[-1]
    depth, x = where_ref[0], where_ref[1]
    rows, features = att[0].shape
    cut = features // 2
    mine = pl.ds(pl.multiple_of(depth * cut, cut), cut)
    theirs = pl.ds(pl.multiple_of((1 - depth) * cut, cut), cut)
    all_full = jnp.concatenate([ref[...] for ref in att], axis=0)
    all_mine = jnp.concatenate([ref[:, mine] for ref in att], axis=0)
    all_theirs = jnp.concatenate([ref[:, theirs] for ref in att], axis=0)
    for j in range(NX):
        if j == 0:
            total = jnp.dot(all_full, weights[0][...], preferred_element_type=f32)
        else:
            total = jnp.dot(all_mine, weights[j][...], preferred_element_type=f32)
            total += jnp.dot(all_theirs, weights[j + NX - 1][...], preferred_element_type=f32)
        total = total.astype(bf16)
        place = (x + j) % NX
        out_ref[place] = total[: 2 * rows]
        out_ref[place + NX] = total[2 * rows :]


def out_project(where, attended, w_out, own, other):
    rows, features = attended[0].shape
    width = w_out.shape[1]
    operands = [*attended, w_out, *own, *other]
    return pl.pallas_call(
        out_kernel,
        in_specs=[pl.BlockSpec(memory_space=pltpu.SMEM)]
        + [pl.BlockSpec(memory_space=pltpu.VMEM)] * len(operands),
        out_specs=pl.BlockSpec(memory_space=pltpu.VMEM),
        out_shape=jax.ShapeDtypeStruct((2 * NX, 2 * rows, width), bf16),
        compiler_params=pltpu.CompilerParams(vmem_limit_bytes=VMEM_BYTES),
        cost_estimate=pl.CostEstimate(
            flops=2 * NY * rows * features * NX * width,
            bytes_accessed=2 * (NY * rows * features + NX * features * width + 4 * NX * rows * width),
            transcendentals=0,
        ),
    )(where, *operands)


def gate_kernel(seqs, where_ref, *refs):
    own, other = refs[:NZ], refs[NZ : 2 * NZ]
    weight_ref = refs[2 * NZ]
    outs, total_ref, square_ref = refs[2 * NZ + 1 : -2], refs[-2], refs[-1]
    step = pl.program_id(0)
    z = where_ref[2]
    rows = own[0].shape[0]
    for j in range(NX):

        @pl.when(step == j)
        def _():
            near_is_first = (z + j) % NZ < NX
            for i, k in enumerate(seqs):
                use_near = near_is_first if k < 2 else jnp.logical_not(near_is_first)
                own_rows = jnp.where(use_near, own[j][...], own[j + NX][...])
                other_rows = jnp.where(use_near, other[j][...], other[j + NX][...])
                both = jnp.concatenate([own_rows, other_rows], axis=0)
                add = jnp.dot(both, weight_ref[...], preferred_element_type=f32)
                wide = both.astype(f32)
                wide = wide * wide
                square = sum(wide[:, c : c + DH] for c in range(0, wide.shape[1], DH))
                if j > 0:
                    add = total_ref[i] + add
                    square = square_ref[i] + square
                if j < NX - 1:
                    total_ref[i] = add
                    square_ref[i] = square
                else:
                    outs[3 * i][...] = add[:rows].astype(bf16)
                    outs[3 * i + 1][...] = add[rows:].astype(bf16)
                    column = jnp.sum(square, axis=1, keepdims=True)
                    column = jnp.broadcast_to(column, square.shape)
                    outs[3 * i + 2][...] = column.T[:8]


def gate_products(seqs, where, own, other, weights):
    rows = own[0].shape[0] // 2
    block = own[0].shape[1]
    width = weights.shape[1]
    place = seqs[0] % 2
    spec = pl.BlockSpec((rows, block), lambda j, where: (place, 0))
    return pl.pallas_call(
        functools.partial(gate_kernel, seqs),
        grid_spec=pltpu.PrefetchScalarGridSpec(
            num_scalar_prefetch=1,
            grid=(NX,),
            in_specs=[spec] * (2 * NZ)
            + [pl.BlockSpec((block, width), lambda j, where: ((where[2] + j) % NX, 0))],
            out_specs=(
                [pl.BlockSpec((rows, width), lambda j, where: (0, 0))] * 2
                + [pl.BlockSpec((8, 2 * rows), lambda j, where: (0, 0))]
            )
            * len(seqs),
            scratch_shapes=[
                pltpu.VMEM((len(seqs), 2 * rows, width), f32),
                pltpu.VMEM((len(seqs), 2 * rows, DH), f32),
            ],
        ),
        out_shape=(
            [jax.ShapeDtypeStruct((rows, width), bf16)] * 2
            + [jax.ShapeDtypeStruct((8, 2 * rows), f32)]
        )
        * len(seqs),
        compiler_params=pltpu.CompilerParams(vmem_limit_bytes=VMEM_BYTES),
        cost_estimate=pl.CostEstimate(
            flops=4 * len(seqs) * rows * NX * block * width,
            bytes_accessed=2 * NX * block * width + 4 * NZ * rows * block,
            transcendentals=0,
        ),
    )(where, *own, *other, weights)


def reduce_scatter_z(parts):
    z = lax.axis_index("col")
    rows = parts.shape[1]
    cut = rows // 2

    def part(offset):
        return lax.dynamic_index_in_dim(parts, (z + offset + NZ) % NZ, 0, keepdims=False)

    right = shift(part(4)[:cut], "col", NZ, 1)
    left = shift(part(-4)[cut:], "col", NZ, -1)
    first, second = part(3), part(-3)
    right = jnp.concatenate(
        [(right.astype(f32) + first[:cut].astype(f32)).astype(bf16), first[cut:]], axis=0
    )
    left = jnp.concatenate(
        [second[:cut], (left.astype(f32) + second[cut:].astype(f32)).astype(bf16)], axis=0
    )
    right = shift(right, "col", NZ, 1)
    left = shift(left, "col", NZ, -1)
    for offset in (2, 1):
        right = shift((right.astype(f32) + part(offset).astype(f32)).astype(bf16), "col", NZ, 1)
        left = shift((left.astype(f32) + part(-offset).astype(f32)).astype(bf16), "col", NZ, -1)
    return part(0).astype(f32) + right.astype(f32) + left.astype(f32)


def all_gather_z(block):
    cut = block.shape[0] // 2
    right = [block]
    left = [block]
    for _ in range(3):
        right.append(shift(right[-1], "col", NZ, 1))
        left.append(shift(left[-1], "col", NZ, -1))
    far_a = shift(right[3][:cut], "col", NZ, 1)
    far_b = shift(left[3][cut:], "col", NZ, -1)
    far = jnp.concatenate([far_a, far_b], axis=0)
    return [block, left[1], left[2], left[3], far, right[3], right[2], right[1]]


def natural_to_work(h):
    pairs = []
    for x in range(NX):
        for y in range(NY):
            for high in range(2):
                for low in range(4):
                    seq = 4 * x + (y + 2 * high + h) % 4
                    there = (low * NY + y) * NZ + seq // 2
                    here = (x * NY + y) * NZ + high * 4 + low
                    pairs.append((there, here))
    return pairs


def per_device(queries, key_states, value_states, residual, gain, w_out, w_gate, w_up):
    half = queries.shape[1]
    depth = lax.axis_index("depth")
    x = lax.axis_index("x")
    y = lax.axis_index("y")
    z = lax.axis_index("col")
    odd = (y % 2) == 1
    where = jnp.stack([depth, x, z]).astype(jnp.int32)

    out_rows = w_out.shape[0] // 2
    wo_half = lax.dynamic_slice_in_dim(w_out, depth * out_rows, out_rows, 0)
    wo_own = [shift(wo_half, "x", NX, -1), shift(wo_half, "x", NX, 2), shift(wo_half, "x", NX, 1)]
    wo_other = [swap(block) for block in wo_own]

    kv = jnp.concatenate([key_states[0], value_states[0]], axis=1)
    kv = lax.all_gather(kv, "depth", axis=0)
    attended = attend(where, queries[0], kv)

    units = w_gate.shape[1] // 2
    scaled_gate = lax.dynamic_slice_in_dim(w_gate, depth * units, units, 1).astype(f32) * gain[:, None]
    scaled_up = lax.dynamic_slice_in_dim(w_up, depth * units, units, 1).astype(f32) * gain[:, None]
    w2_half = jnp.concatenate([scaled_gate.astype(bf16), scaled_up.astype(bf16)], axis=1)
    w2_half, _, _ = lax.optimization_barrier((w2_half, attended, wo_own))
    w2 = lax.all_gather(w2_half, "x", axis=0, tiled=True)

    four = [
        attended,
        shift(attended, "y", NY, -1),
        shift(attended, "y", NY, 2),
        shift(attended, "y", NY, 1),
    ]

    res_first = jnp.where(odd, residual[1], residual[0])
    res_second = jnp.where(odd, residual[0], residual[1])
    axes = ("x", "y", "col")
    res_work = jnp.concatenate(
        [
            lax.ppermute(res_first, axes, natural_to_work(0)),
            lax.ppermute(res_second, axes, natural_to_work(1)),
        ],
        axis=0,
    )

    four, res_work = lax.optimization_barrier((four, res_work))
    parts = out_project(where, four, w_out, wo_own, wo_other)
    projected = reduce_scatter_z(parts)
    stream = (res_work.astype(f32) + projected).astype(bf16)

    own = all_gather_z(stream)
    other = [swap(block) for block in own]

    stream_late, _ = lax.optimization_barrier((stream, own[1:]))
    work_to_natural = [[(b, a) for a, b in natural_to_work(h)] for h in range(2)]
    back_first = lax.ppermute(stream_late[:half], axes, work_to_natural[0])
    back_second = lax.ppermute(stream_late[half:], axes, work_to_natural[1])
    stream_out = jnp.stack(
        [jnp.where(odd, back_second, back_first), jnp.where(odd, back_first, back_second)]
    )

    def add(a, b):
        return (a.astype(f32) + b.astype(f32)).astype(bf16)

    far_own, far_other, far_square = gate_products((2,), where, own, other, w2)
    far_own = shift(far_own, "y", NY, 1)
    far_other = shift(far_other, "y", NY, -1)
    near = gate_products((1, 3), where, own, other, w2)
    right_other = shift(near[1], "y", NY, 1)
    left_own = shift(near[3], "y", NY, -1)
    right_own = shift(add(near[0], far_own), "y", NY, 1)
    left_other = shift(add(near[4], far_other), "y", NY, -1)
    mine_own, mine_other, mine_square = gate_products((0,), where, own, other, w2)
    square_total = (
        mine_square[0]
        + shift(near[2], "y", NY, 1)[0]
        + shift(far_square, "y", NY, 2)[0]
        + shift(near[5], "y", NY, -1)[0]
    )
    inverse = lax.rsqrt(square_total / D + eps_norm)[:, None]

    def activate(mine, right, left, factor):
        total = (mine.astype(f32) + right.astype(f32) + left.astype(f32)) * factor
        return (jax.nn.silu(total[:, :units]) * total[:, units:]).astype(bf16)

    hidden_other = swap(activate(mine_other, right_other, left_other, inverse[half:]))
    hidden_own = activate(mine_own, right_own, left_own, inverse[:half])
    hidden = jnp.where(
        depth == 0,
        jnp.concatenate([hidden_own, hidden_other], axis=1),
        jnp.concatenate([hidden_other, hidden_own], axis=1),
    )
    return (hidden[None], stream_out)


def solution(mesh):
    fine = Mesh(mesh.devices.reshape(2, NX, NY, NZ), ("depth", "x", "y", "col"))
    row = ("x", "y")
    return jax.shard_map(
        per_device,
        mesh=fine,
        in_specs=(
            P(row, "depth", "col"),
            P(row, "depth", "col"),
            P(row, "depth", "col"),
            P("col", "depth", row),
            P(row),
            P("col", row),
            P(row, "col"),
            P(row, "col"),
        ),
        out_specs=(P(row, "depth", "col"), P("col", "depth", row)),
        check_vma=False,
    )
```

```python
import functools
import jax
import jax.numpy as jnp
from jax import lax
from jax.experimental import pallas as pl
from jax.experimental.pallas import tpu as pltpu
from jax.sharding import Mesh, PartitionSpec as P

D = 8192
DH = 128
GROUP = 8
NX = 4
NY = 4
NZ = 8

eps_norm = 1e-05
masked_score = -1e30
bf16 = jnp.bfloat16
f32 = jnp.float32
VMEM_BYTES = 48 * 1024 * 1024
SMALL_COST = pl.CostEstimate(flops=1024, bytes_accessed=1024, transcendentals=0)


def shift(value, axis, size, by):
    return lax.ppermute(value, axis, [(i, (i + by) % size) for i in range(size)])


def swap(value):
    return shift(value, "depth", 2, 1)


def attend_kernel(where_ref, q_ref, kv_ref, out_ref):
    depth = where_ref[0]
    half = q_ref.shape[0]
    keys = jnp.concatenate([kv_ref[0, :, :DH], kv_ref[1, :, :DH]], axis=0)
    values = jnp.concatenate([kv_ref[0, :, DH:], kv_ref[1, :, DH:]], axis=0)
    rows = jnp.concatenate([q_ref[:, h * DH : (h + 1) * DH] for h in range(GROUP)], axis=0)
    scores = lax.dot_general(
        rows, keys, (((1,), (1,)), ((), ())), preferred_element_type=f32
    ) * DH ** (-0.5)
    shape = scores.shape
    position = lax.broadcasted_iota(jnp.int32, shape, 0) % half + depth * half
    allowed = lax.broadcasted_iota(jnp.int32, shape, 1) <= position
    scores = jnp.where(allowed, scores, masked_score)
    top = jnp.max(scores, axis=-1, keepdims=True)
    expo = jnp.exp(scores - top)
    totals = jnp.sum(expo, axis=-1, keepdims=True)
    mixed = jnp.dot(expo.astype(bf16), values, preferred_element_type=f32) / totals
    mixed = mixed.astype(bf16)
    for h in range(GROUP):
        out_ref[:, h * DH : (h + 1) * DH] = mixed[h * half : (h + 1) * half]


def attend(where, queries, kv):
    half, features = queries.shape
    length = 2 * half
    return pl.pallas_call(
        attend_kernel,
        in_specs=[pl.BlockSpec(memory_space=pltpu.SMEM)]
        + [pl.BlockSpec(memory_space=pltpu.VMEM)] * 2,
        out_specs=pl.BlockSpec(memory_space=pltpu.VMEM),
        out_shape=jax.ShapeDtypeStruct((half, features), bf16),
        compiler_params=pltpu.CompilerParams(vmem_limit_bytes=VMEM_BYTES),
        cost_estimate=SMALL_COST,
    )(where, queries, kv)


def out_kernel(where_ref, *refs):
    att, own_ref, other_ref, out_ref = refs[:NY], *refs[NY:]
    depth = where_ref[0]
    rows, features = att[0].shape
    cut = features // 2
    mine = pl.ds(pl.multiple_of(depth * cut, cut), cut)
    theirs = pl.ds(pl.multiple_of((1 - depth) * cut, cut), cut)
    all_mine = jnp.concatenate([ref[:, mine] for ref in att], axis=0)
    all_theirs = jnp.concatenate([ref[:, theirs] for ref in att], axis=0)
    total = jnp.dot(all_mine, own_ref[0], preferred_element_type=f32)
    total += jnp.dot(all_theirs, other_ref[0], preferred_element_type=f32)
    total = total.astype(bf16)
    out_ref[0, 0] = total[: 2 * rows]
    out_ref[1, 0] = total[2 * rows :]


def out_project(where, attended, own, other):
    rows, features = attended[0].shape
    width = own.shape[2]
    weight_spec = pl.BlockSpec((1, features // 2, width), lambda j, where: (j, 0, 0))
    parts = pl.pallas_call(
        out_kernel,
        grid_spec=pltpu.PrefetchScalarGridSpec(
            num_scalar_prefetch=1,
            grid=(NX,),
            in_specs=[pl.BlockSpec((rows, features), lambda j, where: (0, 0))] * NY
            + [weight_spec] * 2,
            out_specs=pl.BlockSpec((2, 1, 2 * rows, width), lambda j, where: (0, j, 0, 0)),
        ),
        out_shape=jax.ShapeDtypeStruct((2, NX, 2 * rows, width), bf16),
        compiler_params=pltpu.CompilerParams(vmem_limit_bytes=VMEM_BYTES),
        cost_estimate=SMALL_COST,
    )(where, *attended, own, other)
    return parts.reshape(2 * NX, 2 * rows, width)


def gate_kernel(seqs, where_ref, *refs):
    own, other = refs[:NZ], refs[NZ : 2 * NZ]
    weight_ref = refs[2 * NZ]
    outs, total_ref, square_ref = refs[2 * NZ + 1 : -2], refs[-2], refs[-1]
    step = pl.program_id(0)
    z = where_ref[1]
    for j in range(NX):

        @pl.when(step == j)
        def _():
            near_is_first = (z + j) % NZ < NX
            for i, k in enumerate(seqs):
                use_near = near_is_first if k < 2 else jnp.logical_not(near_is_first)
                own_rows = jnp.where(use_near, own[j][...], own[j + NX][...])
                other_rows = jnp.where(use_near, other[j][...], other[j + NX][...])
                both = jnp.concatenate([own_rows, other_rows], axis=0)
                add = jnp.dot(both, weight_ref[...], preferred_element_type=f32)
                wide = both.astype(f32)
                wide = wide * wide
                square = sum(wide[:, c : c + DH] for c in range(0, wide.shape[1], DH))
                if j > 0:
                    add = total_ref[i] + add
                    square = square_ref[i] + square
                if j < NX - 1:
                    total_ref[i] = add
                    square_ref[i] = square
                else:
                    outs[2 * i][...] = add.astype(bf16)
                    column = jnp.sum(square, axis=1, keepdims=True)
                    column = jnp.broadcast_to(column, square.shape)
                    outs[2 * i + 1][...] = column.T[:8]


def gate_products(seqs, where, own, other, weights):
    rows = own[0].shape[0] // 2
    block = own[0].shape[1]
    width = weights.shape[1]
    place = seqs[0] % 2
    spec = pl.BlockSpec((rows, block), lambda j, where: (place, 0))
    return pl.pallas_call(
        functools.partial(gate_kernel, seqs),
        grid_spec=pltpu.PrefetchScalarGridSpec(
            num_scalar_prefetch=1,
            grid=(NX,),
            in_specs=[spec] * (2 * NZ)
            + [pl.BlockSpec((block, width), lambda j, where: ((where[1] + j) % NX, 0))],
            out_specs=(
                [
                    pl.BlockSpec((2 * rows, width), lambda j, where: (0, 0)),
                    pl.BlockSpec((8, 2 * rows), lambda j, where: (0, 0)),
                ]
                * len(seqs)
            ),
            scratch_shapes=[
                pltpu.VMEM((len(seqs), 2 * rows, width), f32),
                pltpu.VMEM((len(seqs), 2 * rows, DH), f32),
            ],
        ),
        out_shape=(
            [
                jax.ShapeDtypeStruct((2 * rows, width), bf16),
                jax.ShapeDtypeStruct((8, 2 * rows), f32),
            ]
            * len(seqs)
        ),
        compiler_params=pltpu.CompilerParams(vmem_limit_bytes=VMEM_BYTES),
        cost_estimate=SMALL_COST,
    )(where, *own, *other, weights)


def reduce_scatter_z(parts):
    z = lax.axis_index("col")
    rows = parts.shape[1]
    cut = rows // 2

    def part(offset):
        return lax.dynamic_index_in_dim(parts, (z + offset + NZ) % NZ, 0, keepdims=False)

    right = shift(part(4)[:cut], "col", NZ, 1)
    left = shift(part(-4)[cut:], "col", NZ, -1)
    first, second = part(3), part(-3)
    right = jnp.concatenate(
        [(right.astype(f32) + first[:cut].astype(f32)).astype(bf16), first[cut:]], axis=0
    )
    left = jnp.concatenate(
        [second[:cut], (left.astype(f32) + second[cut:].astype(f32)).astype(bf16)], axis=0
    )
    right = shift(right, "col", NZ, 1)
    left = shift(left, "col", NZ, -1)
    for offset in (2, 1):
        right = shift((right.astype(f32) + part(offset).astype(f32)).astype(bf16), "col", NZ, 1)
        left = shift((left.astype(f32) + part(-offset).astype(f32)).astype(bf16), "col", NZ, -1)
    return part(0).astype(f32) + right.astype(f32) + left.astype(f32)


def all_gather_z(block):
    cut = block.shape[0] // 2
    right, left = [block], [block]
    swapped_right, swapped_left = [swap(block)], []
    for step in range(3):
        sent_right, sent_left = right[-1], left[-1]
        if step > 0:
            waited = (swapped_right[step - 1], swapped_left[max(step - 2, 0) : step - 1])
            (sent_right, sent_left), _ = lax.optimization_barrier(((sent_right, sent_left), waited))
            swapped_right.append(swap(right[step]))
            swapped_left.append(swap(left[step]))
        right.append(shift(sent_right, "col", NZ, 1))
        left.append(shift(sent_left, "col", NZ, -1))
    (sent_right, sent_left), _ = lax.optimization_barrier(
        ((right[3], left[3]), (swapped_right[2], swapped_left[1]))
    )
    swapped_right.append(swap(right[3]))
    swapped_left.append(swap(left[3]))
    far_a = shift(sent_right[:cut], "col", NZ, 1)
    far_b = shift(sent_left[cut:], "col", NZ, -1)
    far = jnp.concatenate([far_a, far_b], axis=0)
    own = [block, left[1], left[2], left[3], far, right[3], right[2], right[1]]
    other = [swapped_right[0], *swapped_left, swap(far), *swapped_right[:0:-1]]
    return own, other


def natural_to_work(h):
    pairs = []
    for x in range(NX):
        for y in range(NY):
            for high in range(2):
                for low in range(4):
                    seq = 4 * x + (y + 2 * high + h) % 4
                    there = (low * NY + y) * NZ + seq // 2
                    here = (x * NY + y) * NZ + high * 4 + low
                    pairs.append((there, here))
    return pairs


def per_device(queries, key_states, value_states, residual, gain, w_out, w_gate, w_up):
    half = queries.shape[1]
    depth = lax.axis_index("depth")
    y = lax.axis_index("y")
    z = lax.axis_index("col")
    odd = (y % 2) == 1
    where = jnp.stack([depth, z]).astype(jnp.int32)

    out_rows = w_out.shape[0] // 2
    wo_half = lax.dynamic_slice_in_dim(w_out, depth * out_rows, out_rows, 0)
    wo_own = lax.all_gather(wo_half, "x", axis=0)

    kv = jnp.concatenate([key_states[0], value_states[0]], axis=1)
    kv = lax.all_gather(kv, "depth", axis=0)
    attended = attend(where, queries[0], kv)

    units = w_gate.shape[1] // 2
    scaled_gate = lax.dynamic_slice_in_dim(w_gate, depth * units, units, 1).astype(f32) * gain[:, None]
    scaled_up = lax.dynamic_slice_in_dim(w_up, depth * units, units, 1).astype(f32) * gain[:, None]
    w2_half = jnp.concatenate([scaled_gate.astype(bf16), scaled_up.astype(bf16)], axis=1)
    w2_half, _ = lax.optimization_barrier((w2_half, attended))
    w2 = lax.all_gather(w2_half, "x", axis=0, tiled=True)

    four = [
        attended,
        shift(attended, "y", NY, -1),
        shift(attended, "y", NY, 2),
        shift(attended, "y", NY, 1),
    ]

    res_first = jnp.where(odd, residual[1], residual[0])
    res_second = jnp.where(odd, residual[0], residual[1])
    axes = ("x", "y", "col")
    res_work = jnp.concatenate(
        [
            lax.ppermute(res_first, axes, natural_to_work(0)),
            lax.ppermute(res_second, axes, natural_to_work(1)),
        ],
        axis=0,
    )

    four, res_work = lax.optimization_barrier((four, res_work))
    wo_own, four = lax.optimization_barrier((wo_own, four))
    wo_other = swap(wo_own)
    parts = out_project(where, four, wo_own, wo_other)
    projected = reduce_scatter_z(parts)
    stream = (res_work.astype(f32) + projected).astype(bf16)

    own, other = all_gather_z(stream)

    far, far_square = gate_products((2,), where, own, other, w2)
    pairs = []
    for i in range(NY):
        pairs.append((i, (i + 1) % NY))
    for i in range(NY):
        pairs.append((NY + i, NY + (i - 1) % NY))
    far = lax.ppermute(far, ("depth", "y"), pairs).astype(f32)
    near_right, right_square, near_left, left_square = gate_products((1, 3), where, own, other, w2)
    near_right = (near_right.astype(f32) + jnp.where(depth == 0, far, 0.0)).astype(bf16)
    near_left = (near_left.astype(f32) + jnp.where(depth == 1, far, 0.0)).astype(bf16)
    from_left = shift(near_right, "y", NY, 1)
    from_right = shift(near_left, "y", NY, -1)
    mine, mine_square = gate_products((0,), where, own, other, w2)

    (far_square, right_square, left_square, stream_late), _ = lax.optimization_barrier(
        ((far_square, right_square, left_square, stream), mine)
    )
    square_total = (
        mine_square[0]
        + shift(right_square, "y", NY, 1)[0]
        + shift(far_square, "y", NY, 2)[0]
        + shift(left_square, "y", NY, -1)[0]
    )
    inverse = lax.rsqrt(square_total / D + eps_norm)[:, None]
    work_to_natural = [[(b, a) for a, b in natural_to_work(h)] for h in range(2)]
    back_first = lax.ppermute(stream_late[:half], axes, work_to_natural[0])
    back_second = lax.ppermute(stream_late[half:], axes, work_to_natural[1])
    stream_out = jnp.stack(
        [jnp.where(odd, back_second, back_first), jnp.where(odd, back_first, back_second)]
    )

    total = (mine.astype(f32) + from_left.astype(f32) + from_right.astype(f32)) * inverse
    hidden_both = (jax.nn.silu(total[:, :units]) * total[:, units:]).astype(bf16)
    hidden_own = hidden_both[:half]
    hidden_other = swap(hidden_both[half:])
    hidden = jnp.where(
        depth == 0,
        jnp.concatenate([hidden_own, hidden_other], axis=1),
        jnp.concatenate([hidden_other, hidden_own], axis=1),
    )
    return (hidden[None], stream_out)


def solution(mesh):
    fine = Mesh(mesh.devices.reshape(2, NX, NY, NZ), ("depth", "x", "y", "col"))
    row = ("x", "y")
    return jax.shard_map(
        per_device,
        mesh=fine,
        in_specs=(
            P(row, "depth", "col"),
            P(row, "depth", "col"),
            P(row, "depth", "col"),
            P("col", "depth", row),
            P(row),
            P("col", row),
            P(row, "col"),
            P(row, "col"),
        ),
        out_specs=(P(row, "depth", "col"), P("col", "depth", row)),
        check_vma=False,
    )
```

```python
import functools
import jax
import jax.numpy as jnp
from jax import lax
from jax.experimental import pallas as pl
from jax.experimental.pallas import tpu as pltpu
from jax.sharding import Mesh, PartitionSpec as P

D = 8192
DH = 128
GROUP = 8
NX = 4
NY = 4
NZ = 8

eps_norm = 1e-05
masked_score = -1e30
bf16 = jnp.bfloat16
f32 = jnp.float32
VMEM_BYTES = 48 * 1024 * 1024
SMALL_COST = pl.CostEstimate(flops=1024, bytes_accessed=1024, transcendentals=0)


def shift(value, axis, size, by):
    return lax.ppermute(value, axis, [(i, (i + by) % size) for i in range(size)])


def swap(value):
    return shift(value, "depth", 2, 1)


def attend_kernel(where_ref, q_ref, kv_ref, out_ref):
    depth = where_ref[0]
    half = q_ref.shape[0]
    keys = jnp.concatenate([kv_ref[0, :, :DH], kv_ref[1, :, :DH]], axis=0)
    values = jnp.concatenate([kv_ref[0, :, DH:], kv_ref[1, :, DH:]], axis=0)
    rows = jnp.concatenate([q_ref[:, h * DH : (h + 1) * DH] for h in range(GROUP)], axis=0)
    scores = lax.dot_general(
        rows, keys, (((1,), (1,)), ((), ())), preferred_element_type=f32
    ) * DH ** (-0.5)
    shape = scores.shape
    position = lax.broadcasted_iota(jnp.int32, shape, 0) % half + depth * half
    allowed = lax.broadcasted_iota(jnp.int32, shape, 1) <= position
    scores = jnp.where(allowed, scores, masked_score)
    top = jnp.max(scores, axis=-1, keepdims=True)
    expo = jnp.exp(scores - top)
    totals = jnp.sum(expo, axis=-1, keepdims=True)
    mixed = jnp.dot(expo.astype(bf16), values, preferred_element_type=f32) / totals
    mixed = mixed.astype(bf16)
    for h in range(GROUP):
        out_ref[:, h * DH : (h + 1) * DH] = mixed[h * half : (h + 1) * half]


def attend(where, queries, kv):
    half, features = queries.shape
    length = 2 * half
    return pl.pallas_call(
        attend_kernel,
        in_specs=[pl.BlockSpec(memory_space=pltpu.SMEM)]
        + [pl.BlockSpec(memory_space=pltpu.VMEM)] * 2,
        out_specs=pl.BlockSpec(memory_space=pltpu.VMEM),
        out_shape=jax.ShapeDtypeStruct((half, features), bf16),
        compiler_params=pltpu.CompilerParams(vmem_limit_bytes=VMEM_BYTES),
        cost_estimate=SMALL_COST,
    )(where, queries, kv)


ANYWHERE = pl.BlockSpec(memory_space=pl.ANY)
SCALARS = pl.BlockSpec(memory_space=pltpu.SMEM)
WHOLE = pl.BlockSpec(memory_space=pltpu.VMEM)


def out_kernel(where_ref, *refs):
    att, w_ref, own, other = refs[:4], refs[4], refs[5:9], refs[9:13]
    out_ref, att_buf, w_buf, att_sem, w_sem = refs[13:]
    depth, x = where_ref[0], where_ref[2]
    rows = att[0].shape[0]
    cut = own[0].shape[0]
    quarter = own[2].shape[0]
    copies = [[] for _ in range(NX)]
    first = [
        pltpu.make_async_copy(ref, att_buf.at[pl.ds(k * rows, rows)], att_sem.at[k])
        for k, ref in enumerate(att)
    ]
    copies[0].append(pltpu.make_async_copy(w_ref, w_buf.at[0], w_sem.at[0]))
    slot = 1
    for side, blocks in ((depth, own), (1 - depth, other)):
        base = pl.multiple_of(side * cut, cut)
        for j, ref, start in (
            (1, blocks[0], 0),
            (3, blocks[1], 0),
            (2, blocks[2], 0),
            (2, blocks[3], quarter),
        ):
            place = w_buf.at[j, pl.ds(pl.multiple_of(base + start, quarter), ref.shape[0])]
            copies[j].append(pltpu.make_async_copy(ref, place, w_sem.at[slot]))
            slot += 1
    for copy in first:
        copy.start()
    for j in (0, 1, 3, 2):
        for copy in copies[j]:
            copy.start()
    for copy in first:
        copy.wait()
    for j in (0, 1, 3, 2):
        for copy in copies[j]:
            copy.wait()
        total = jnp.dot(att_buf[...], w_buf[j], preferred_element_type=f32).astype(bf16)
        place = (x + j) % NX
        out_ref[place] = total[: 2 * rows]
        out_ref[place + NX] = total[2 * rows :]


def out_project(where, attended, w_out, own, other):
    rows, features = attended[0].shape
    width = w_out.shape[1]
    return pl.pallas_call(
        out_kernel,
        in_specs=[SCALARS] + [ANYWHERE] * 13,
        out_specs=WHOLE,
        out_shape=jax.ShapeDtypeStruct((2 * NX, 2 * rows, width), bf16),
        scratch_shapes=[
            pltpu.VMEM((NY * rows, features), bf16),
            pltpu.VMEM((NX, features, width), bf16),
            pltpu.SemaphoreType.DMA((NY,)),
            pltpu.SemaphoreType.DMA((9,)),
        ],
        compiler_params=pltpu.CompilerParams(vmem_limit_bytes=VMEM_BYTES),
        cost_estimate=SMALL_COST,
    )(where, *attended, w_out, *own, *other)


def gate_kernel(seqs, where_ref, *refs):
    own, other, weight_ref = refs[:NZ], refs[NZ : 2 * NZ], refs[2 * NZ]
    outs = refs[2 * NZ + 1 : -6]
    w_buf, x_buf, total_ref, square_ref, w_sem, x_sem = refs[-6:]
    z = where_ref[1]
    block = own[0].shape[1]
    rows = own[0].shape[0] // 2

    def rows_copy(ref, i, k, j, side):
        return pltpu.make_async_copy(
            ref.at[pl.ds((k % 2) * rows, rows)],
            x_buf.at[i, j, pl.ds(side * rows, rows)],
            x_sem.at[i, j, side],
        )

    def weight_copy(j):
        start = pl.multiple_of(((z + j) % NX) * block, block)
        return pltpu.make_async_copy(weight_ref.at[pl.ds(start, block)], w_buf.at[j], w_sem.at[j])

    for j in range(NX):
        near_is_first = (z + j) % NZ < NX
        for i, k in enumerate(seqs):
            use_near = near_is_first if k < 2 else jnp.logical_not(near_is_first)
            for side, blocks in enumerate((own, other)):

                @pl.when(use_near)
                def _():
                    rows_copy(blocks[j], i, k, j, side).start()

                @pl.when(jnp.logical_not(use_near))
                def _():
                    rows_copy(blocks[j + NX], i, k, j, side).start()

        weight_copy(j).start()
    for j in range(NX):
        weight_copy(j).wait()
        for i, k in enumerate(seqs):
            for side, blocks in enumerate((own, other)):
                rows_copy(blocks[j], i, k, j, side).wait()
            both = x_buf[i, j]
            add = jnp.dot(both, w_buf[j], preferred_element_type=f32)
            wide = both.astype(f32)
            wide = wide * wide
            square = sum(wide[:, c : c + DH] for c in range(0, wide.shape[1], DH))
            if j > 0:
                add = total_ref[i] + add
                square = square_ref[i] + square
            if j < NX - 1:
                total_ref[i] = add
                square_ref[i] = square
            else:
                outs[2 * i][...] = add.astype(bf16)
                column = jnp.sum(square, axis=1, keepdims=True)
                column = jnp.broadcast_to(column, square.shape)
                outs[2 * i + 1][...] = column.T[:8]


def gate_products(seqs, where, own, other, weights):
    rows, block = own[0].shape
    width = weights.shape[1]
    n = len(seqs)
    return pl.pallas_call(
        functools.partial(gate_kernel, seqs),
        in_specs=[SCALARS] + [ANYWHERE] * (2 * NZ + 1),
        out_specs=[WHOLE] * (2 * n),
        scratch_shapes=[
            pltpu.VMEM((NX, block, width), bf16),
            pltpu.VMEM((n, NX, rows, block), bf16),
            pltpu.VMEM((n, rows, width), f32),
            pltpu.VMEM((n, rows, DH), f32),
            pltpu.SemaphoreType.DMA((NX,)),
            pltpu.SemaphoreType.DMA((n, NX, 2)),
        ],
        out_shape=[
            jax.ShapeDtypeStruct((rows, width), bf16),
            jax.ShapeDtypeStruct((8, rows), f32),
        ]
        * n,
        compiler_params=pltpu.CompilerParams(vmem_limit_bytes=VMEM_BYTES),
        cost_estimate=SMALL_COST,
    )(where, *own, *other, weights)


def ring_kernel(offset, where_ref, parts_ref, right_ref, left_ref, *refs):
    z = where_ref[1]
    buf, sem = refs[-2:]
    if offset:
        sources = (parts_ref.at[(z + offset) % NZ], parts_ref.at[(z + NZ - offset) % NZ])
    else:
        sources = (parts_ref.at[z], refs[0])
    arrived = (right_ref, left_ref)
    starts = (0, buf.shape[1] - left_ref.shape[0])
    copies = []
    for i in range(2):
        copies.append(pltpu.make_async_copy(sources[i], buf.at[i], sem.at[i]))
        place = buf.at[2 + i, pl.ds(starts[i], arrived[i].shape[0])]
        copies.append(pltpu.make_async_copy(arrived[i], place, sem.at[2 + i]))
    for copy in copies:
        copy.start()
    for copy in copies:
        copy.wait()
    if not offset:
        refs[1][...] = (
            (buf[0].astype(f32) + buf[2].astype(f32) + buf[3].astype(f32)) + buf[1].astype(f32)
        ).astype(bf16)
        return
    for i in range(2):
        rows = arrived[i].shape[0]
        held = pl.ds(starts[i], rows)
        total = buf[i, held].astype(f32) + buf[2 + i, held].astype(f32)
        refs[i][held] = total.astype(bf16)
        if rows < buf.shape[1]:
            rest = pl.ds(rows - starts[i], rows)
            refs[i][rest] = buf[i, rest]


def ring_add(offset, where, parts, right, left, residual=None):
    _, rows, width = parts.shape
    extra = [] if residual is None else [residual]
    return pl.pallas_call(
        functools.partial(ring_kernel, offset),
        in_specs=[SCALARS] + [ANYWHERE] * (3 + len(extra)),
        out_specs=[WHOLE] * (2 - len(extra)),
        scratch_shapes=[pltpu.VMEM((4, rows, width), bf16), pltpu.SemaphoreType.DMA((4,))],
        out_shape=[jax.ShapeDtypeStruct((rows, width), bf16)] * (2 - len(extra)),
        compiler_params=pltpu.CompilerParams(vmem_limit_bytes=VMEM_BYTES),
        cost_estimate=SMALL_COST,
    )(where, parts, right, left, *extra)


def reduce_scatter_z(where, parts, residual):
    z = lax.axis_index("col")
    cut = parts.shape[1] // 2
    far = lax.dynamic_index_in_dim(parts, (z + 4) % NZ, 0, keepdims=False)
    right = shift(far[:cut], "col", NZ, 1)
    left = shift(far[cut:], "col", NZ, -1)
    for offset in (3, 2, 1):
        right, left = ring_add(offset, where, parts, right, left)
        right = shift(right, "col", NZ, 1)
        left = shift(left, "col", NZ, -1)
    return ring_add(0, where, parts, right, left, residual)[0]


def all_gather_z(block):
    cut = block.shape[0] // 2
    right, left = [block], [block]
    swapped_right, swapped_left = [swap(block)], []
    for step in range(3):
        sent_right, sent_left = right[-1], left[-1]
        if step > 0:
            waited = (swapped_right[step - 1], swapped_left[max(step - 2, 0) : step - 1])
            (sent_right, sent_left), _ = lax.optimization_barrier(((sent_right, sent_left), waited))
            swapped_right.append(swap(right[step]))
            swapped_left.append(swap(left[step]))
        right.append(shift(sent_right, "col", NZ, 1))
        left.append(shift(sent_left, "col", NZ, -1))
    (sent_right, sent_left), _ = lax.optimization_barrier(
        ((right[3], left[3]), (swapped_right[2], swapped_left[1]))
    )
    swapped_right.append(swap(right[3]))
    swapped_left.append(swap(left[3]))
    far_a = shift(sent_right[:cut], "col", NZ, 1)
    far_b = shift(sent_left[cut:], "col", NZ, -1)
    far = jnp.concatenate([far_a, far_b], axis=0)
    own = [block, left[1], left[2], left[3], far, right[3], right[2], right[1]]
    other = [swapped_right[0], *swapped_left, swap(far), *swapped_right[:0:-1]]
    return own, other


def natural_to_work(h):
    pairs = []
    for x in range(NX):
        for y in range(NY):
            for high in range(2):
                for low in range(4):
                    seq = 4 * x + (y + 2 * high + h) % 4
                    there = (low * NY + y) * NZ + seq // 2
                    here = (x * NY + y) * NZ + high * 4 + low
                    pairs.append((there, here))
    return pairs


def per_device(queries, key_states, value_states, residual, gain, w_out, w_gate, w_up):
    half = queries.shape[1]
    depth = lax.axis_index("depth")
    y = lax.axis_index("y")
    z = lax.axis_index("col")
    odd = (y % 2) == 1
    where = jnp.stack([depth, z, lax.axis_index("x")]).astype(jnp.int32)

    out_rows = w_out.shape[0] // 2
    quarter = out_rows // 2
    wo_half = lax.dynamic_slice_in_dim(w_out, depth * out_rows, out_rows, 0)
    wo_next = shift(wo_half, "x", NX, -1)
    wo_last = shift(wo_half, "x", NX, 1)
    wo_own = [
        wo_next,
        wo_last,
        shift(wo_next[:quarter], "x", NX, -1),
        shift(wo_last[quarter:], "x", NX, 1),
    ]
    wo_other = [swap(block) for block in wo_own]

    kv = jnp.concatenate([key_states[0], value_states[0]], axis=1)
    kv = lax.all_gather(kv, "depth", axis=0)
    attended = attend(where, queries[0], kv)

    units = w_gate.shape[1] // 2
    scaled_gate = lax.dynamic_slice_in_dim(w_gate, depth * units, units, 1).astype(f32) * gain[:, None]
    scaled_up = lax.dynamic_slice_in_dim(w_up, depth * units, units, 1).astype(f32) * gain[:, None]
    w2_half = jnp.concatenate([scaled_gate.astype(bf16), scaled_up.astype(bf16)], axis=1)
    four = [
        attended,
        shift(attended, "y", NY, -1),
        shift(attended, "y", NY, 2),
        shift(attended, "y", NY, 1),
    ]

    res_first = jnp.where(odd, residual[1], residual[0])
    res_second = jnp.where(odd, residual[0], residual[1])
    axes = ("x", "y", "col")
    res_work = jnp.concatenate(
        [
            lax.ppermute(res_first, axes, natural_to_work(0)),
            lax.ppermute(res_second, axes, natural_to_work(1)),
        ],
        axis=0,
    )

    early = (four, wo_own, wo_other[:2], res_work)
    w2_half, _ = lax.optimization_barrier((w2_half, early))
    w2 = lax.all_gather(w2_half, "x", axis=0, tiled=True)
    four, res_work = lax.optimization_barrier((four, res_work))
    parts = out_project(where, four, w_out, wo_own, wo_other)
    stream = reduce_scatter_z(where, parts, res_work)

    own, other = all_gather_z(stream)

    far, far_square = gate_products((2,), where, own, other, w2)
    pairs = []
    for i in range(NY):
        pairs.append((i, (i + 1) % NY))
    for i in range(NY):
        pairs.append((NY + i, NY + (i - 1) % NY))
    far = lax.ppermute(far, ("depth", "y"), pairs).astype(f32)
    near_right, right_square, near_left, left_square = gate_products((1, 3), where, own, other, w2)
    near_right = (near_right.astype(f32) + jnp.where(depth == 0, far, 0.0)).astype(bf16)
    near_left = (near_left.astype(f32) + jnp.where(depth == 1, far, 0.0)).astype(bf16)
    from_left = shift(near_right, "y", NY, 1)
    from_right = shift(near_left, "y", NY, -1)
    mine, mine_square = gate_products((0,), where, own, other, w2)

    (far_square, right_square, left_square, stream_late), _ = lax.optimization_barrier(
        ((far_square, right_square, left_square, stream), mine)
    )
    square_total = (
        mine_square[0]
        + shift(right_square, "y", NY, 1)[0]
        + shift(far_square, "y", NY, 2)[0]
        + shift(left_square, "y", NY, -1)[0]
    )
    inverse = lax.rsqrt(square_total / D + eps_norm)[:, None]
    work_to_natural = [[(b, a) for a, b in natural_to_work(h)] for h in range(2)]
    back_first = lax.ppermute(stream_late[:half], axes, work_to_natural[0])
    back_second = lax.ppermute(stream_late[half:], axes, work_to_natural[1])
    stream_out = jnp.stack(
        [jnp.where(odd, back_second, back_first), jnp.where(odd, back_first, back_second)]
    )

    total = (mine.astype(f32) + from_left.astype(f32) + from_right.astype(f32)) * inverse
    hidden_both = (jax.nn.silu(total[:, :units]) * total[:, units:]).astype(bf16)
    hidden_own = hidden_both[:half]
    hidden_other = swap(hidden_both[half:])
    hidden = jnp.where(
        depth == 0,
        jnp.concatenate([hidden_own, hidden_other], axis=1),
        jnp.concatenate([hidden_other, hidden_own], axis=1),
    )
    return (hidden[None], stream_out)


def solution(mesh):
    fine = Mesh(mesh.devices.reshape(2, NX, NY, NZ), ("depth", "x", "y", "col"))
    row = ("x", "y")
    return jax.shard_map(
        per_device,
        mesh=fine,
        in_specs=(
            P(row, "depth", "col"),
            P(row, "depth", "col"),
            P(row, "depth", "col"),
            P("col", "depth", row),
            P(row),
            P("col", row),
            P(row, "col"),
            P(row, "col"),
        ),
        out_specs=(P(row, "depth", "col"), P("col", "depth", row)),
        check_vma=False,
    )
```

```python
import functools
import jax
import jax.numpy as jnp
from jax import lax
from jax.experimental import pallas as pl
from jax.experimental.pallas import tpu as pltpu
from jax.sharding import Mesh, PartitionSpec as P

D = 8192
DH = 128
GROUP = 8
NX = 4
NY = 4
NZ = 8

eps_norm = 1e-05
masked_score = -1e30
bf16 = jnp.bfloat16
f32 = jnp.float32
VMEM_BYTES = 20 * 1024 * 1024
SMALL_COST = pl.CostEstimate(flops=1024, bytes_accessed=1024, transcendentals=0)


def shift(value, axis, size, by):
    return lax.ppermute(value, axis, [(i, (i + by) % size) for i in range(size)])


def swap(value):
    return shift(value, "depth", 2, 1)


def attend_kernel(where_ref, q_ref, kv_ref, out_ref):
    depth = where_ref[0]
    half = q_ref.shape[0]
    keys = jnp.concatenate([kv_ref[0, :, :DH], kv_ref[1, :, :DH]], axis=0)
    values = jnp.concatenate([kv_ref[0, :, DH:], kv_ref[1, :, DH:]], axis=0)
    rows = jnp.concatenate([q_ref[:, h * DH : (h + 1) * DH] for h in range(GROUP)], axis=0)
    scores = lax.dot_general(
        rows, keys, (((1,), (1,)), ((), ())), preferred_element_type=f32
    ) * DH ** (-0.5)
    shape = scores.shape
    position = lax.broadcasted_iota(jnp.int32, shape, 0) % half + depth * half
    allowed = lax.broadcasted_iota(jnp.int32, shape, 1) <= position
    scores = jnp.where(allowed, scores, masked_score)
    top = jnp.max(scores, axis=-1, keepdims=True)
    expo = jnp.exp(scores - top)
    totals = jnp.sum(expo, axis=-1, keepdims=True)
    mixed = jnp.dot(expo.astype(bf16), values, preferred_element_type=f32) / totals
    mixed = mixed.astype(bf16)
    for h in range(GROUP):
        out_ref[:, h * DH : (h + 1) * DH] = mixed[h * half : (h + 1) * half]


def attend(where, queries, kv):
    half, features = queries.shape
    length = 2 * half
    return pl.pallas_call(
        attend_kernel,
        in_specs=[pl.BlockSpec(memory_space=pltpu.SMEM)]
        + [pl.BlockSpec(memory_space=pltpu.VMEM)] * 2,
        out_specs=pl.BlockSpec(memory_space=pltpu.VMEM),
        out_shape=jax.ShapeDtypeStruct((half, features), bf16),
        compiler_params=pltpu.CompilerParams(vmem_limit_bytes=VMEM_BYTES),
        cost_estimate=SMALL_COST,
    )(where, queries, kv)


ANYWHERE = pl.BlockSpec(memory_space=pl.ANY)
SCALARS = pl.BlockSpec(memory_space=pltpu.SMEM)
WHOLE = pl.BlockSpec(memory_space=pltpu.VMEM)


def out_kernel(where_ref, *refs):
    att, w_ref, own, other = refs[:4], refs[4], refs[5:9], refs[9:13]
    out_ref, far_a_ref, far_b_ref, att_buf, w_buf, att_sem, w_sem = refs[13:]
    depth, z, x, y = (where_ref[i] for i in range(4))
    rows = att[0].shape[0]
    cut = own[0].shape[0]
    quarter = own[2].shape[0]
    width = w_ref.shape[1]
    copies = [[] for _ in range(NY)]
    first = [
        pltpu.make_async_copy(ref, att_buf.at[pl.ds(k * rows, rows)], att_sem.at[k])
        for k, ref in enumerate(att)
    ]
    copies[0].append(pltpu.make_async_copy(w_ref, w_buf.at[0], w_sem.at[0]))
    slot = 1
    for side, blocks in ((depth, own), (1 - depth, other)):
        base = pl.multiple_of(side * cut, cut)
        for j, ref, start in (
            (1, blocks[0], 0),
            (3, blocks[1], 0),
            (2, blocks[2], 0),
            (2, blocks[3], quarter),
        ):
            place = w_buf.at[j, pl.ds(pl.multiple_of(base + start, quarter), ref.shape[0])]
            copies[j].append(pltpu.make_async_copy(ref, place, w_sem.at[slot]))
            slot += 1
    for copy in first:
        copy.start()
    for j in (0, 1, 3, 2):
        for copy in copies[j]:
            copy.start()
    for copy in first:
        copy.wait()
    for j in (0, 1, 3, 2):
        for copy in copies[j]:
            copy.wait()
        total = jnp.dot(att_buf[...], w_buf[j], preferred_element_type=f32).astype(bf16)
        block = (y + j) % NY
        columns = pl.ds(pl.multiple_of((block % 2) * width, width), width)
        for k in range(NX):
            place = 2 * ((x + k) % NX) + block // 2
            out_ref[place, :, columns] = total[k * rows : (k + 1) * rows]
    far = (z + NZ // 2) % NZ
    far_a_ref[...] = out_ref[far, : rows // 2]
    far_b_ref[...] = out_ref[far, rows // 2 :]


def out_project(where, attended, w_out, own, other):
    rows, features = attended[0].shape
    width = w_out.shape[1]
    return pl.pallas_call(
        out_kernel,
        in_specs=[SCALARS] + [ANYWHERE] * 13,
        out_specs=[WHOLE] * 3,
        out_shape=[jax.ShapeDtypeStruct((NZ, rows, 2 * width), bf16)]
        + [jax.ShapeDtypeStruct((rows // 2, 2 * width), bf16)] * 2,
        scratch_shapes=[
            pltpu.VMEM((NX * rows, features), bf16),
            pltpu.VMEM((NY, features, width), bf16),
            pltpu.SemaphoreType.DMA((NX,)),
            pltpu.SemaphoreType.DMA((9,)),
        ],
        compiler_params=pltpu.CompilerParams(vmem_limit_bytes=VMEM_BYTES),
        cost_estimate=SMALL_COST,
    )(where, *attended, w_out, *own, *other)


def gate_kernel(seqs, where_ref, *refs):
    own, other, weight_ref = refs[:NZ], refs[NZ : 2 * NZ], refs[2 * NZ]
    outs = refs[2 * NZ + 1 : -6]
    w_buf, x_buf, total_ref, square_ref, w_sem, x_sem = refs[-6:]
    z, x = where_ref[1], where_ref[2]
    rows, pair = own[0].shape
    chunk = w_buf.shape[1]
    chunks = w_buf.shape[0]
    per_pair = pair // chunk

    def rows_copy(ref, i, h, side):
        return pltpu.make_async_copy(
            ref,
            x_buf.at[h, pl.ds((2 * i + side) * rows, rows)],
            x_sem.at[i, h, side],
        )

    def weight_copy(c):
        return pltpu.make_async_copy(
            weight_ref.at[pl.ds(c * chunk, chunk)], w_buf.at[c], w_sem.at[c]
        )

    for h in range(2):
        for i, k in enumerate(seqs):
            ring = (2 * ((x + k) % NX) + h - z + NZ) % NZ
            for j in range(NZ):

                @pl.when(ring == j)
                def _():
                    rows_copy(own[j], i, h, 0).start()
                    rows_copy(other[j], i, h, 1).start()

        for c in range(h * per_pair, (h + 1) * per_pair):
            weight_copy(c).start()
    for c in range(chunks):
        h = c // per_pair
        if c % per_pair == 0:
            for i in range(len(seqs)):
                for side in range(2):
                    rows_copy(own[0], i, h, side).wait()
        weight_copy(c).wait()
        start = (c % per_pair) * chunk
        part = x_buf[h, :, start : start + chunk]
        add = jnp.dot(part, w_buf[c], preferred_element_type=f32)
        wide = part.astype(f32)
        wide = wide * wide
        square = sum(wide[:, n : n + DH] for n in range(0, chunk, DH))
        if c > 0:
            add = total_ref[...] + add
            square = square_ref[...] + square
        if c < chunks - 1:
            total_ref[...] = add
            square_ref[...] = square
        else:
            column = jnp.sum(square, axis=1, keepdims=True)
            column = jnp.broadcast_to(column, square.shape)
            for i in range(len(seqs)):
                held = slice(2 * i * rows, 2 * (i + 1) * rows)
                outs[2 * i][...] = add[held].astype(bf16)
                outs[2 * i + 1][...] = column[held].T[:8]


def gate_products(seqs, where, own, other, weights):
    rows, pair = own[0].shape
    features, width = weights.shape
    n = len(seqs)
    chunk = pair // 2
    return pl.pallas_call(
        functools.partial(gate_kernel, seqs),
        in_specs=[SCALARS] + [ANYWHERE] * (2 * NZ + 1),
        out_specs=[WHOLE] * (2 * n),
        scratch_shapes=[
            pltpu.VMEM((features // chunk, chunk, width), bf16),
            pltpu.VMEM((2, 2 * n * rows, pair), bf16),
            pltpu.VMEM((2 * n * rows, width), f32),
            pltpu.VMEM((2 * n * rows, DH), f32),
            pltpu.SemaphoreType.DMA((features // chunk,)),
            pltpu.SemaphoreType.DMA((n, 2, 2)),
        ],
        out_shape=[
            jax.ShapeDtypeStruct((2 * rows, width), bf16),
            jax.ShapeDtypeStruct((8, 2 * rows), f32),
        ]
        * n,
        compiler_params=pltpu.CompilerParams(vmem_limit_bytes=VMEM_BYTES),
        cost_estimate=SMALL_COST,
    )(where, *own, *other, weights)


def ring_kernel(offset, where_ref, parts_ref, right_ref, left_ref, *refs):
    z = where_ref[1]
    buf, sem = refs[-2:]
    if offset:
        sources = (parts_ref.at[(z + offset) % NZ], parts_ref.at[(z + NZ - offset) % NZ])
    else:
        sources = (parts_ref.at[z], refs[0])
    arrived = (right_ref, left_ref)
    starts = (0, buf.shape[1] - left_ref.shape[0])
    copies = []
    for i in range(2):
        copies.append(pltpu.make_async_copy(sources[i], buf.at[i], sem.at[i]))
        place = buf.at[2 + i, pl.ds(starts[i], arrived[i].shape[0])]
        copies.append(pltpu.make_async_copy(arrived[i], place, sem.at[2 + i]))
    for copy in copies:
        copy.start()
    for copy in copies:
        copy.wait()
    if not offset:
        refs[1][...] = (
            (buf[0].astype(f32) + buf[2].astype(f32) + buf[3].astype(f32)) + buf[1].astype(f32)
        ).astype(bf16)
        return
    for i in range(2):
        rows = arrived[i].shape[0]
        held = pl.ds(starts[i], rows)
        total = buf[i, held].astype(f32) + buf[2 + i, held].astype(f32)
        refs[i][held] = total.astype(bf16)
        if rows < buf.shape[1]:
            rest = pl.ds(rows - starts[i], rows)
            refs[i][rest] = buf[i, rest]


def ring_add(offset, where, parts, right, left, residual=None):
    _, rows, width = parts.shape
    extra = [] if residual is None else [residual]
    return pl.pallas_call(
        functools.partial(ring_kernel, offset),
        in_specs=[SCALARS] + [ANYWHERE] * (3 + len(extra)),
        out_specs=[WHOLE] * (2 - len(extra)),
        scratch_shapes=[pltpu.VMEM((4, rows, width), bf16), pltpu.SemaphoreType.DMA((4,))],
        out_shape=[jax.ShapeDtypeStruct((rows, width), bf16)] * (2 - len(extra)),
        compiler_params=pltpu.CompilerParams(vmem_limit_bytes=VMEM_BYTES),
        cost_estimate=SMALL_COST,
    )(where, parts, right, left, *extra)


def reduce_scatter_z(where, parts, far_a, far_b, residual):
    right = shift(far_a, "col", NZ, 1)
    left = shift(far_b, "col", NZ, -1)
    for offset in (3, 2, 1):
        right, left = ring_add(offset, where, parts, right, left)
        right = shift(right, "col", NZ, 1)
        left = shift(left, "col", NZ, -1)
    return ring_add(0, where, parts, right, left, residual)[0]


def all_gather_z(block):
    cut = block.shape[0] // 2
    right, left = [block], [block]
    swapped_right, swapped_left = [swap(block)], []
    for step in range(3):
        sent_right, sent_left = right[-1], left[-1]
        if step > 0:
            waited = (swapped_right[step - 1], swapped_left[max(step - 2, 0) : step - 1])
            (sent_right, sent_left), _ = lax.optimization_barrier(((sent_right, sent_left), waited))
            swapped_right.append(swap(right[step]))
            swapped_left.append(swap(left[step]))
        right.append(shift(sent_right, "col", NZ, 1))
        left.append(shift(sent_left, "col", NZ, -1))
    (sent_right, sent_left), _ = lax.optimization_barrier(
        ((right[3], left[3]), (swapped_right[2], swapped_left[1]))
    )
    swapped_right.append(swap(right[3]))
    swapped_left.append(swap(left[3]))
    far_a = shift(sent_right[:cut], "col", NZ, 1)
    far_b = shift(sent_left[cut:], "col", NZ, -1)
    far = jnp.concatenate([far_a, far_b], axis=0)
    own = [block, left[1], left[2], left[3], far, right[3], right[2], right[1]]
    other = [swapped_right[0], *swapped_left, swap(far), *swapped_right[:0:-1]]
    return own, other


def work_to_natural(m):
    pairs = []
    for y in range(NY):
        for z in range(NZ):
            there = 2 * (z % 2) + (m ^ (y % 2)), 2 * (z // 2) + y // 2
            pairs.append((y * NZ + z, there[0] * NZ + there[1]))
    return pairs


def per_device(queries, key_states, value_states, residual, gain, w_out, w_gate, w_up):
    half = queries.shape[1]
    depth, x, y, z = (lax.axis_index(name) for name in ("depth", "x", "y", "col"))
    odd = (y % 2) == 1
    where = jnp.stack([depth, z, x, y]).astype(jnp.int32)
    block = w_out.shape[1]

    out_rows = w_out.shape[0] // 2
    quarter = out_rows // 2
    wo_half = lax.dynamic_slice_in_dim(w_out, depth * out_rows, out_rows, 0)
    wo_next = shift(wo_half, "y", NY, -1)
    wo_last = shift(wo_half, "y", NY, 1)
    wo_own = [
        wo_next,
        wo_last,
        shift(wo_next[:quarter], "y", NY, -1),
        shift(wo_last[quarter:], "y", NY, 1),
    ]
    wo_other = [swap(block) for block in wo_own]

    kv = jnp.concatenate([key_states[0], value_states[0]], axis=1)
    kv = lax.all_gather(kv, "depth", axis=0)
    attended = attend(where, queries[0], kv)

    units = w_gate.shape[1] // 2
    scaled_gate = lax.dynamic_slice_in_dim(w_gate, depth * units, units, 1).astype(f32) * gain[:, None]
    scaled_up = lax.dynamic_slice_in_dim(w_up, depth * units, units, 1).astype(f32) * gain[:, None]
    w2_half = jnp.concatenate([scaled_gate.astype(bf16), scaled_up.astype(bf16)], axis=1)
    four = [
        attended,
        shift(attended, "x", NX, -1),
        shift(attended, "x", NX, 2),
        shift(attended, "x", NX, 1),
    ]

    axes = ("y", "col")
    residual, _ = lax.optimization_barrier((residual, attended))
    got = []
    for m in range(2):
        sent = jnp.where(odd, residual[1 - m], residual[m])
        got.append(lax.ppermute(sent, axes, [(b, a) for a, b in work_to_natural(m)]))
    res_work = jnp.concatenate(
        [jnp.where(odd, got[1], got[0]), jnp.where(odd, got[0], got[1])], axis=1
    )

    early = (four, wo_own, wo_other[:2], res_work)
    w2_half, _ = lax.optimization_barrier((w2_half, early))
    w2 = lax.all_gather(w2_half, "y", axis=0, tiled=True)
    four, res_work = lax.optimization_barrier((four, res_work))
    parts, far_a, far_b = out_project(where, four, w_out, wo_own, wo_other)
    stream = reduce_scatter_z(where, parts, far_a, far_b, res_work)

    own, other = all_gather_z(stream)

    far, far_square = gate_products((2,), where, own, other, w2)
    pairs = []
    for i in range(NX):
        pairs.append((i, (i + 1) % NX))
    for i in range(NX):
        pairs.append((NX + i, NX + (i - 1) % NX))
    far = lax.ppermute(far, ("depth", "x"), pairs).astype(f32)
    near_right, right_square, near_left, left_square = gate_products((1, 3), where, own, other, w2)
    near_right = (near_right.astype(f32) + jnp.where(depth == 0, far, 0.0)).astype(bf16)
    near_left = (near_left.astype(f32) + jnp.where(depth == 1, far, 0.0)).astype(bf16)
    from_left = shift(near_right, "x", NX, 1)
    from_right = shift(near_left, "x", NX, -1)
    mine, mine_square = gate_products((0,), where, own, other, w2)

    (far_square, right_square, left_square, stream_late), _ = lax.optimization_barrier(
        ((far_square, right_square, left_square, stream), mine)
    )
    square_total = (
        mine_square[0]
        + shift(right_square, "x", NX, 1)[0]
        + shift(far_square, "x", NX, 2)[0]
        + shift(left_square, "x", NX, -1)[0]
    )
    inverse = lax.rsqrt(square_total / D + eps_norm)[:, None]
    back = []
    for m in range(2):
        first, second = stream_late[:, :block], stream_late[:, block:]
        sent = jnp.where(odd, second, first) if m == 0 else jnp.where(odd, first, second)
        back.append(lax.ppermute(sent, axes, work_to_natural(m)))
    stream_out = jnp.stack(
        [jnp.where(odd, back[1], back[0]), jnp.where(odd, back[0], back[1])]
    )

    total = (mine.astype(f32) + from_left.astype(f32) + from_right.astype(f32)) * inverse
    hidden_both = (jax.nn.silu(total[:, :units]) * total[:, units:]).astype(bf16)
    hidden_own = hidden_both[:half]
    hidden_other = swap(hidden_both[half:])
    hidden = jnp.where(
        depth == 0,
        jnp.concatenate([hidden_own, hidden_other], axis=1),
        jnp.concatenate([hidden_other, hidden_own], axis=1),
    )
    return (hidden[None], stream_out)


def solution(mesh):
    fine = Mesh(mesh.devices.reshape(2, NX, NY, NZ), ("depth", "x", "y", "col"))
    row = ("x", "y")
    return jax.shard_map(
        per_device,
        mesh=fine,
        in_specs=(
            P(row, "depth", "col"),
            P(row, "depth", "col"),
            P(row, "depth", "col"),
            P("col", "depth", row),
            P(row),
            P("col", row),
            P(row, "col"),
            P(row, "col"),
        ),
        out_specs=(P(row, "depth", "col"), P("col", "depth", row)),
        check_vma=False,
    )
```

```python
import functools
import jax
import jax.numpy as jnp
from jax import lax
from jax.experimental import pallas as pl
from jax.experimental.pallas import tpu as pltpu
from jax.sharding import Mesh, PartitionSpec as P

D = 8192
DH = 128
GROUP = 8
NX = 4
NY = 4
NZ = 8
EXTRA = 16

eps_norm = 1e-05
masked_score = -1e30
bf16 = jnp.bfloat16
f32 = jnp.float32
VMEM_BYTES = 20 * 1024 * 1024
SMALL_COST = pl.CostEstimate(flops=1024, bytes_accessed=1024, transcendentals=0)


def shift(value, axis, size, by):
    return lax.ppermute(value, axis, [(i, (i + by) % size) for i in range(size)])


def swap(value):
    return shift(value, "depth", 2, 1)


def attend_kernel(where_ref, q_ref, kv_ref, out_ref):
    depth = where_ref[0]
    half = q_ref.shape[0]
    keys = jnp.concatenate([kv_ref[0, :, :DH], kv_ref[1, :, :DH]], axis=0)
    values = jnp.concatenate([kv_ref[0, :, DH:], kv_ref[1, :, DH:]], axis=0)
    rows = jnp.concatenate([q_ref[:, h * DH : (h + 1) * DH] for h in range(GROUP)], axis=0)
    scores = lax.dot_general(
        rows, keys, (((1,), (1,)), ((), ())), preferred_element_type=f32
    ) * DH ** (-0.5)
    shape = scores.shape
    position = lax.broadcasted_iota(jnp.int32, shape, 0) % half + depth * half
    allowed = lax.broadcasted_iota(jnp.int32, shape, 1) <= position
    scores = jnp.where(allowed, scores, masked_score)
    top = jnp.max(scores, axis=-1, keepdims=True)
    expo = jnp.exp(scores - top)
    totals = jnp.sum(expo, axis=-1, keepdims=True)
    mixed = jnp.dot(expo.astype(bf16), values, preferred_element_type=f32) / totals
    mixed = mixed.astype(bf16)
    for h in range(GROUP):
        out_ref[:, h * DH : (h + 1) * DH] = mixed[h * half : (h + 1) * half]


def attend(where, queries, kv):
    half, features = queries.shape
    length = 2 * half
    return pl.pallas_call(
        attend_kernel,
        in_specs=[pl.BlockSpec(memory_space=pltpu.SMEM)]
        + [pl.BlockSpec(memory_space=pltpu.VMEM)] * 2,
        out_specs=pl.BlockSpec(memory_space=pltpu.VMEM),
        out_shape=jax.ShapeDtypeStruct((half, features), bf16),
        compiler_params=pltpu.CompilerParams(vmem_limit_bytes=VMEM_BYTES),
        cost_estimate=SMALL_COST,
    )(where, queries, kv)


ANYWHERE = pl.BlockSpec(memory_space=pl.ANY)
IN_HBM = pl.BlockSpec(memory_space=pltpu.HBM)
SCALARS = pl.BlockSpec(memory_space=pltpu.SMEM)
WHOLE = pl.BlockSpec(memory_space=pltpu.VMEM)


def out_kernel(where_ref, *refs):
    att, w_ref, own, other = refs[:4], refs[4], refs[5:9], refs[9:13]
    out_ref, far_a_ref, far_b_ref, att_buf, w_buf, att_sem, w_sem = refs[13:]
    depth, z, x, y = (where_ref[i] for i in range(4))
    rows = att[0].shape[0]
    cut = own[0].shape[0]
    quarter = own[2].shape[0]
    width = w_ref.shape[1]
    copies = [[] for _ in range(NY)]
    first = [
        pltpu.make_async_copy(ref, att_buf.at[pl.ds(k * rows, rows)], att_sem.at[k])
        for k, ref in enumerate(att)
    ]
    copies[0].append(pltpu.make_async_copy(w_ref, w_buf.at[0], w_sem.at[0]))
    slot = 1
    for side, blocks in ((depth, own), (1 - depth, other)):
        base = pl.multiple_of(side * cut, cut)
        for j, ref, start in (
            (1, blocks[0], 0),
            (3, blocks[1], 0),
            (2, blocks[2], 0),
            (2, blocks[3], quarter),
        ):
            place = w_buf.at[j, pl.ds(pl.multiple_of(base + start, quarter), ref.shape[0])]
            copies[j].append(pltpu.make_async_copy(ref, place, w_sem.at[slot]))
            slot += 1
    for copy in first:
        copy.start()
    for j in (0, 1, 3, 2):
        for copy in copies[j]:
            copy.start()
    for copy in first:
        copy.wait()
    for j in (0, 1, 3, 2):
        for copy in copies[j]:
            copy.wait()
        total = jnp.dot(att_buf[...], w_buf[j], preferred_element_type=f32).astype(bf16)
        block = (y + j) % NY
        columns = pl.ds(pl.multiple_of((block % 2) * width, width), width)
        for k in range(NX):
            place = 2 * ((x + k) % NX) + block // 2
            out_ref[place, :, columns] = total[k * rows : (k + 1) * rows]
    far = (z + NZ // 2) % NZ
    far_a_ref[...] = out_ref[far, : rows // 2]
    far_b_ref[...] = out_ref[far, rows // 2 :]


def out_project(where, attended, w_out, own, other):
    rows, features = attended[0].shape
    width = w_out.shape[1]
    return pl.pallas_call(
        out_kernel,
        in_specs=[SCALARS] + [ANYWHERE] * 4 + [IN_HBM] + [ANYWHERE] * 8,
        out_specs=[WHOLE] * 3,
        out_shape=[jax.ShapeDtypeStruct((NZ, rows, 2 * width), bf16)]
        + [jax.ShapeDtypeStruct((rows // 2, 2 * width), bf16)] * 2,
        scratch_shapes=[
            pltpu.VMEM((NX * rows, features), bf16),
            pltpu.VMEM((NY, features, width), bf16),
            pltpu.SemaphoreType.DMA((NX,)),
            pltpu.SemaphoreType.DMA((9,)),
        ],
        compiler_params=pltpu.CompilerParams(vmem_limit_bytes=VMEM_BYTES),
        cost_estimate=SMALL_COST,
    )(where, *attended, w_out, *own, *other)


def put_squares(ref, row):
    rows = ref.shape[0] - EXTRA
    high = row.astype(bf16)
    rest = row - high.astype(f32)
    middle = rest.astype(bf16)
    low = (rest - middle.astype(f32)).astype(bf16)
    index = lax.broadcasted_iota(jnp.int32, row.shape, 0)
    first = jnp.where(index == 0, high.astype(f32), jnp.where(index == 1, middle.astype(f32), 0.0))
    first = jnp.where(index == 2, low.astype(f32), first)
    both = jnp.concatenate([first, jnp.zeros_like(first)], axis=0).astype(bf16)
    ref[rows:] = jnp.zeros((EXTRA, ref.shape[1]), bf16)
    ref[rows:, : row.shape[1]] = both


def get_squares(ref, count):
    held = ref[ref.shape[0] - EXTRA :, :count].astype(f32)
    return jnp.broadcast_to(jnp.sum(held, axis=0, keepdims=True), (8, count))


def near_kernel(where_ref, far_ref, right_ref, right_sq_ref, left_ref, left_sq_ref, *outs):
    rows = right_ref.shape[0]
    far = far_ref[:rows].astype(f32)
    far_square = get_squares(far_ref, rows)
    for i, (ref, sq_ref) in enumerate(((right_ref, right_sq_ref), (left_ref, left_sq_ref))):
        mine = where_ref[0] == i
        total = ref[...].astype(f32) + jnp.where(mine, far, 0.0)
        outs[i][:rows] = total.astype(bf16)
        put_squares(outs[i], sq_ref[...] + jnp.where(mine, far_square, 0.0))


def near_sums(where, far, right, right_square, left, left_square):
    return pl.pallas_call(
        near_kernel,
        in_specs=[SCALARS] + [WHOLE] * 5,
        out_specs=[WHOLE] * 2,
        out_shape=[jax.ShapeDtypeStruct(far.shape, bf16)] * 2,
        compiler_params=pltpu.CompilerParams(vmem_limit_bytes=VMEM_BYTES),
        cost_estimate=SMALL_COST,
    )(where, far, right, right_square, left, left_square)


def last_kernel(mine_ref, square_ref, left_ref, right_ref, *outs):
    rows, width = mine_ref.shape
    units = width // 2
    squares = square_ref[...] + get_squares(left_ref, rows) + get_squares(right_ref, rows)
    squares = jnp.broadcast_to(squares[:1], (DH, rows)).T[:, :1]
    inverse = lax.rsqrt(squares / D + eps_norm)
    total = mine_ref[...].astype(f32) + left_ref[:rows].astype(f32) + right_ref[:rows].astype(f32)
    total = total * inverse
    gate, up = total[:, :units], total[:, units:]
    hidden = (gate / (1.0 + jnp.exp(-gate)) * up).astype(bf16)
    for i in range(2):
        outs[i][...] = hidden[i * rows // 2 : (i + 1) * rows // 2]


def last_sums(mine, square, left, right):
    rows, width = mine.shape
    return pl.pallas_call(
        last_kernel,
        in_specs=[WHOLE] * 4,
        out_specs=[WHOLE] * 2,
        out_shape=[jax.ShapeDtypeStruct((rows // 2, width // 2), bf16)] * 2,
        compiler_params=pltpu.CompilerParams(vmem_limit_bytes=VMEM_BYTES),
        cost_estimate=SMALL_COST,
    )(mine, square, left, right)


def gate_kernel(seqs, where_ref, *refs):
    own, other, weight_ref = refs[:NZ], refs[NZ : 2 * NZ], refs[2 * NZ]
    outs = refs[2 * NZ + 1 : -6]
    w_buf, x_buf, total_ref, square_ref, w_sem, x_sem = refs[-6:]
    z, x = where_ref[1], where_ref[2]
    rows, pair = own[0].shape
    chunk = w_buf.shape[1]
    chunks = w_buf.shape[0]
    per_pair = pair // chunk

    def rows_copy(ref, i, h, side):
        return pltpu.make_async_copy(
            ref,
            x_buf.at[h, pl.ds((2 * i + side) * rows, rows)],
            x_sem.at[i, h, side],
        )

    def weight_copy(c):
        return pltpu.make_async_copy(
            weight_ref.at[pl.ds(c * chunk, chunk)], w_buf.at[c], w_sem.at[c]
        )

    for h in range(2):
        for i, k in enumerate(seqs):
            ring = (2 * ((x + k) % NX) + h - z + NZ) % NZ
            for j in range(NZ):

                @pl.when(ring == j)
                def _():
                    rows_copy(own[j], i, h, 0).start()
                    rows_copy(other[j], i, h, 1).start()

        for c in range(h * per_pair, (h + 1) * per_pair):
            weight_copy(c).start()
    for c in range(chunks):
        h = c // per_pair
        if c % per_pair == 0:
            for i in range(len(seqs)):
                for side in range(2):
                    rows_copy(own[0], i, h, side).wait()
        weight_copy(c).wait()
        start = (c % per_pair) * chunk
        part = x_buf[h, :, start : start + chunk]
        add = jnp.dot(part, w_buf[c], preferred_element_type=f32)
        wide = part.astype(f32)
        wide = wide * wide
        square = sum(wide[:, n : n + DH] for n in range(0, chunk, DH))
        if c > 0:
            add = total_ref[...] + add
            square = square_ref[...] + square
        if c < chunks - 1:
            total_ref[...] = add
            square_ref[...] = square
        else:
            column = jnp.sum(square, axis=1, keepdims=True)
            column = jnp.broadcast_to(column, square.shape)
            for i in range(len(seqs)):
                held = slice(2 * i * rows, 2 * (i + 1) * rows)
                row = column[held].T[:8]
                if len(outs) == 1:
                    outs[0][: 2 * rows] = add[held].astype(bf16)
                    put_squares(outs[0], row)
                else:
                    outs[2 * i][...] = add[held].astype(bf16)
                    outs[2 * i + 1][...] = row


def gate_products(seqs, where, own, other, weights, to_send=False):
    rows, pair = own[0].shape
    features, width = weights.shape
    n = len(seqs)
    chunk = pair // 2
    if to_send:
        outs = [jax.ShapeDtypeStruct((2 * rows + EXTRA, width), bf16)]
    else:
        outs = [
            jax.ShapeDtypeStruct((2 * rows, width), bf16),
            jax.ShapeDtypeStruct((8, 2 * rows), f32),
        ] * n
    return pl.pallas_call(
        functools.partial(gate_kernel, seqs),
        in_specs=[SCALARS] + [ANYWHERE] * (2 * NZ) + [IN_HBM],
        out_specs=[WHOLE] * len(outs),
        scratch_shapes=[
            pltpu.VMEM((features // chunk, chunk, width), bf16),
            pltpu.VMEM((2, 2 * n * rows, pair), bf16),
            pltpu.VMEM((2 * n * rows, width), f32),
            pltpu.VMEM((2 * n * rows, DH), f32),
            pltpu.SemaphoreType.DMA((features // chunk,)),
            pltpu.SemaphoreType.DMA((n, 2, 2)),
        ],
        out_shape=outs,
        compiler_params=pltpu.CompilerParams(vmem_limit_bytes=VMEM_BYTES),
        cost_estimate=SMALL_COST,
    )(where, *own, *other, weights)


def ring_kernel(offset, where_ref, parts_ref, right_ref, left_ref, *refs):
    z = where_ref[1]
    buf, sem = refs[-2:]
    if offset:
        sources = (parts_ref.at[(z + offset) % NZ], parts_ref.at[(z + NZ - offset) % NZ])
    else:
        sources = (parts_ref.at[z], refs[0])
    arrived = (right_ref, left_ref)
    starts = (0, buf.shape[1] - left_ref.shape[0])
    copies = []
    for i in range(2):
        copies.append(pltpu.make_async_copy(sources[i], buf.at[i], sem.at[i]))
        place = buf.at[2 + i, pl.ds(starts[i], arrived[i].shape[0])]
        copies.append(pltpu.make_async_copy(arrived[i], place, sem.at[2 + i]))
    for copy in copies:
        copy.start()
    for copy in copies:
        copy.wait()
    if not offset:
        refs[1][...] = (
            (buf[0].astype(f32) + buf[2].astype(f32) + buf[3].astype(f32)) + buf[1].astype(f32)
        ).astype(bf16)
        return
    for i in range(2):
        rows = arrived[i].shape[0]
        held = pl.ds(starts[i], rows)
        total = buf[i, held].astype(f32) + buf[2 + i, held].astype(f32)
        refs[i][held] = total.astype(bf16)
        if rows < buf.shape[1]:
            rest = pl.ds(rows - starts[i], rows)
            refs[i][rest] = buf[i, rest]


def ring_add(offset, where, parts, right, left, residual=None):
    _, rows, width = parts.shape
    extra = [] if residual is None else [residual]
    return pl.pallas_call(
        functools.partial(ring_kernel, offset),
        in_specs=[SCALARS] + [ANYWHERE] * (3 + len(extra)),
        out_specs=[WHOLE] * (2 - len(extra)),
        scratch_shapes=[pltpu.VMEM((4, rows, width), bf16), pltpu.SemaphoreType.DMA((4,))],
        out_shape=[jax.ShapeDtypeStruct((rows, width), bf16)] * (2 - len(extra)),
        compiler_params=pltpu.CompilerParams(vmem_limit_bytes=VMEM_BYTES),
        cost_estimate=SMALL_COST,
    )(where, parts, right, left, *extra)


def reduce_scatter_z(where, parts, far_a, far_b, residual):
    right = shift(far_a, "col", NZ, 1)
    left = shift(far_b, "col", NZ, -1)
    (right, left), residual = lax.optimization_barrier(((right, left), residual))
    for offset in (3, 2, 1):
        right, left = ring_add(offset, where, parts, right, left)
        right = shift(right, "col", NZ, 1)
        left = shift(left, "col", NZ, -1)
    return ring_add(0, where, parts, right, left, residual)[0]


def all_gather_z(block):
    cut = block.shape[0] // 2
    right, left = [block], [block]
    swapped_right, swapped_left = [swap(block)], []
    for step in range(3):
        sent_right, sent_left = right[-1], left[-1]
        if step > 0:
            waited = (swapped_right[step - 1], swapped_left[max(step - 2, 0) : step - 1])
            (sent_right, sent_left), _ = lax.optimization_barrier(((sent_right, sent_left), waited))
            swapped_right.append(swap(right[step]))
            swapped_left.append(swap(left[step]))
        right.append(shift(sent_right, "col", NZ, 1))
        left.append(shift(sent_left, "col", NZ, -1))
    (sent_right, sent_left), _ = lax.optimization_barrier(
        ((right[3], left[3]), (swapped_right[2], swapped_left[1]))
    )
    swapped_right.append(swap(right[3]))
    swapped_left.append(swap(left[3]))
    far_a = shift(sent_right[:cut], "col", NZ, 1)
    far_b = shift(sent_left[cut:], "col", NZ, -1)
    far = jnp.concatenate([far_a, far_b], axis=0)
    own = [block, left[1], left[2], left[3], far, right[3], right[2], right[1]]
    other = [swapped_right[0], *swapped_left, swap(far), *swapped_right[:0:-1]]
    return own, other


def work_to_natural(m):
    pairs = []
    for y in range(NY):
        for z in range(NZ):
            there = 2 * (z % 2) + (m ^ (y % 2)), 2 * (z // 2) + y // 2
            pairs.append((y * NZ + z, there[0] * NZ + there[1]))
    return pairs


def per_device(queries, key_states, value_states, residual, gain, w_out, w_gate, w_up):
    half = queries.shape[1]
    depth, x, y, z = (lax.axis_index(name) for name in ("depth", "x", "y", "col"))
    odd = (y % 2) == 1
    where = jnp.stack([depth, z, x, y]).astype(jnp.int32)
    block = w_out.shape[1]

    out_rows = w_out.shape[0] // 2
    quarter = out_rows // 2
    wo_half = lax.dynamic_slice_in_dim(w_out, depth * out_rows, out_rows, 0)
    wo_next = shift(wo_half, "y", NY, -1)
    wo_last = shift(wo_half, "y", NY, 1)
    wo_own = [
        wo_next,
        wo_last,
        shift(wo_next[:quarter], "y", NY, -1),
        shift(wo_last[quarter:], "y", NY, 1),
    ]
    wo_other = [swap(block) for block in wo_own]

    kv = jnp.concatenate([key_states[0], value_states[0]], axis=1)
    kv = lax.all_gather(kv, "depth", axis=0)
    attended = attend(where, queries[0], kv)

    units = w_gate.shape[1] // 2
    scaled_gate = lax.dynamic_slice_in_dim(w_gate, depth * units, units, 1).astype(f32) * gain[:, None]
    scaled_up = lax.dynamic_slice_in_dim(w_up, depth * units, units, 1).astype(f32) * gain[:, None]
    w2_half = jnp.concatenate([scaled_gate.astype(bf16), scaled_up.astype(bf16)], axis=1)
    four = [
        attended,
        shift(attended, "x", NX, -1),
        shift(attended, "x", NX, 2),
        shift(attended, "x", NX, 1),
    ]

    axes = ("y", "col")
    residual, _ = lax.optimization_barrier((residual, wo_own[2:]))
    got = []
    for m in range(2):
        sent = jnp.where(odd, residual[1 - m], residual[m])
        got.append(lax.ppermute(sent, axes, [(b, a) for a, b in work_to_natural(m)]))
    res_work = jnp.concatenate(
        [jnp.where(odd, got[1], got[0]), jnp.where(odd, got[0], got[1])], axis=1
    )

    early = (four, wo_own, wo_other[:2])
    w2_half, _ = lax.optimization_barrier((w2_half, early))
    w2 = lax.all_gather(w2_half, "y", axis=0, tiled=True)
    parts, far_a, far_b = out_project(where, four, w_out, wo_own, wo_other)
    stream = reduce_scatter_z(where, parts, far_a, far_b, res_work)

    own, other = all_gather_z(stream)

    (far,) = gate_products((2,), where, own, other, w2, to_send=True)
    pairs = []
    for i in range(NX):
        pairs.append((i, (i + 1) % NX))
    for i in range(NX):
        pairs.append((NX + i, NX + (i - 1) % NX))
    far = lax.ppermute(far, ("depth", "x"), pairs)
    near = gate_products((1, 3), where, own, other, w2)
    near_right, near_left = near_sums(where, far, *near)
    from_left = shift(near_right, "x", NX, 1)
    from_right = shift(near_left, "x", NX, -1)

    stream_late, _ = lax.optimization_barrier((stream, (near_right, near_left)))
    back = []
    for m in range(2):
        first, second = stream_late[:, :block], stream_late[:, block:]
        sent = jnp.where(odd, second, first) if m == 0 else jnp.where(odd, first, second)
        back.append(lax.ppermute(sent, axes, work_to_natural(m)))
    late, back = lax.optimization_barrier((where, back))
    stream_out = jnp.stack(
        [jnp.where(odd, back[1], back[0]), jnp.where(odd, back[0], back[1])]
    )
    mine, mine_square = gate_products((0,), late, own, other, w2)
    hidden_own, hidden_other = last_sums(mine, mine_square, from_left, from_right)
    hidden_other = swap(hidden_other)
    hidden = jnp.where(
        depth == 0,
        jnp.concatenate([hidden_own, hidden_other], axis=1),
        jnp.concatenate([hidden_other, hidden_own], axis=1),
    )
    return (hidden[None], stream_out)


def solution(mesh):
    fine = Mesh(mesh.devices.reshape(2, NX, NY, NZ), ("depth", "x", "y", "col"))
    row = ("x", "y")
    return jax.shard_map(
        per_device,
        mesh=fine,
        in_specs=(
            P(row, "depth", "col"),
            P(row, "depth", "col"),
            P(row, "depth", "col"),
            P("col", "depth", row),
            P(row),
            P("col", row),
            P(row, "col"),
            P(row, "col"),
        ),
        out_specs=(P(row, "depth", "col"), P("col", "depth", row)),
        check_vma=False,
    )
```

```python
import functools
import jax
import jax.numpy as jnp
from jax import lax
from jax.experimental import pallas as pl
from jax.experimental.pallas import tpu as pltpu
from jax.sharding import Mesh, PartitionSpec as P

D = 8192
DH = 128
GROUP = 8
NX = 4
NY = 4
NZ = 8
EXTRA = 16

eps_norm = 1e-05
masked_score = -1e30
bf16 = jnp.bfloat16
f32 = jnp.float32
VMEM_BYTES = 24 * 1024 * 1024
SMALL_COST = pl.CostEstimate(flops=1024, bytes_accessed=1024, transcendentals=0)


def shift(value, axis, size, by):
    return lax.ppermute(value, axis, [(i, (i + by) % size) for i in range(size)])


def in_hbm(value):
    return pltpu.with_memory_space_constraint(value, pltpu.HBM)


def swap(value):
    return shift(value, "depth", 2, 1)


def attend_kernel(where_ref, q_ref, kv_ref, out_ref):
    depth = where_ref[0]
    half = q_ref.shape[0]
    keys = jnp.concatenate([kv_ref[0, :, :DH], kv_ref[1, :, :DH]], axis=0)
    values = jnp.concatenate([kv_ref[0, :, DH:], kv_ref[1, :, DH:]], axis=0)
    rows = jnp.concatenate([q_ref[:, h * DH : (h + 1) * DH] for h in range(GROUP)], axis=0)
    scores = lax.dot_general(
        rows, keys, (((1,), (1,)), ((), ())), preferred_element_type=f32
    ) * DH ** (-0.5)
    shape = scores.shape
    position = lax.broadcasted_iota(jnp.int32, shape, 0) % half + depth * half
    allowed = lax.broadcasted_iota(jnp.int32, shape, 1) <= position
    scores = jnp.where(allowed, scores, masked_score)
    top = jnp.max(scores, axis=-1, keepdims=True)
    expo = jnp.exp(scores - top)
    totals = jnp.sum(expo, axis=-1, keepdims=True)
    mixed = jnp.dot(expo.astype(bf16), values, preferred_element_type=f32) / totals
    mixed = mixed.astype(bf16)
    for h in range(GROUP):
        out_ref[:, h * DH : (h + 1) * DH] = mixed[h * half : (h + 1) * half]


def attend(where, queries, kv):
    half, features = queries.shape
    length = 2 * half
    return pl.pallas_call(
        attend_kernel,
        in_specs=[pl.BlockSpec(memory_space=pltpu.SMEM)]
        + [pl.BlockSpec(memory_space=pltpu.VMEM)] * 2,
        out_specs=pl.BlockSpec(memory_space=pltpu.VMEM),
        out_shape=jax.ShapeDtypeStruct((half, features), bf16),
        compiler_params=pltpu.CompilerParams(vmem_limit_bytes=VMEM_BYTES),
        cost_estimate=SMALL_COST,
    )(where, queries, kv)


ANYWHERE = pl.BlockSpec(memory_space=pl.ANY)
SCALARS = pl.BlockSpec(memory_space=pltpu.SMEM)
WHOLE = pl.BlockSpec(memory_space=pltpu.VMEM)


def out_kernel(where_ref, *refs):
    own, other, w_ref, pieces = refs[:4], refs[4:8], refs[8], refs[9:15]
    out_ref, far_a_ref, far_b_ref, att_buf, w_buf, att_sem, w_sem = refs[15:]
    depth, z, x, y = (where_ref[i] for i in range(4))
    rows = own[0].shape[0]
    width = w_buf.shape[2]
    cut = pieces[0].shape[0]
    first = []
    for k in range(NX):
        for i, (side, ref) in enumerate(((depth, own[k]), (1 - depth, other[k]))):
            place = pl.ds(pl.multiple_of((2 * k + side) * rows, rows), rows)
            first.append(pltpu.make_async_copy(ref, att_buf.at[place], att_sem.at[k, i]))
    columns = pl.ds(pl.multiple_of(depth * width, width), width)
    copies = [[pltpu.make_async_copy(w_ref.at[:, columns], w_buf.at[0], w_sem.at[0, 0])]]
    for j in range(1, NY):
        copies.append([])
        for i in range(2):
            place = w_buf.at[j, pl.ds(i * cut, cut)]
            copies[j].append(pltpu.make_async_copy(pieces[2 * j - 2 + i], place, w_sem.at[j, i]))
    for copy in first:
        copy.start()
    for j in range(NY):
        for copy in copies[j]:
            copy.start()
    for copy in first:
        copy.wait()
    for j in range(NY):
        for copy in copies[j]:
            copy.wait()
        total = jnp.dot(att_buf[...], w_buf[j], preferred_element_type=f32).astype(bf16)
        block = (y + j) % NY
        held = pl.ds(pl.multiple_of((block % 2) * width, width), width)
        for k in range(NX):
            place = 2 * ((x + k) % NX) + block // 2
            out_ref[place, :, held] = total[2 * k * rows : 2 * (k + 1) * rows]
    far = (z + NZ // 2) % NZ
    far_a_ref[...] = out_ref[far, :rows]
    far_b_ref[...] = out_ref[far, rows:]


def out_project(where, own, other, w_out, pieces):
    rows, features = own[0].shape
    width = w_out.shape[1] // 2
    return pl.pallas_call(
        out_kernel,
        in_specs=[SCALARS] + [ANYWHERE] * 15,
        out_specs=[WHOLE] * 3,
        out_shape=[jax.ShapeDtypeStruct((NZ, 2 * rows, 2 * width), bf16)]
        + [jax.ShapeDtypeStruct((rows, 2 * width), bf16)] * 2,
        scratch_shapes=[
            pltpu.VMEM((2 * NX * rows, features), bf16),
            pltpu.VMEM((NY, features, width), bf16),
            pltpu.SemaphoreType.DMA((NX, 2)),
            pltpu.SemaphoreType.DMA((NY, 2)),
        ],
        compiler_params=pltpu.CompilerParams(vmem_limit_bytes=VMEM_BYTES),
        cost_estimate=SMALL_COST,
    )(where, *own, *other, in_hbm(w_out), *pieces)


def put_squares(ref, row):
    rows = ref.shape[0] - EXTRA
    high = row.astype(bf16)
    rest = row - high.astype(f32)
    middle = rest.astype(bf16)
    low = (rest - middle.astype(f32)).astype(bf16)
    index = lax.broadcasted_iota(jnp.int32, row.shape, 0)
    first = jnp.where(index == 0, high.astype(f32), jnp.where(index == 1, middle.astype(f32), 0.0))
    first = jnp.where(index == 2, low.astype(f32), first)
    both = jnp.concatenate([first, jnp.zeros_like(first)], axis=0).astype(bf16)
    ref[rows:] = jnp.zeros((EXTRA, ref.shape[1]), bf16)
    ref[rows:, : row.shape[1]] = both


def get_squares(ref, count):
    held = ref[ref.shape[0] - EXTRA :, :count].astype(f32)
    return jnp.broadcast_to(jnp.sum(held, axis=0, keepdims=True), (8, count))


def gate_kernel(seqs, where_ref, *refs):
    blocks, weight_ref = refs[:NZ], refs[NZ]
    outs = refs[NZ + 1 : -4]
    w_buf, x_buf, w_sem, x_sem = refs[-4:]
    depth, z, x = (where_ref[i] for i in range(3))
    rows, pair = blocks[0].shape[0] // 2, blocks[0].shape[1]
    chunks, _, chunk = w_buf.shape

    def rows_copy(ref, i, h, side):
        place = depth if side == 0 else 1 - depth
        return pltpu.make_async_copy(
            ref.at[pl.ds(pl.multiple_of(place * rows, rows), rows)],
            x_buf.at[pl.ds((2 * i + side) * rows, rows), pl.ds(h * pair, pair)],
            x_sem.at[i, h, side],
        )

    def weight_copy(c):
        return pltpu.make_async_copy(
            weight_ref.at[:, pl.ds(c * chunk, chunk)], w_buf.at[c], w_sem.at[c]
        )

    for c in range(chunks):
        weight_copy(c).start()
    for h in range(2):
        for i, k in enumerate(seqs):
            ring = (2 * ((x + k) % NX) + h - z + NZ) % NZ
            for j in range(NZ):

                @pl.when(ring == j)
                def _():
                    rows_copy(blocks[j], i, h, 0).start()
                    rows_copy(blocks[j], i, h, 1).start()

    for h in range(2):
        for i in range(len(seqs)):
            for side in range(2):
                rows_copy(blocks[0], i, h, side).wait()
    squares = 0.0
    for n in range(0, 2 * pair, DH):
        wide = x_buf[:, n : n + DH].astype(f32)
        squares = squares + wide * wide
    column = jnp.sum(squares, axis=1, keepdims=True)
    column = jnp.broadcast_to(column, squares.shape)
    for i in range(len(seqs)):
        start = 2 * i * rows
        outs[3 * i + 1][...] = column[start : start + rows].T[:8]
        put_squares(outs[3 * i + 2], column[start + rows : start + 2 * rows].T[:8])
    for c in range(chunks):
        weight_copy(c).wait()
        total = jnp.dot(x_buf[...], w_buf[c], preferred_element_type=f32).astype(bf16)
        held = slice(c * chunk, (c + 1) * chunk)
        for i in range(len(seqs)):
            start = 2 * i * rows
            outs[3 * i][:, held] = total[start : start + rows]
            outs[3 * i + 2][:rows, held] = total[start + rows : start + 2 * rows]


def gate_products(seqs, where, blocks, weights):
    rows, pair = blocks[0].shape
    rows = rows // 2
    features, width = weights.shape
    n = len(seqs)
    chunks = 4
    return pl.pallas_call(
        functools.partial(gate_kernel, seqs),
        in_specs=[SCALARS] + [ANYWHERE] * (NZ + 1),
        out_specs=[WHOLE] * (3 * n),
        scratch_shapes=[
            pltpu.VMEM((chunks, features, width // chunks), bf16),
            pltpu.VMEM((2 * n * rows, 2 * pair), bf16),
            pltpu.SemaphoreType.DMA((chunks,)),
            pltpu.SemaphoreType.DMA((n, 2, 2)),
        ],
        out_shape=[
            jax.ShapeDtypeStruct((rows, width), bf16),
            jax.ShapeDtypeStruct((8, rows), f32),
            jax.ShapeDtypeStruct((rows + EXTRA, width), bf16),
        ]
        * n,
        compiler_params=pltpu.CompilerParams(vmem_limit_bytes=VMEM_BYTES),
        cost_estimate=SMALL_COST,
    )(where, *blocks, in_hbm(weights))


def far_kernel(own_ref, square_ref, other_ref, out_ref):
    rows = own_ref.shape[0]
    out_ref[:rows] = (own_ref[...].astype(f32) + other_ref[:rows].astype(f32)).astype(bf16)
    put_squares(out_ref, square_ref[...] + get_squares(other_ref, rows))


def near_kernel(where_ref, far_ref, *refs):
    rows = refs[0].shape[0]
    far = far_ref[:rows].astype(f32)
    far_square = get_squares(far_ref, rows)
    for i in range(2):
        own_ref, square_ref, other_ref = refs[3 * i : 3 * i + 3]
        out_ref = refs[6 + i]
        mine = where_ref[0] == i
        total = own_ref[...].astype(f32) + other_ref[:rows].astype(f32)
        out_ref[:rows] = (total + jnp.where(mine, far, 0.0)).astype(bf16)
        squares = square_ref[...] + get_squares(other_ref, rows)
        put_squares(out_ref, squares + jnp.where(mine, far_square, 0.0))


def last_kernel(own_ref, square_ref, other_ref, left_ref, right_ref, out_ref):
    rows, width = own_ref.shape
    units = width // 2
    squares = square_ref[...]
    total = own_ref[...].astype(f32)
    for ref in (other_ref, left_ref, right_ref):
        squares = squares + get_squares(ref, rows)
        total = total + ref[:rows].astype(f32)
    squares = jnp.broadcast_to(squares[:1], (DH, rows)).T[:, :1]
    total = total * lax.rsqrt(squares / D + eps_norm)
    gate, up = total[:, :units], total[:, units:]
    out_ref[0] = (gate / (1.0 + jnp.exp(-gate)) * up).astype(bf16)


def small_call(kernel, shapes, *operands):
    first = operands[0].dtype == jnp.int32
    return pl.pallas_call(
        kernel,
        in_specs=[SCALARS] * first + [WHOLE] * (len(operands) - first),
        out_specs=[WHOLE] * len(shapes),
        out_shape=[jax.ShapeDtypeStruct(shape, bf16) for shape in shapes],
        compiler_params=pltpu.CompilerParams(vmem_limit_bytes=VMEM_BYTES),
        cost_estimate=SMALL_COST,
    )(*operands)


def ring_kernel(offset, where_ref, parts_ref, right_ref, left_ref, *refs):
    z = where_ref[1]
    buf, sem = refs[-2:]
    if offset:
        sources = (parts_ref.at[(z + offset) % NZ], parts_ref.at[(z + NZ - offset) % NZ])
    else:
        sources = (parts_ref.at[z], refs[0])
    arrived = (right_ref, left_ref)
    starts = (0, buf.shape[1] - left_ref.shape[0])
    copies = []
    for i in range(2):
        copies.append(pltpu.make_async_copy(sources[i], buf.at[i], sem.at[i]))
        place = buf.at[2 + i, pl.ds(starts[i], arrived[i].shape[0])]
        copies.append(pltpu.make_async_copy(arrived[i], place, sem.at[2 + i]))
    for copy in copies:
        copy.start()
    for copy in copies:
        copy.wait()
    if not offset:
        refs[1][...] = (
            (buf[0].astype(f32) + buf[2].astype(f32) + buf[3].astype(f32)) + buf[1].astype(f32)
        ).astype(bf16)
        return
    for i in range(2):
        rows = arrived[i].shape[0]
        held = pl.ds(starts[i], rows)
        total = buf[i, held].astype(f32) + buf[2 + i, held].astype(f32)
        refs[i][held] = total.astype(bf16)
        if rows < buf.shape[1]:
            rest = pl.ds(rows - starts[i], rows)
            refs[i][rest] = buf[i, rest]


def ring_add(offset, where, parts, right, left, residual=None):
    _, rows, width = parts.shape
    extra = [] if residual is None else [residual]
    return pl.pallas_call(
        functools.partial(ring_kernel, offset),
        in_specs=[SCALARS] + [ANYWHERE] * (3 + len(extra)),
        out_specs=[WHOLE] * (2 - len(extra)),
        scratch_shapes=[pltpu.VMEM((4, rows, width), bf16), pltpu.SemaphoreType.DMA((4,))],
        out_shape=[jax.ShapeDtypeStruct((rows, width), bf16)] * (2 - len(extra)),
        compiler_params=pltpu.CompilerParams(vmem_limit_bytes=VMEM_BYTES),
        cost_estimate=SMALL_COST,
    )(where, parts, right, left, *extra)


def reduce_scatter_z(where, parts, far_a, far_b, residual):
    right = shift(far_a, "col", NZ, 1)
    left = shift(far_b, "col", NZ, -1)
    (right, left), residual = lax.optimization_barrier(((right, left), residual))
    for offset in (3, 2, 1):
        right, left = ring_add(offset, where, parts, right, left)
        right = shift(right, "col", NZ, 1)
        left = shift(left, "col", NZ, -1)
    return ring_add(0, where, parts, right, left, residual)[0]


def all_gather_z(block):
    cut = block.shape[0] // 2
    right, left = [block], [block]
    for _ in range(3):
        right.append(shift(right[-1], "col", NZ, 1))
        left.append(shift(left[-1], "col", NZ, -1))
    far_a = shift(right[3][:cut], "col", NZ, 1)
    far_b = shift(left[3][cut:], "col", NZ, -1)
    far = jnp.concatenate([far_a, far_b], axis=0)
    return [block, left[1], left[2], left[3], far, right[3], right[2], right[1]]


def work_to_natural(m, flip):
    pairs = []
    for depth in range(2):
        for y in range(NY):
            for z in range(NZ):
                there = 2 * (z % 2) + (m ^ (y % 2)), 2 * (z // 2) + y // 2
                pairs.append(
                    (
                        (depth * NY + y) * NZ + z,
                        ((depth ^ flip) * NY + there[0]) * NZ + there[1],
                    )
                )
    return pairs


def in_order(depth, same, other, axis):
    return jnp.where(
        depth == 0,
        jnp.concatenate([same, other], axis=axis),
        jnp.concatenate([other, same], axis=axis),
    )


def per_device(queries, key_states, value_states, residual, gain, w_out, w_gate, w_up):
    half = queries.shape[1]
    depth, x, y, z = (lax.axis_index(name) for name in ("depth", "x", "y", "col"))
    odd = (y % 2) == 1
    where = jnp.stack([depth, z, x, y]).astype(jnp.int32)
    block = w_out.shape[1]
    width = block // 2

    cut = w_out.shape[0] // 2
    wo_half = [
        lax.dynamic_slice(w_out, (i * cut, depth * width), (cut, width)) for i in range(2)
    ]
    wo_next = [shift(piece, "y", NY, -1) for piece in wo_half]
    wo_last = [shift(piece, "y", NY, 1) for piece in wo_half]
    wo_next, wo_last = lax.optimization_barrier((wo_next, wo_last))
    wo_far = [shift(wo_next[0], "y", NY, -1), shift(wo_last[1], "y", NY, 1)]

    kv = jnp.concatenate([key_states[0], value_states[0]], axis=1)
    kv = lax.all_gather(kv, "depth", axis=0)
    attended = attend(where, queries[0], kv)
    own = [
        attended,
        shift(attended, "x", NX, -1),
        shift(attended, "x", NX, 2),
        shift(attended, "x", NX, 1),
    ]
    other = [swap(value) for value in own]

    rows = w_gate.shape[0] // 2
    held = [
        lax.dynamic_slice_in_dim(value, depth * rows, rows, 0) for value in (w_gate, w_up, gain[:, None])
    ]
    w2_half = jnp.concatenate(
        [(weights.astype(f32) * held[2]).astype(bf16) for weights in held[:2]], axis=1
    )
    w2_half, _ = lax.optimization_barrier((w2_half, (other, wo_far)))
    w2 = lax.all_gather(w2_half, "y", axis=0, tiled=True)

    axes = ("depth", "y", "col")
    residual, _ = lax.optimization_barrier((residual, own))
    got = []
    for m in range(2):
        for flip in range(2):
            sent = jnp.where(odd, residual[1 - m], residual[m])
            sent = lax.dynamic_slice_in_dim(sent, (depth ^ flip) * width, width, 1)
            got.append(lax.ppermute(sent, axes, [(b, a) for a, b in work_to_natural(m, flip)]))
    same = jnp.concatenate([jnp.where(odd, got[2], got[0]), jnp.where(odd, got[0], got[2])], axis=1)
    flipped = jnp.concatenate([jnp.where(odd, got[3], got[1]), jnp.where(odd, got[1], got[3])], axis=1)
    res_work = in_order(depth, same, flipped, 0)

    pieces = [*wo_next, *wo_far, *wo_last]
    parts, far_a, far_b = out_project(where, own, other, w_out, pieces)
    stream = reduce_scatter_z(where, parts, far_a, far_b, res_work)
    blocks = all_gather_z(stream)

    far, far_square, sent = gate_products((2,), where, blocks, w2)
    payload = (half + EXTRA, w2.shape[1])
    (far,) = small_call(far_kernel, [payload], far, far_square, swap(sent))
    after_far, far = lax.optimization_barrier((where, far))
    pairs = []
    for i in range(NX):
        pairs.append((i, (i + 1) % NX))
    for i in range(NX):
        pairs.append((NX + i, NX + (i - 1) % NX))
    far = lax.ppermute(far, ("depth", "x"), pairs)
    right, right_square, right_sent, left, left_square, left_sent = gate_products(
        (1, 3), after_far, blocks, w2
    )
    near_right, near_left = small_call(
        near_kernel,
        [payload] * 2,
        where,
        far,
        right,
        right_square,
        swap(right_sent),
        left,
        left_square,
        swap(left_sent),
    )
    from_left = shift(near_right, "x", NX, 1)
    from_right = shift(near_left, "x", NX, -1)

    mine, mine_square, mine_sent = gate_products((0,), where, blocks, w2)
    stream_late, _ = lax.optimization_barrier((stream, mine))
    back = []
    for m in range(2):
        for flip in range(2):
            first, second = stream_late[:, :width], stream_late[:, width:]
            sent = jnp.where(odd, second, first) if m == 0 else jnp.where(odd, first, second)
            sent = lax.dynamic_slice_in_dim(sent, (depth ^ flip) * half, half, 0)
            back.append(lax.ppermute(sent, axes, work_to_natural(m, flip)))
    pair = [in_order(depth, back[2 * m], back[2 * m + 1], 1) for m in range(2)]
    stream_out = jnp.stack(
        [jnp.where(odd, pair[1], pair[0]), jnp.where(odd, pair[0], pair[1])]
    )
    (hidden,) = small_call(
        last_kernel,
        [(1, half, w2.shape[1] // 2)],
        mine,
        mine_square,
        swap(mine_sent),
        from_left,
        from_right,
    )
    return (hidden, stream_out)


def solution(mesh):
    fine = Mesh(mesh.devices.reshape(2, NX, NY, NZ), ("depth", "x", "y", "col"))
    row = ("x", "y")
    return jax.shard_map(
        per_device,
        mesh=fine,
        in_specs=(
            P(row, "depth", "col"),
            P(row, "depth", "col"),
            P(row, "depth", "col"),
            P("col", "depth", row),
            P(row),
            P("col", row),
            P(row, "col"),
            P(row, "col"),
        ),
        out_specs=(P(row, "depth", "col"), P("col", "depth", row)),
        check_vma=False,
    )
```

```python
import functools
import jax
import jax.numpy as jnp
from jax import lax
from jax.experimental import pallas as pl
from jax.experimental.pallas import tpu as pltpu
from jax.sharding import Mesh, PartitionSpec as P

D = 8192
DH = 128
GROUP = 8
NX = 4
NY = 4
NZ = 8
EXTRA = 16

eps_norm = 1e-05
masked_score = -1e30
bf16 = jnp.bfloat16
f32 = jnp.float32
VMEM_BYTES = 24 * 1024 * 1024
SMALL_COST = pl.CostEstimate(flops=1024, bytes_accessed=1024, transcendentals=0)


def shift(value, axis, size, by):
    return lax.ppermute(value, axis, [(i, (i + by) % size) for i in range(size)])


def in_hbm(value):
    return pltpu.with_memory_space_constraint(value, pltpu.HBM)


def swap(value):
    return shift(value, "depth", 2, 1)


def attend_kernel(where_ref, q_ref, kv_ref, out_ref):
    depth = where_ref[0]
    half = q_ref.shape[0]
    keys = jnp.concatenate([kv_ref[0, :, :DH], kv_ref[1, :, :DH]], axis=0)
    values = jnp.concatenate([kv_ref[0, :, DH:], kv_ref[1, :, DH:]], axis=0)
    rows = jnp.concatenate([q_ref[:, h * DH : (h + 1) * DH] for h in range(GROUP)], axis=0)
    scores = lax.dot_general(
        rows, keys, (((1,), (1,)), ((), ())), preferred_element_type=f32
    ) * DH ** (-0.5)
    shape = scores.shape
    position = lax.broadcasted_iota(jnp.int32, shape, 0) % half + depth * half
    allowed = lax.broadcasted_iota(jnp.int32, shape, 1) <= position
    scores = jnp.where(allowed, scores, masked_score)
    top = jnp.max(scores, axis=-1, keepdims=True)
    expo = jnp.exp(scores - top)
    totals = jnp.sum(expo, axis=-1, keepdims=True)
    mixed = jnp.dot(expo.astype(bf16), values, preferred_element_type=f32) / totals
    mixed = mixed.astype(bf16)
    for h in range(GROUP):
        out_ref[:, h * DH : (h + 1) * DH] = mixed[h * half : (h + 1) * half]


def attend(where, queries, kv):
    half, features = queries.shape
    length = 2 * half
    return pl.pallas_call(
        attend_kernel,
        in_specs=[pl.BlockSpec(memory_space=pltpu.SMEM)]
        + [pl.BlockSpec(memory_space=pltpu.VMEM)] * 2,
        out_specs=pl.BlockSpec(memory_space=pltpu.VMEM),
        out_shape=jax.ShapeDtypeStruct((half, features), bf16),
        compiler_params=pltpu.CompilerParams(vmem_limit_bytes=VMEM_BYTES),
        cost_estimate=SMALL_COST,
    )(where, queries, kv)


ANYWHERE = pl.BlockSpec(memory_space=pl.ANY)
SCALARS = pl.BlockSpec(memory_space=pltpu.SMEM)
WHOLE = pl.BlockSpec(memory_space=pltpu.VMEM)


def out_kernel(where_ref, *refs):
    own, other, w_ref, pieces = refs[:4], refs[4:8], refs[8], refs[9:12]
    out_ref, far_a_ref, far_b_ref, att_buf, w_buf, att_sem, w_sem = refs[12:]
    depth, z, x, y = (where_ref[i] for i in range(4))
    rows = own[0].shape[0]
    width = w_buf.shape[2]
    first = []
    for k in range(NX):
        for i, (side, ref) in enumerate(((depth, own[k]), (1 - depth, other[k]))):
            place = pl.ds(pl.multiple_of((2 * k + side) * rows, rows), rows)
            first.append(pltpu.make_async_copy(ref, att_buf.at[place], att_sem.at[k, i]))
    columns = pl.ds(pl.multiple_of(depth * width, width), width)
    copies = [pltpu.make_async_copy(w_ref.at[:, columns], w_buf.at[0], w_sem.at[0])]
    for j in range(1, NY):
        copies.append(pltpu.make_async_copy(pieces[j - 1], w_buf.at[j], w_sem.at[j]))
    for copy in first:
        copy.start()
    for copy in copies:
        copy.start()
    for copy in first:
        copy.wait()
    for j in range(NY):
        copies[j].wait()
        total = jnp.dot(att_buf[...], w_buf[j], preferred_element_type=f32).astype(bf16)
        block = (y + j) % NY
        held = pl.ds(pl.multiple_of((block % 2) * width, width), width)
        for k in range(NX):
            place = 2 * ((x + k) % NX) + block // 2
            out_ref[place, :, held] = total[2 * k * rows : 2 * (k + 1) * rows]
    far = (z + NZ // 2) % NZ
    far_a_ref[...] = out_ref[far, :rows]
    far_b_ref[...] = out_ref[far, rows:]


def out_project(where, own, other, w_out, pieces):
    rows, features = own[0].shape
    width = w_out.shape[1] // 2
    return pl.pallas_call(
        out_kernel,
        in_specs=[SCALARS] + [ANYWHERE] * 12,
        out_specs=[WHOLE] * 3,
        out_shape=[jax.ShapeDtypeStruct((NZ, 2 * rows, 2 * width), bf16)]
        + [jax.ShapeDtypeStruct((rows, 2 * width), bf16)] * 2,
        scratch_shapes=[
            pltpu.VMEM((2 * NX * rows, features), bf16),
            pltpu.VMEM((NY, features, width), bf16),
            pltpu.SemaphoreType.DMA((NX, 2)),
            pltpu.SemaphoreType.DMA((NY,)),
        ],
        compiler_params=pltpu.CompilerParams(vmem_limit_bytes=VMEM_BYTES),
        cost_estimate=SMALL_COST,
    )(where, *own, *other, in_hbm(w_out), *pieces)


def put_squares(ref, row):
    rows = ref.shape[0] - EXTRA
    high = row.astype(bf16)
    rest = row - high.astype(f32)
    middle = rest.astype(bf16)
    low = (rest - middle.astype(f32)).astype(bf16)
    index = lax.broadcasted_iota(jnp.int32, row.shape, 0)
    first = jnp.where(index == 0, high.astype(f32), jnp.where(index == 1, middle.astype(f32), 0.0))
    first = jnp.where(index == 2, low.astype(f32), first)
    both = jnp.concatenate([first, jnp.zeros_like(first)], axis=0).astype(bf16)
    ref[rows:] = jnp.zeros((EXTRA, ref.shape[1]), bf16)
    ref[rows:, : row.shape[1]] = both


def get_squares(ref, count):
    held = ref[ref.shape[0] - EXTRA :, :count].astype(f32)
    return jnp.broadcast_to(jnp.sum(held, axis=0, keepdims=True), (8, count))


def gate_kernel(seqs, where_ref, *refs):
    blocks, weight_ref = refs[:NZ], refs[NZ]
    outs = refs[NZ + 1 : -4]
    w_buf, x_buf, w_sem, x_sem = refs[-4:]
    depth, z, x = (where_ref[i] for i in range(3))
    rows, pair = blocks[0].shape[0] // 2, blocks[0].shape[1]
    chunks, _, chunk = w_buf.shape

    def rows_copy(ref, i, h, side):
        place = depth if side == 0 else 1 - depth
        return pltpu.make_async_copy(
            ref.at[pl.ds(pl.multiple_of(place * rows, rows), rows)],
            x_buf.at[pl.ds((2 * i + side) * rows, rows), pl.ds(h * pair, pair)],
            x_sem.at[i, h, side],
        )

    def weight_copy(c):
        return pltpu.make_async_copy(
            weight_ref.at[:, pl.ds(c * chunk, chunk)], w_buf.at[c], w_sem.at[c]
        )

    for c in range(chunks):
        weight_copy(c).start()
    for h in range(2):
        for i, k in enumerate(seqs):
            ring = (2 * ((x + k) % NX) + h - z + NZ) % NZ
            for j in range(NZ):

                @pl.when(ring == j)
                def _():
                    rows_copy(blocks[j], i, h, 0).start()
                    rows_copy(blocks[j], i, h, 1).start()

    for h in range(2):
        for i in range(len(seqs)):
            for side in range(2):
                rows_copy(blocks[0], i, h, side).wait()
    squares = 0.0
    for n in range(0, 2 * pair, DH):
        wide = x_buf[:, n : n + DH].astype(f32)
        squares = squares + wide * wide
    column = jnp.sum(squares, axis=1, keepdims=True)
    column = jnp.broadcast_to(column, squares.shape)
    for i in range(len(seqs)):
        start = 2 * i * rows
        outs[3 * i + 1][...] = column[start : start + rows].T[:8]
        put_squares(outs[3 * i + 2], column[start + rows : start + 2 * rows].T[:8])
    for c in range(chunks):
        weight_copy(c).wait()
        total = jnp.dot(x_buf[...], w_buf[c], preferred_element_type=f32).astype(bf16)
        held = slice(c * chunk, (c + 1) * chunk)
        for i in range(len(seqs)):
            start = 2 * i * rows
            outs[3 * i][:, held] = total[start : start + rows]
            outs[3 * i + 2][:rows, held] = total[start + rows : start + 2 * rows]


def gate_products(seqs, where, blocks, weights):
    rows, pair = blocks[0].shape
    rows = rows // 2
    features, width = weights.shape
    n = len(seqs)
    chunks = 4
    results = pl.pallas_call(
        functools.partial(gate_kernel, seqs),
        in_specs=[SCALARS] + [ANYWHERE] * (NZ + 1),
        out_specs=[WHOLE] * (3 * n),
        scratch_shapes=[
            pltpu.VMEM((chunks, features, width // chunks), bf16),
            pltpu.VMEM((2 * n * rows, 2 * pair), bf16),
            pltpu.SemaphoreType.DMA((chunks,)),
            pltpu.SemaphoreType.DMA((n, 2, 2)),
        ],
        out_shape=[
            jax.ShapeDtypeStruct((rows, width), bf16),
            jax.ShapeDtypeStruct((8, rows), f32),
            jax.ShapeDtypeStruct((rows + EXTRA, width), bf16),
        ]
        * n,
        compiler_params=pltpu.CompilerParams(vmem_limit_bytes=VMEM_BYTES),
        cost_estimate=SMALL_COST,
    )(where, *blocks, in_hbm(weights))
    return [results[3 * i : 3 * i + 3] for i in range(n)]


def far_kernel(own_ref, square_ref, other_ref, out_ref):
    rows = own_ref.shape[0]
    out_ref[:rows] = (own_ref[...].astype(f32) + other_ref[:rows].astype(f32)).astype(bf16)
    put_squares(out_ref, square_ref[...] + get_squares(other_ref, rows))


def near_kernel(where_ref, far_ref, *refs):
    rows = refs[0].shape[0]
    far = far_ref[:rows].astype(f32)
    far_square = get_squares(far_ref, rows)
    for i in range(2):
        own_ref, square_ref, other_ref = refs[3 * i : 3 * i + 3]
        out_ref = refs[6 + i]
        mine = where_ref[0] == i
        total = own_ref[...].astype(f32) + other_ref[:rows].astype(f32)
        out_ref[:rows] = (total + jnp.where(mine, far, 0.0)).astype(bf16)
        squares = square_ref[...] + get_squares(other_ref, rows)
        put_squares(out_ref, squares + jnp.where(mine, far_square, 0.0))


def last_kernel(own_ref, square_ref, other_ref, left_ref, right_ref, out_ref):
    rows, width = own_ref.shape
    units = width // 2
    squares = square_ref[...]
    total = own_ref[...].astype(f32)
    for ref in (other_ref, left_ref, right_ref):
        squares = squares + get_squares(ref, rows)
        total = total + ref[:rows].astype(f32)
    squares = jnp.broadcast_to(squares[:1], (DH, rows)).T[:, :1]
    total = total * lax.rsqrt(squares / D + eps_norm)
    gate, up = total[:, :units], total[:, units:]
    out_ref[0] = (gate / (1.0 + jnp.exp(-gate)) * up).astype(bf16)


def small_call(kernel, shapes, *operands):
    first = operands[0].dtype == jnp.int32
    return pl.pallas_call(
        kernel,
        in_specs=[SCALARS] * first + [WHOLE] * (len(operands) - first),
        out_specs=[WHOLE] * len(shapes),
        out_shape=[jax.ShapeDtypeStruct(shape, bf16) for shape in shapes],
        compiler_params=pltpu.CompilerParams(vmem_limit_bytes=VMEM_BYTES),
        cost_estimate=SMALL_COST,
    )(*operands)


def ring_kernel(offset, where_ref, parts_ref, right_ref, left_ref, *refs):
    z = where_ref[1]
    buf, sem = refs[-2:]
    if offset:
        sources = (parts_ref.at[(z + offset) % NZ], parts_ref.at[(z + NZ - offset) % NZ])
    else:
        sources = (parts_ref.at[z], refs[0])
    arrived = (right_ref, left_ref)
    starts = (0, buf.shape[1] - left_ref.shape[0])
    copies = []
    for i in range(2):
        copies.append(pltpu.make_async_copy(sources[i], buf.at[i], sem.at[i]))
        place = buf.at[2 + i, pl.ds(starts[i], arrived[i].shape[0])]
        copies.append(pltpu.make_async_copy(arrived[i], place, sem.at[2 + i]))
    for copy in copies:
        copy.start()
    for copy in copies:
        copy.wait()
    if not offset:
        refs[1][...] = (
            (buf[0].astype(f32) + buf[2].astype(f32) + buf[3].astype(f32)) + buf[1].astype(f32)
        ).astype(bf16)
        return
    for i in range(2):
        rows = arrived[i].shape[0]
        held = pl.ds(starts[i], rows)
        total = buf[i, held].astype(f32) + buf[2 + i, held].astype(f32)
        refs[i][held] = total.astype(bf16)
        if rows < buf.shape[1]:
            rest = pl.ds(rows - starts[i], rows)
            refs[i][rest] = buf[i, rest]


def ring_add(offset, where, parts, right, left, residual=None):
    _, rows, width = parts.shape
    extra = [] if residual is None else [residual]
    return pl.pallas_call(
        functools.partial(ring_kernel, offset),
        in_specs=[SCALARS] + [ANYWHERE] * (3 + len(extra)),
        out_specs=[WHOLE] * (2 - len(extra)),
        scratch_shapes=[pltpu.VMEM((4, rows, width), bf16), pltpu.SemaphoreType.DMA((4,))],
        out_shape=[jax.ShapeDtypeStruct((rows, width), bf16)] * (2 - len(extra)),
        compiler_params=pltpu.CompilerParams(vmem_limit_bytes=VMEM_BYTES),
        cost_estimate=SMALL_COST,
    )(where, parts, right, left, *extra)


def reduce_scatter_z(where, parts, far_a, far_b, residual):
    right = shift(far_a, "col", NZ, 1)
    left = shift(far_b, "col", NZ, -1)
    (right, left), residual = lax.optimization_barrier(((right, left), residual))
    for offset in (3, 2, 1):
        right, left = ring_add(offset, where, parts, right, left)
        right = shift(right, "col", NZ, 1)
        left = shift(left, "col", NZ, -1)
    return ring_add(0, where, parts, right, left, residual)[0]


def all_gather_z(block):
    cut = block.shape[0] // 2
    right, left = [block], [block]
    for _ in range(3):
        got = (shift(right[-1], "col", NZ, 1), shift(left[-1], "col", NZ, -1))
        got = lax.optimization_barrier(got)
        right.append(got[0])
        left.append(got[1])
    far_a = shift(right[3][:cut], "col", NZ, 1)
    far_b = shift(left[3][cut:], "col", NZ, -1)
    far = jnp.concatenate([far_a, far_b], axis=0)
    return [block, left[1], left[2], left[3], far, right[3], right[2], right[1]]


def work_to_natural(m, flip):
    pairs = []
    for depth in range(2):
        for y in range(NY):
            for z in range(NZ):
                there = 2 * (z % 2) + (m ^ (y % 2)), 2 * (z // 2) + y // 2
                pairs.append(
                    (
                        (depth * NY + y) * NZ + z,
                        ((depth ^ flip) * NY + there[0]) * NZ + there[1],
                    )
                )
    return pairs


def in_order(depth, same, other, axis):
    return jnp.where(
        depth == 0,
        jnp.concatenate([same, other], axis=axis),
        jnp.concatenate([other, same], axis=axis),
    )


def per_device(queries, key_states, value_states, residual, gain, w_out, w_gate, w_up):
    half = queries.shape[1]
    depth, x, y, z = (lax.axis_index(name) for name in ("depth", "x", "y", "col"))
    odd = (y % 2) == 1
    where = jnp.stack([depth, z, x, y]).astype(jnp.int32)
    block = w_out.shape[1]
    width = block // 2

    wo_half = lax.dynamic_slice_in_dim(w_out, depth * width, width, 1)
    pieces = [shift(wo_half, "y", NY, -1), shift(wo_half, "y", NY, 2), shift(wo_half, "y", NY, 1)]

    kv = jnp.concatenate([key_states[0], value_states[0]], axis=1)
    kv = lax.all_gather(kv, "depth", axis=0)
    attended = attend(where, queries[0], kv)
    own = [
        attended,
        shift(attended, "x", NX, -1),
        shift(attended, "x", NX, 2),
        shift(attended, "x", NX, 1),
    ]
    other = [swap(value) for value in own]

    axes = ("depth", "y", "col")
    sent = []
    for m in range(2):
        chosen = jnp.where(odd, residual[1 - m], residual[m])
        for flip in range(2):
            sent.append(lax.dynamic_slice_in_dim(chosen, (depth ^ flip) * width, width, 1))
    sent, _ = lax.optimization_barrier((sent, own[1]))
    got = [
        lax.ppermute(sent[2 * m + flip], axes, [(b, a) for a, b in work_to_natural(m, flip)])
        for m in range(2)
        for flip in range(2)
    ]
    same = jnp.concatenate([jnp.where(odd, got[2], got[0]), jnp.where(odd, got[0], got[2])], axis=1)
    flipped = jnp.concatenate([jnp.where(odd, got[3], got[1]), jnp.where(odd, got[1], got[3])], axis=1)
    res_work = in_order(depth, same, flipped, 0)

    rows = w_gate.shape[0] // 2
    held = [
        lax.dynamic_slice_in_dim(value, depth * rows, rows, 0) for value in (w_gate, w_up, gain[:, None])
    ]
    w2_half = jnp.concatenate(
        [(weights.astype(f32) * held[2]).astype(bf16) for weights in held[:2]], axis=1
    )
    w2_half, _ = lax.optimization_barrier((w2_half, (other, pieces, got)))
    w2 = lax.all_gather(w2_half, "y", axis=0, tiled=True)

    parts, far_a, far_b = out_project(where, own, other, w_out, pieces)
    stream = reduce_scatter_z(where, parts, far_a, far_b, res_work)
    blocks = all_gather_z(stream)

    ((far, far_square, sent),) = gate_products((2,), where, blocks, w2)
    payload = (half + EXTRA, w2.shape[1])
    (far,) = small_call(far_kernel, [payload], far, far_square, swap(sent))
    after_far, far = lax.optimization_barrier((where, far))
    pairs = []
    for i in range(NX):
        pairs.append((i, (i + 1) % NX))
    for i in range(NX):
        pairs.append((NX + i, NX + (i - 1) % NX))
    far = lax.ppermute(far, ("depth", "x"), pairs)
    (right, right_square, right_sent), (left, left_square, left_sent) = gate_products(
        (1, 3), after_far, blocks, w2
    )
    ((mine, mine_square, mine_sent),) = gate_products((0,), where, blocks, w2)
    near_right, near_left = small_call(
        near_kernel,
        [payload] * 2,
        where,
        far,
        right,
        right_square,
        swap(right_sent),
        left,
        left_square,
        swap(left_sent),
    )
    from_left = shift(near_right, "x", NX, 1)
    from_right = shift(near_left, "x", NX, -1)
    stream_late, _ = lax.optimization_barrier((stream, near_right))
    back = []
    for m in range(2):
        for flip in range(2):
            first, second = stream_late[:, :width], stream_late[:, width:]
            sent = jnp.where(odd, second, first) if m == 0 else jnp.where(odd, first, second)
            sent = lax.dynamic_slice_in_dim(sent, (depth ^ flip) * half, half, 0)
            back.append(lax.ppermute(sent, axes, work_to_natural(m, flip)))
    pair = [in_order(depth, back[2 * m], back[2 * m + 1], 1) for m in range(2)]
    stream_out = jnp.stack(
        [jnp.where(odd, pair[1], pair[0]), jnp.where(odd, pair[0], pair[1])]
    )
    (hidden,) = small_call(
        last_kernel,
        [(1, half, w2.shape[1] // 2)],
        mine,
        mine_square,
        swap(mine_sent),
        from_left,
        from_right,
    )
    return (hidden, stream_out)


def solution(mesh):
    fine = Mesh(mesh.devices.reshape(2, NX, NY, NZ), ("depth", "x", "y", "col"))
    row = ("x", "y")
    return jax.shard_map(
        per_device,
        mesh=fine,
        in_specs=(
            P(row, "depth", "col"),
            P(row, "depth", "col"),
            P(row, "depth", "col"),
            P("col", "depth", row),
            P(row),
            P("col", row),
            P(row, "col"),
            P(row, "col"),
        ),
        out_specs=(P(row, "depth", "col"), P("col", "depth", row)),
        check_vma=False,
    )
```

```python
import functools
import jax
import jax.numpy as jnp
from jax import lax
from jax.experimental import pallas as pl
from jax.experimental.pallas import tpu as pltpu
from jax.sharding import Mesh, PartitionSpec as P

D = 8192
DH = 128
GROUP = 8
NX = 4
NY = 4
NZ = 8
EXTRA = 16

eps_norm = 1e-05
masked_score = -1e30
bf16 = jnp.bfloat16
f32 = jnp.float32
VMEM_BYTES = 24 * 1024 * 1024
SMALL_COST = pl.CostEstimate(flops=1024, bytes_accessed=1024, transcendentals=0)


def shift(value, axis, size, by):
    return lax.ppermute(value, axis, [(i, (i + by) % size) for i in range(size)])


def in_hbm(value):
    return pltpu.with_memory_space_constraint(value, pltpu.HBM)


def swap(value):
    return shift(value, "depth", 2, 1)


def attend_kernel(where_ref, q_ref, kv_ref, out_ref):
    depth = where_ref[0]
    half = q_ref.shape[0]
    keys = jnp.concatenate([kv_ref[0, :, :DH], kv_ref[1, :, :DH]], axis=0)
    values = jnp.concatenate([kv_ref[0, :, DH:], kv_ref[1, :, DH:]], axis=0)
    rows = jnp.concatenate([q_ref[:, h * DH : (h + 1) * DH] for h in range(GROUP)], axis=0)
    scores = lax.dot_general(
        rows, keys, (((1,), (1,)), ((), ())), preferred_element_type=f32
    ) * DH ** (-0.5)
    shape = scores.shape
    position = lax.broadcasted_iota(jnp.int32, shape, 0) % half + depth * half
    allowed = lax.broadcasted_iota(jnp.int32, shape, 1) <= position
    scores = jnp.where(allowed, scores, masked_score)
    top = jnp.max(scores, axis=-1, keepdims=True)
    expo = jnp.exp(scores - top)
    totals = jnp.sum(expo, axis=-1, keepdims=True)
    mixed = jnp.dot(expo.astype(bf16), values, preferred_element_type=f32) / totals
    mixed = mixed.astype(bf16)
    for h in range(GROUP):
        out_ref[:, h * DH : (h + 1) * DH] = mixed[h * half : (h + 1) * half]


def attend(where, queries, kv):
    half, features = queries.shape
    length = 2 * half
    return pl.pallas_call(
        attend_kernel,
        in_specs=[pl.BlockSpec(memory_space=pltpu.SMEM)]
        + [pl.BlockSpec(memory_space=pltpu.VMEM)] * 2,
        out_specs=pl.BlockSpec(memory_space=pltpu.VMEM),
        out_shape=jax.ShapeDtypeStruct((half, features), bf16),
        compiler_params=pltpu.CompilerParams(vmem_limit_bytes=VMEM_BYTES),
        cost_estimate=SMALL_COST,
    )(where, queries, kv)


ANYWHERE = pl.BlockSpec(memory_space=pl.ANY)
SCALARS = pl.BlockSpec(memory_space=pltpu.SMEM)
WHOLE = pl.BlockSpec(memory_space=pltpu.VMEM)


def out_kernel(where_ref, *refs):
    own, other, w_ref, pieces = refs[:4], refs[4:8], refs[8], refs[9:12]
    out_ref, far_a_ref, far_b_ref, att_buf, w_buf, att_sem, w_sem = refs[12:]
    depth, z, x, y = (where_ref[i] for i in range(4))
    rows = own[0].shape[0]
    width = w_buf.shape[2]
    first = []
    for k in range(NX):
        for i, (side, ref) in enumerate(((depth, own[k]), (1 - depth, other[k]))):
            place = pl.ds(pl.multiple_of((2 * k + side) * rows, rows), rows)
            first.append(pltpu.make_async_copy(ref, att_buf.at[place], att_sem.at[k, i]))
    columns = pl.ds(pl.multiple_of(depth * width, width), width)
    copies = [pltpu.make_async_copy(w_ref.at[:, columns], w_buf.at[0], w_sem.at[0])]
    for j in range(1, NY):
        copies.append(pltpu.make_async_copy(pieces[j - 1], w_buf.at[j], w_sem.at[j]))
    for copy in first:
        copy.start()
    for copy in copies:
        copy.start()
    for copy in first:
        copy.wait()
    for j in range(NY):
        copies[j].wait()
        total = jnp.dot(att_buf[...], w_buf[j], preferred_element_type=f32).astype(bf16)
        block = (y + j) % NY
        held = pl.ds(pl.multiple_of((block % 2) * width, width), width)
        for k in range(NX):
            place = 2 * ((x + k) % NX) + block // 2
            out_ref[place, :, held] = total[2 * k * rows : 2 * (k + 1) * rows]
    far = (z + NZ // 2) % NZ
    far_a_ref[...] = out_ref[far, :rows]
    far_b_ref[...] = out_ref[far, rows:]


def out_project(where, own, other, w_out, pieces):
    rows, features = own[0].shape
    width = w_out.shape[1] // 2
    return pl.pallas_call(
        out_kernel,
        in_specs=[SCALARS] + [ANYWHERE] * 12,
        out_specs=[WHOLE] * 3,
        out_shape=[jax.ShapeDtypeStruct((NZ, 2 * rows, 2 * width), bf16)]
        + [jax.ShapeDtypeStruct((rows, 2 * width), bf16)] * 2,
        scratch_shapes=[
            pltpu.VMEM((2 * NX * rows, features), bf16),
            pltpu.VMEM((NY, features, width), bf16),
            pltpu.SemaphoreType.DMA((NX, 2)),
            pltpu.SemaphoreType.DMA((NY,)),
        ],
        compiler_params=pltpu.CompilerParams(vmem_limit_bytes=VMEM_BYTES),
        cost_estimate=SMALL_COST,
    )(where, *own, *other, in_hbm(w_out), *pieces)


def put_squares(ref, row):
    rows = ref.shape[0] - EXTRA
    high = row.astype(bf16)
    rest = row - high.astype(f32)
    middle = rest.astype(bf16)
    low = (rest - middle.astype(f32)).astype(bf16)
    index = lax.broadcasted_iota(jnp.int32, row.shape, 0)
    first = jnp.where(index == 0, high.astype(f32), jnp.where(index == 1, middle.astype(f32), 0.0))
    first = jnp.where(index == 2, low.astype(f32), first)
    both = jnp.concatenate([first, jnp.zeros_like(first)], axis=0).astype(bf16)
    ref[rows:] = jnp.zeros((EXTRA, ref.shape[1]), bf16)
    ref[rows:, : row.shape[1]] = both


def get_squares(ref, count):
    held = ref[ref.shape[0] - EXTRA :, :count].astype(f32)
    return jnp.broadcast_to(jnp.sum(held, axis=0, keepdims=True), (8, count))


def gate_kernel(seqs, where_ref, *refs):
    blocks, weight_ref = refs[:NZ], refs[NZ]
    outs = refs[NZ + 1 : -4]
    w_buf, x_buf, w_sem, x_sem = refs[-4:]
    depth, z, x = (where_ref[i] for i in range(3))
    rows, pair = blocks[0].shape[0] // 2, blocks[0].shape[1]
    chunks, _, chunk = w_buf.shape

    def rows_copy(ref, i, h, side):
        place = depth if side == 0 else 1 - depth
        return pltpu.make_async_copy(
            ref.at[pl.ds(pl.multiple_of(place * rows, rows), rows)],
            x_buf.at[pl.ds((2 * i + side) * rows, rows), pl.ds(h * pair, pair)],
            x_sem.at[i, h, side],
        )

    def weight_copy(c):
        return pltpu.make_async_copy(
            weight_ref.at[:, pl.ds(c * chunk, chunk)], w_buf.at[c], w_sem.at[c]
        )

    for c in range(chunks):
        weight_copy(c).start()
    for h in range(2):
        for i, k in enumerate(seqs):
            ring = (2 * ((x + k) % NX) + h - z + NZ) % NZ
            for j in range(NZ):

                @pl.when(ring == j)
                def _():
                    rows_copy(blocks[j], i, h, 0).start()
                    rows_copy(blocks[j], i, h, 1).start()

    for h in range(2):
        for i in range(len(seqs)):
            for side in range(2):
                rows_copy(blocks[0], i, h, side).wait()
    squares = 0.0
    for n in range(0, 2 * pair, DH):
        wide = x_buf[:, n : n + DH].astype(f32)
        squares = squares + wide * wide
    column = jnp.sum(squares, axis=1, keepdims=True)
    column = jnp.broadcast_to(column, squares.shape)
    for i in range(len(seqs)):
        start = 2 * i * rows
        outs[3 * i + 1][...] = column[start : start + rows].T[:8]
        put_squares(outs[3 * i + 2], column[start + rows : start + 2 * rows].T[:8])
    for c in range(chunks):
        weight_copy(c).wait()
        total = jnp.dot(x_buf[...], w_buf[c], preferred_element_type=f32).astype(bf16)
        held = slice(c * chunk, (c + 1) * chunk)
        for i in range(len(seqs)):
            start = 2 * i * rows
            outs[3 * i][:, held] = total[start : start + rows]
            outs[3 * i + 2][:rows, held] = total[start + rows : start + 2 * rows]


def gate_products(seqs, where, blocks, weights):
    rows, pair = blocks[0].shape
    rows = rows // 2
    features, width = weights.shape
    n = len(seqs)
    chunks = 4
    results = pl.pallas_call(
        functools.partial(gate_kernel, seqs),
        in_specs=[SCALARS] + [ANYWHERE] * (NZ + 1),
        out_specs=[WHOLE] * (3 * n),
        scratch_shapes=[
            pltpu.VMEM((chunks, features, width // chunks), bf16),
            pltpu.VMEM((2 * n * rows, 2 * pair), bf16),
            pltpu.SemaphoreType.DMA((chunks,)),
            pltpu.SemaphoreType.DMA((n, 2, 2)),
        ],
        out_shape=[
            jax.ShapeDtypeStruct((rows, width), bf16),
            jax.ShapeDtypeStruct((8, rows), f32),
            jax.ShapeDtypeStruct((rows + EXTRA, width), bf16),
        ]
        * n,
        compiler_params=pltpu.CompilerParams(vmem_limit_bytes=VMEM_BYTES),
        cost_estimate=SMALL_COST,
    )(where, *blocks, in_hbm(weights))
    return [results[3 * i : 3 * i + 3] for i in range(n)]


def far_kernel(own_ref, square_ref, other_ref, out_ref):
    rows = own_ref.shape[0]
    out_ref[:rows] = (own_ref[...].astype(f32) + other_ref[:rows].astype(f32)).astype(bf16)
    put_squares(out_ref, square_ref[...] + get_squares(other_ref, rows))


def near_kernel(where_ref, far_ref, *refs):
    rows = refs[0].shape[0]
    far = far_ref[:rows].astype(f32)
    far_square = get_squares(far_ref, rows)
    for i in range(2):
        own_ref, square_ref, other_ref = refs[3 * i : 3 * i + 3]
        out_ref = refs[6 + i]
        mine = where_ref[0] == i
        total = own_ref[...].astype(f32) + other_ref[:rows].astype(f32)
        out_ref[:rows] = (total + jnp.where(mine, far, 0.0)).astype(bf16)
        squares = square_ref[...] + get_squares(other_ref, rows)
        put_squares(out_ref, squares + jnp.where(mine, far_square, 0.0))


def last_kernel(own_ref, square_ref, other_ref, left_ref, right_ref, out_ref):
    rows, width = own_ref.shape
    units = width // 2
    squares = square_ref[...]
    total = own_ref[...].astype(f32)
    for ref in (other_ref, left_ref, right_ref):
        squares = squares + get_squares(ref, rows)
        total = total + ref[:rows].astype(f32)
    squares = jnp.broadcast_to(squares[:1], (DH, rows)).T[:, :1]
    total = total * lax.rsqrt(squares / D + eps_norm)
    gate, up = total[:, :units], total[:, units:]
    out_ref[0] = (gate / (1.0 + jnp.exp(-gate)) * up).astype(bf16)


def small_call(kernel, shapes, *operands):
    first = operands[0].dtype == jnp.int32
    return pl.pallas_call(
        kernel,
        in_specs=[SCALARS] * first + [WHOLE] * (len(operands) - first),
        out_specs=[WHOLE] * len(shapes),
        out_shape=[jax.ShapeDtypeStruct(shape, bf16) for shape in shapes],
        compiler_params=pltpu.CompilerParams(vmem_limit_bytes=VMEM_BYTES),
        cost_estimate=SMALL_COST,
    )(*operands)


def ring_kernel(offset, where_ref, parts_ref, right_ref, left_ref, *refs):
    z = where_ref[1]
    buf, sem = refs[-2:]
    if offset:
        sources = (parts_ref.at[(z + offset) % NZ], parts_ref.at[(z + NZ - offset) % NZ])
    else:
        sources = (parts_ref.at[z], refs[0])
    arrived = (right_ref, left_ref)
    starts = (0, buf.shape[1] - left_ref.shape[0])
    copies = []
    for i in range(2):
        copies.append(pltpu.make_async_copy(sources[i], buf.at[i], sem.at[i]))
        place = buf.at[2 + i, pl.ds(starts[i], arrived[i].shape[0])]
        copies.append(pltpu.make_async_copy(arrived[i], place, sem.at[2 + i]))
    for copy in copies:
        copy.start()
    for copy in copies:
        copy.wait()
    if not offset:
        refs[1][...] = (
            (buf[0].astype(f32) + buf[2].astype(f32) + buf[3].astype(f32)) + buf[1].astype(f32)
        ).astype(bf16)
        return
    for i in range(2):
        rows = arrived[i].shape[0]
        held = pl.ds(starts[i], rows)
        total = buf[i, held].astype(f32) + buf[2 + i, held].astype(f32)
        refs[i][held] = total.astype(bf16)
        if rows < buf.shape[1]:
            rest = pl.ds(rows - starts[i], rows)
            refs[i][rest] = buf[i, rest]


def ring_add(offset, where, parts, right, left, residual=None):
    _, rows, width = parts.shape
    extra = [] if residual is None else [residual]
    return pl.pallas_call(
        functools.partial(ring_kernel, offset),
        in_specs=[SCALARS] + [ANYWHERE] * (3 + len(extra)),
        out_specs=[WHOLE] * (2 - len(extra)),
        scratch_shapes=[pltpu.VMEM((4, rows, width), bf16), pltpu.SemaphoreType.DMA((4,))],
        out_shape=[jax.ShapeDtypeStruct((rows, width), bf16)] * (2 - len(extra)),
        compiler_params=pltpu.CompilerParams(vmem_limit_bytes=VMEM_BYTES),
        cost_estimate=SMALL_COST,
    )(where, parts, right, left, *extra)


def reduce_scatter_z(where, parts, far_a, far_b, residual):
    right = shift(far_a, "col", NZ, 1)
    left = shift(far_b, "col", NZ, -1)
    (right, left), residual = lax.optimization_barrier(((right, left), residual))
    for offset in (3, 2, 1):
        right, left = ring_add(offset, where, parts, right, left)
        right = shift(right, "col", NZ, 1)
        left = shift(left, "col", NZ, -1)
    return ring_add(0, where, parts, right, left, residual)[0]


def all_gather_z(block):
    cut = block.shape[0] // 2
    right, left = [block], [block]
    for _ in range(3):
        got = (shift(right[-1], "col", NZ, 1), shift(left[-1], "col", NZ, -1))
        got = lax.optimization_barrier(got)
        right.append(got[0])
        left.append(got[1])
    far_a = shift(right[3][:cut], "col", NZ, 1)
    far_b = shift(left[3][cut:], "col", NZ, -1)
    far = jnp.concatenate([far_a, far_b], axis=0)
    return [block, left[1], left[2], left[3], far, right[3], right[2], right[1]]


def work_to_natural(m, flip):
    pairs = []
    for depth in range(2):
        for y in range(NY):
            for z in range(NZ):
                there = 2 * (z % 2) + (m ^ (y % 2)), 2 * (z // 2) + y // 2
                pairs.append(
                    (
                        (depth * NY + y) * NZ + z,
                        ((depth ^ flip) * NY + there[0]) * NZ + there[1],
                    )
                )
    return pairs


def in_order(depth, same, other, axis):
    return jnp.where(
        depth == 0,
        jnp.concatenate([same, other], axis=axis),
        jnp.concatenate([other, same], axis=axis),
    )


def per_device(queries, key_states, value_states, residual, gain, w_out, w_gate, w_up):
    half = queries.shape[1]
    depth, x, y, z = (lax.axis_index(name) for name in ("depth", "x", "y", "col"))
    odd = (y % 2) == 1
    where = jnp.stack([depth, z, x, y]).astype(jnp.int32)
    block = w_out.shape[1]
    width = block // 2

    wo_half = lax.dynamic_slice_in_dim(w_out, depth * width, width, 1)
    wo_next = shift(wo_half, "y", NY, -1)
    wo_last = shift(wo_half, "y", NY, 1)
    pairs = []
    for i in range(NY):
        pairs.append((i, (i - 1) % NY))
    for i in range(NY):
        pairs.append((NY + i, NY + (i + 1) % NY))
    wo_far = lax.ppermute(jnp.where(depth == 0, wo_next, wo_last), ("depth", "y"), pairs)

    kv = jnp.concatenate([key_states[0], value_states[0]], axis=1)
    kv = lax.all_gather(kv, "depth", axis=0)
    attended = attend(where, queries[0], kv)
    own = [
        attended,
        shift(attended, "x", NX, -1),
        shift(attended, "x", NX, 2),
        shift(attended, "x", NX, 1),
    ]
    last_own, wo_far = lax.optimization_barrier((own[2], wo_far))
    other = [swap(value) for value in (own[0], own[1], last_own, own[3])]

    axes = ("depth", "y", "col")
    sent = []
    for m in range(2):
        chosen = jnp.where(odd, residual[1 - m], residual[m])
        for flip in range(2):
            sent.append(lax.dynamic_slice_in_dim(chosen, (depth ^ flip) * width, width, 1))
    sent, _ = lax.optimization_barrier((sent, own[1:]))
    got = [
        lax.ppermute(sent[2 * m + flip], axes, [(b, a) for a, b in work_to_natural(m, flip)])
        for m in range(2)
        for flip in range(2)
    ]
    same = jnp.concatenate([jnp.where(odd, got[2], got[0]), jnp.where(odd, got[0], got[2])], axis=1)
    flipped = jnp.concatenate([jnp.where(odd, got[3], got[1]), jnp.where(odd, got[1], got[3])], axis=1)
    res_work = in_order(depth, same, flipped, 0)

    rows = w_gate.shape[0] // 2
    held = [
        lax.dynamic_slice_in_dim(value, depth * rows, rows, 0) for value in (w_gate, w_up, gain[:, None])
    ]
    w2_half = jnp.concatenate(
        [(weights.astype(f32) * held[2]).astype(bf16) for weights in held[:2]], axis=1
    )
    w2_half, _ = lax.optimization_barrier((w2_half, (other, wo_far, got)))
    w2 = lax.all_gather(w2_half, "y", axis=0, tiled=True)

    pieces = [wo_next, wo_far, wo_last]
    parts, far_a, far_b = out_project(where, own, other, w_out, pieces)
    stream = reduce_scatter_z(where, parts, far_a, far_b, res_work)
    blocks = all_gather_z(stream)

    ((far, far_square, sent),) = gate_products((2,), where, blocks, w2)
    payload = (half + EXTRA, w2.shape[1])
    (far,) = small_call(far_kernel, [payload], far, far_square, swap(sent))
    after_far, far = lax.optimization_barrier((where, far))
    pairs = []
    for i in range(NX):
        pairs.append((i, (i + 1) % NX))
    for i in range(NX):
        pairs.append((NX + i, NX + (i - 1) % NX))
    far = lax.ppermute(far, ("depth", "x"), pairs)
    (right, right_square, right_sent), (left, left_square, left_sent) = gate_products(
        (1, 3), after_far, blocks, w2
    )
    ((mine, mine_square, mine_sent),) = gate_products((0,), where, blocks, w2)
    near_right, near_left = small_call(
        near_kernel,
        [payload] * 2,
        where,
        far,
        right,
        right_square,
        swap(right_sent),
        left,
        left_square,
        swap(left_sent),
    )
    from_left = shift(near_right, "x", NX, 1)
    from_right = shift(near_left, "x", NX, -1)
    stream_late, _ = lax.optimization_barrier((stream, near_right))
    back = []
    for m in range(2):
        for flip in range(2):
            first, second = stream_late[:, :width], stream_late[:, width:]
            sent = jnp.where(odd, second, first) if m == 0 else jnp.where(odd, first, second)
            sent = lax.dynamic_slice_in_dim(sent, (depth ^ flip) * half, half, 0)
            back.append(lax.ppermute(sent, axes, work_to_natural(m, flip)))
    pair = [in_order(depth, back[2 * m], back[2 * m + 1], 1) for m in range(2)]
    stream_out = jnp.stack(
        [jnp.where(odd, pair[1], pair[0]), jnp.where(odd, pair[0], pair[1])]
    )
    (hidden,) = small_call(
        last_kernel,
        [(1, half, w2.shape[1] // 2)],
        mine,
        mine_square,
        swap(mine_sent),
        from_left,
        from_right,
    )
    return (hidden, stream_out)


def solution(mesh):
    fine = Mesh(mesh.devices.reshape(2, NX, NY, NZ), ("depth", "x", "y", "col"))
    row = ("x", "y")
    return jax.shard_map(
        per_device,
        mesh=fine,
        in_specs=(
            P(row, "depth", "col"),
            P(row, "depth", "col"),
            P(row, "depth", "col"),
            P("col", "depth", row),
            P(row),
            P("col", row),
            P(row, "col"),
            P(row, "col"),
        ),
        out_specs=(P(row, "depth", "col"), P("col", "depth", row)),
        check_vma=False,
    )
```

```python
import functools
import jax
import jax.numpy as jnp
from jax import lax
from jax.experimental import pallas as pl
from jax.experimental.pallas import tpu as pltpu
from jax.sharding import Mesh, PartitionSpec as P

D = 8192
DH = 128
GROUP = 8
NX = 4
NY = 4
NZ = 8
EXTRA = 16

eps_norm = 1e-05
masked_score = -1e30
bf16 = jnp.bfloat16
f32 = jnp.float32
VMEM_BYTES = 24 * 1024 * 1024
SMALL_COST = pl.CostEstimate(flops=1024, bytes_accessed=1024, transcendentals=0)


def shift(value, axis, size, by):
    return lax.ppermute(value, axis, [(i, (i + by) % size) for i in range(size)])


def in_hbm(value):
    return pltpu.with_memory_space_constraint(value, pltpu.HBM)


def swap(value):
    return shift(value, "depth", 2, 1)


def attend_kernel(where_ref, q_ref, kv_ref, out_ref):
    depth = where_ref[0]
    half = q_ref.shape[0]
    keys = jnp.concatenate([kv_ref[0, :, :DH], kv_ref[1, :, :DH]], axis=0)
    values = jnp.concatenate([kv_ref[0, :, DH:], kv_ref[1, :, DH:]], axis=0)
    rows = jnp.concatenate([q_ref[:, h * DH : (h + 1) * DH] for h in range(GROUP)], axis=0)
    scores = lax.dot_general(
        rows, keys, (((1,), (1,)), ((), ())), preferred_element_type=f32
    ) * DH ** (-0.5)
    shape = scores.shape
    position = lax.broadcasted_iota(jnp.int32, shape, 0) % half + depth * half
    allowed = lax.broadcasted_iota(jnp.int32, shape, 1) <= position
    scores = jnp.where(allowed, scores, masked_score)
    top = jnp.max(scores, axis=-1, keepdims=True)
    expo = jnp.exp(scores - top)
    totals = jnp.sum(expo, axis=-1, keepdims=True)
    mixed = jnp.dot(expo.astype(bf16), values, preferred_element_type=f32) / totals
    mixed = mixed.astype(bf16)
    for h in range(GROUP):
        out_ref[:, h * DH : (h + 1) * DH] = mixed[h * half : (h + 1) * half]


def attend(where, queries, kv):
    half, features = queries.shape
    length = 2 * half
    return pl.pallas_call(
        attend_kernel,
        in_specs=[pl.BlockSpec(memory_space=pltpu.SMEM)]
        + [pl.BlockSpec(memory_space=pltpu.VMEM)] * 2,
        out_specs=pl.BlockSpec(memory_space=pltpu.VMEM),
        out_shape=jax.ShapeDtypeStruct((half, features), bf16),
        compiler_params=pltpu.CompilerParams(vmem_limit_bytes=VMEM_BYTES),
        cost_estimate=SMALL_COST,
    )(where, queries, kv)


ANYWHERE = pl.BlockSpec(memory_space=pl.ANY)
SCALARS = pl.BlockSpec(memory_space=pltpu.SMEM)
WHOLE = pl.BlockSpec(memory_space=pltpu.VMEM)


def out_kernel(where_ref, *refs):
    own, other, w_ref, pieces = refs[:4], refs[4:8], refs[8], refs[9:12]
    out_ref, far_a_ref, far_b_ref, att_buf, w_buf, att_sem, w_sem = refs[12:]
    depth, z, x, y = (where_ref[i] for i in range(4))
    rows = own[0].shape[0]
    width = w_buf.shape[2] // 2
    first = []
    for k in range(NX):
        for i, (side, ref) in enumerate(((depth, own[k]), (1 - depth, other[k]))):
            place = pl.ds(pl.multiple_of((2 * k + side) * rows, rows), rows)
            first.append(pltpu.make_async_copy(ref, att_buf.at[place], att_sem.at[k, i]))
    columns = pl.ds(pl.multiple_of(depth * width, width), width)
    copies = []
    for j, source in enumerate([w_ref.at[:, columns], *pieces]):
        place = w_buf.at[j // 2, :, pl.ds((j % 2) * width, width)]
        copies.append(pltpu.make_async_copy(source, place, w_sem.at[j]))
    for copy in first:
        copy.start()
    for copy in copies:
        copy.start()
    for copy in first:
        copy.wait()
    for j in range(0, NY, 2):
        copies[j].wait()
        copies[j + 1].wait()
        total = jnp.dot(att_buf[...], w_buf[j // 2], preferred_element_type=f32).astype(bf16)
        for i in range(2):
            block = (y + j + i) % NY
            held = pl.ds(pl.multiple_of((block % 2) * width, width), width)
            for k in range(NX):
                place = 2 * ((x + k) % NX) + block // 2
                out_ref[place, :, held] = total[
                    2 * k * rows : 2 * (k + 1) * rows, i * width : (i + 1) * width
                ]
    far = (z + NZ // 2) % NZ
    far_a_ref[...] = out_ref[far, :rows]
    far_b_ref[...] = out_ref[far, rows:]


def out_project(where, own, other, w_out, pieces):
    rows, features = own[0].shape
    width = w_out.shape[1] // 2
    return pl.pallas_call(
        out_kernel,
        in_specs=[SCALARS] + [ANYWHERE] * 12,
        out_specs=[WHOLE] * 3,
        out_shape=[jax.ShapeDtypeStruct((NZ, 2 * rows, 2 * width), bf16)]
        + [jax.ShapeDtypeStruct((rows, 2 * width), bf16)] * 2,
        scratch_shapes=[
            pltpu.VMEM((2 * NX * rows, features), bf16),
            pltpu.VMEM((NY // 2, features, 2 * width), bf16),
            pltpu.SemaphoreType.DMA((NX, 2)),
            pltpu.SemaphoreType.DMA((NY,)),
        ],
        compiler_params=pltpu.CompilerParams(vmem_limit_bytes=VMEM_BYTES),
        cost_estimate=SMALL_COST,
    )(where, *own, *other, in_hbm(w_out), *pieces)


def put_squares(ref, row):
    rows = ref.shape[0] - EXTRA
    high = row.astype(bf16)
    rest = row - high.astype(f32)
    middle = rest.astype(bf16)
    low = (rest - middle.astype(f32)).astype(bf16)
    index = lax.broadcasted_iota(jnp.int32, row.shape, 0)
    first = jnp.where(index == 0, high.astype(f32), jnp.where(index == 1, middle.astype(f32), 0.0))
    first = jnp.where(index == 2, low.astype(f32), first)
    both = jnp.concatenate([first, jnp.zeros_like(first)], axis=0).astype(bf16)
    ref[rows:] = jnp.zeros((EXTRA, ref.shape[1]), bf16)
    ref[rows:, : row.shape[1]] = both


def get_squares(ref, count):
    held = ref[ref.shape[0] - EXTRA :, :count].astype(f32)
    return jnp.broadcast_to(jnp.sum(held, axis=0, keepdims=True), (8, count))


def gate_kernel(seqs, where_ref, *refs):
    blocks, weight_ref = refs[:NZ], refs[NZ]
    outs = refs[NZ + 1 : -4]
    w_buf, x_buf, w_sem, x_sem = refs[-4:]
    depth, z, x = (where_ref[i] for i in range(3))
    rows, pair = blocks[0].shape[0] // 2, blocks[0].shape[1]
    chunks, _, chunk = w_buf.shape

    def rows_copy(ref, i, h, side):
        place = depth if side == 0 else 1 - depth
        return pltpu.make_async_copy(
            ref.at[pl.ds(pl.multiple_of(place * rows, rows), rows)],
            x_buf.at[pl.ds((2 * i + side) * rows, rows), pl.ds(h * pair, pair)],
            x_sem.at[i, h, side],
        )

    def weight_copy(c):
        return pltpu.make_async_copy(
            weight_ref.at[:, pl.ds(c * chunk, chunk)], w_buf.at[c], w_sem.at[c]
        )

    for c in range(chunks):
        weight_copy(c).start()
    for h in range(2):
        for i, k in enumerate(seqs):
            ring = (2 * ((x + k) % NX) + h - z + NZ) % NZ
            for j in range(NZ):

                @pl.when(ring == j)
                def _():
                    rows_copy(blocks[j], i, h, 0).start()
                    rows_copy(blocks[j], i, h, 1).start()

    for h in range(2):
        for i in range(len(seqs)):
            for side in range(2):
                rows_copy(blocks[0], i, h, side).wait()
    squares = 0.0
    for n in range(0, 2 * pair, DH):
        wide = x_buf[:, n : n + DH].astype(f32)
        squares = squares + wide * wide
    column = jnp.sum(squares, axis=1, keepdims=True)
    column = jnp.broadcast_to(column, squares.shape)
    for i in range(len(seqs)):
        start = 2 * i * rows
        outs[3 * i + 1][...] = column[start : start + rows].T[:8]
        put_squares(outs[3 * i + 2], column[start + rows : start + 2 * rows].T[:8])
    for c in range(chunks):
        weight_copy(c).wait()
        total = jnp.dot(x_buf[...], w_buf[c], preferred_element_type=f32).astype(bf16)
        held = slice(c * chunk, (c + 1) * chunk)
        for i in range(len(seqs)):
            start = 2 * i * rows
            outs[3 * i][:, held] = total[start : start + rows]
            outs[3 * i + 2][:rows, held] = total[start + rows : start + 2 * rows]


def gate_products(seqs, where, blocks, weights):
    rows, pair = blocks[0].shape
    rows = rows // 2
    features, width = weights.shape
    n = len(seqs)
    chunks = 4
    results = pl.pallas_call(
        functools.partial(gate_kernel, seqs),
        in_specs=[SCALARS] + [ANYWHERE] * (NZ + 1),
        out_specs=[WHOLE] * (3 * n),
        scratch_shapes=[
            pltpu.VMEM((chunks, features, width // chunks), bf16),
            pltpu.VMEM((2 * n * rows, 2 * pair), bf16),
            pltpu.SemaphoreType.DMA((chunks,)),
            pltpu.SemaphoreType.DMA((n, 2, 2)),
        ],
        out_shape=[
            jax.ShapeDtypeStruct((rows, width), bf16),
            jax.ShapeDtypeStruct((8, rows), f32),
            jax.ShapeDtypeStruct((rows + EXTRA, width), bf16),
        ]
        * n,
        compiler_params=pltpu.CompilerParams(vmem_limit_bytes=VMEM_BYTES),
        cost_estimate=SMALL_COST,
    )(where, *blocks, in_hbm(weights))
    return [results[3 * i : 3 * i + 3] for i in range(n)]


def far_kernel(own_ref, square_ref, other_ref, out_ref):
    rows = own_ref.shape[0]
    out_ref[:rows] = (own_ref[...].astype(f32) + other_ref[:rows].astype(f32)).astype(bf16)
    put_squares(out_ref, square_ref[...] + get_squares(other_ref, rows))


def near_kernel(where_ref, far_ref, *refs):
    rows = refs[0].shape[0]
    far = far_ref[:rows].astype(f32)
    far_square = get_squares(far_ref, rows)
    for i in range(2):
        own_ref, square_ref, other_ref = refs[3 * i : 3 * i + 3]
        out_ref = refs[6 + i]
        mine = where_ref[0] == i
        total = own_ref[...].astype(f32) + other_ref[:rows].astype(f32)
        out_ref[:rows] = (total + jnp.where(mine, far, 0.0)).astype(bf16)
        squares = square_ref[...] + get_squares(other_ref, rows)
        put_squares(out_ref, squares + jnp.where(mine, far_square, 0.0))


def last_kernel(own_ref, square_ref, other_ref, left_ref, right_ref, out_ref):
    rows, width = own_ref.shape
    units = width // 2
    squares = square_ref[...]
    total = own_ref[...].astype(f32)
    for ref in (other_ref, left_ref, right_ref):
        squares = squares + get_squares(ref, rows)
        total = total + ref[:rows].astype(f32)
    squares = jnp.broadcast_to(squares[:1], (DH, rows)).T[:, :1]
    total = total * lax.rsqrt(squares / D + eps_norm)
    gate, up = total[:, :units], total[:, units:]
    out_ref[0] = (gate / (1.0 + jnp.exp(-gate)) * up).astype(bf16)


def small_call(kernel, shapes, *operands):
    first = operands[0].dtype == jnp.int32
    return pl.pallas_call(
        kernel,
        in_specs=[SCALARS] * first + [WHOLE] * (len(operands) - first),
        out_specs=[WHOLE] * len(shapes),
        out_shape=[jax.ShapeDtypeStruct(shape, bf16) for shape in shapes],
        compiler_params=pltpu.CompilerParams(vmem_limit_bytes=VMEM_BYTES),
        cost_estimate=SMALL_COST,
    )(*operands)


def ring_kernel(offset, where_ref, parts_ref, right_ref, left_ref, *refs):
    z = where_ref[1]
    buf, sem = refs[-2:]
    if offset:
        sources = (parts_ref.at[(z + offset) % NZ], parts_ref.at[(z + NZ - offset) % NZ])
    else:
        sources = (parts_ref.at[z], refs[0])
    arrived = (right_ref, left_ref)
    starts = (0, buf.shape[1] - left_ref.shape[0])
    copies = []
    for i in range(2):
        copies.append(pltpu.make_async_copy(sources[i], buf.at[i], sem.at[i]))
        place = buf.at[2 + i, pl.ds(starts[i], arrived[i].shape[0])]
        copies.append(pltpu.make_async_copy(arrived[i], place, sem.at[2 + i]))
    for copy in copies:
        copy.start()
    for copy in copies:
        copy.wait()
    if not offset:
        refs[1][...] = (
            (buf[0].astype(f32) + buf[2].astype(f32) + buf[3].astype(f32)) + buf[1].astype(f32)
        ).astype(bf16)
        return
    for i in range(2):
        rows = arrived[i].shape[0]
        held = pl.ds(starts[i], rows)
        total = buf[i, held].astype(f32) + buf[2 + i, held].astype(f32)
        refs[i][held] = total.astype(bf16)
        if rows < buf.shape[1]:
            rest = pl.ds(rows - starts[i], rows)
            refs[i][rest] = buf[i, rest]


def ring_add(offset, where, parts, right, left, residual=None):
    _, rows, width = parts.shape
    extra = [] if residual is None else [residual]
    return pl.pallas_call(
        functools.partial(ring_kernel, offset),
        in_specs=[SCALARS] + [ANYWHERE] * (3 + len(extra)),
        out_specs=[WHOLE] * (2 - len(extra)),
        scratch_shapes=[pltpu.VMEM((4, rows, width), bf16), pltpu.SemaphoreType.DMA((4,))],
        out_shape=[jax.ShapeDtypeStruct((rows, width), bf16)] * (2 - len(extra)),
        compiler_params=pltpu.CompilerParams(vmem_limit_bytes=VMEM_BYTES),
        cost_estimate=SMALL_COST,
    )(where, parts, right, left, *extra)


def reduce_scatter_z(where, parts, far_a, far_b, residual):
    right = shift(far_a, "col", NZ, 1)
    left = shift(far_b, "col", NZ, -1)
    (right, left), residual = lax.optimization_barrier(((right, left), residual))
    for offset in (3, 2, 1):
        right, left = ring_add(offset, where, parts, right, left)
        right = shift(right, "col", NZ, 1)
        left = shift(left, "col", NZ, -1)
    return ring_add(0, where, parts, right, left, residual)[0]


def all_gather_z(block):
    cut = block.shape[0] // 2
    right, left = [block], [block]
    for _ in range(3):
        got = (shift(right[-1], "col", NZ, 1), shift(left[-1], "col", NZ, -1))
        got = lax.optimization_barrier(got)
        right.append(got[0])
        left.append(got[1])
    far_a = shift(right[3][:cut], "col", NZ, 1)
    far_b = shift(left[3][cut:], "col", NZ, -1)
    far = jnp.concatenate([far_a, far_b], axis=0)
    return [block, left[1], left[2], left[3], far, right[3], right[2], right[1]]


def work_to_natural(m):
    pairs = []
    for y in range(NY):
        for z in range(NZ):
            there = 2 * (z % 2) + (m ^ (y % 2)), 2 * (z // 2) + y // 2
            pairs.append((y * NZ + z, there[0] * NZ + there[1]))
    return pairs


def in_order(depth, same, other, axis):
    return jnp.where(
        depth == 0,
        jnp.concatenate([same, other], axis=axis),
        jnp.concatenate([other, same], axis=axis),
    )


def per_device(queries, key_states, value_states, residual, gain, w_out, w_gate, w_up):
    half = queries.shape[1]
    depth, x, y, z = (lax.axis_index(name) for name in ("depth", "x", "y", "col"))
    odd = (y % 2) == 1
    where = jnp.stack([depth, z, x, y]).astype(jnp.int32)
    block = w_out.shape[1]
    width = block // 2

    wo_half = lax.dynamic_slice_in_dim(w_out, depth * width, width, 1)
    wo_next = shift(wo_half, "y", NY, -1)
    wo_last = shift(wo_half, "y", NY, 1)
    pairs = []
    for i in range(NY):
        pairs.append((i, (i - 1) % NY))
    for i in range(NY):
        pairs.append((NY + i, NY + (i + 1) % NY))
    wo_far = lax.ppermute(jnp.where(depth == 0, wo_next, wo_last), ("depth", "y"), pairs)

    kv = jnp.concatenate([key_states[0], value_states[0]], axis=1)
    kv = lax.all_gather(kv, "depth", axis=0)
    attended = attend(where, queries[0], kv)
    own = [
        attended,
        shift(attended, "x", NX, -1),
        shift(attended, "x", NX, 2),
        shift(attended, "x", NX, 1),
    ]
    rows = w_gate.shape[0] // 2
    held = [
        lax.dynamic_slice_in_dim(value, depth * rows, rows, 0) for value in (w_gate, w_up, gain[:, None])
    ]
    w2_half = jnp.concatenate(
        [(weights.astype(f32) * held[2]).astype(bf16) for weights in held[:2]], axis=1
    )
    own[1:], w2_half = lax.optimization_barrier((own[1:], w2_half))
    last_own, wo_far = lax.optimization_barrier((own[2], wo_far))
    other = [swap(value) for value in (own[0], own[1], last_own, own[3])]

    axes = ("y", "col")
    kept, given = (
        lax.dynamic_slice_in_dim(residual, side * width, width, 2) for side in (depth, 1 - depth)
    )
    both = in_order(depth, kept, swap(given), 1)
    sent = [jnp.where(odd, both[1 - m], both[m]) for m in range(2)]
    sent, _ = lax.optimization_barrier((sent, other[1::2]))
    got = [
        lax.ppermute(sent[m], axes, [(b, a) for a, b in work_to_natural(m)]) for m in range(2)
    ]
    res_work = jnp.concatenate(
        [jnp.where(odd, got[1], got[0]), jnp.where(odd, got[0], got[1])], axis=1
    )

    w2_half, _ = lax.optimization_barrier((w2_half, (other, wo_far, got)))
    w2 = lax.all_gather(w2_half, "y", axis=0, tiled=True)

    pieces = [wo_next, wo_far, wo_last]
    parts, far_a, far_b = out_project(where, own, other, w_out, pieces)
    stream = reduce_scatter_z(where, parts, far_a, far_b, res_work)
    blocks = all_gather_z(stream)

    ((far, far_square, sent),) = gate_products((2,), where, blocks, w2)
    payload = (half + EXTRA, w2.shape[1])
    (far,) = small_call(far_kernel, [payload], far, far_square, swap(sent))
    after_far, far = lax.optimization_barrier((where, far))
    pairs = []
    for i in range(NX):
        pairs.append((i, (i + 1) % NX))
    for i in range(NX):
        pairs.append((NX + i, NX + (i - 1) % NX))
    far = lax.ppermute(far, ("depth", "x"), pairs)
    (right, right_square, right_sent), (left, left_square, left_sent) = gate_products(
        (1, 3), after_far, blocks, w2
    )
    ((mine, mine_square, mine_sent),) = gate_products((0,), where, blocks, w2)
    near_right, near_left = small_call(
        near_kernel,
        [payload] * 2,
        where,
        far,
        right,
        right_square,
        swap(right_sent),
        left,
        left_square,
        swap(left_sent),
    )
    from_left = shift(near_right, "x", NX, 1)
    from_right = shift(near_left, "x", NX, -1)
    stream_late, _ = lax.optimization_barrier((stream, near_right))
    back = []
    for m in range(2):
        first, second = stream_late[:, :width], stream_late[:, width:]
        sent = jnp.where(odd, second, first) if m == 0 else jnp.where(odd, first, second)
        back.append(lax.ppermute(sent, axes, work_to_natural(m)))
    back = jnp.stack([jnp.where(odd, back[1], back[0]), jnp.where(odd, back[0], back[1])])
    kept, given = (
        lax.dynamic_slice_in_dim(back, side * half, half, 1) for side in (depth, 1 - depth)
    )
    stream_out = in_order(depth, kept, swap(given), 2)
    (hidden,) = small_call(
        last_kernel,
        [(1, half, w2.shape[1] // 2)],
        mine,
        mine_square,
        swap(mine_sent),
        from_left,
        from_right,
    )
    return (hidden, stream_out)


def solution(mesh):
    fine = Mesh(mesh.devices.reshape(2, NX, NY, NZ), ("depth", "x", "y", "col"))
    row = ("x", "y")
    return jax.shard_map(
        per_device,
        mesh=fine,
        in_specs=(
            P(row, "depth", "col"),
            P(row, "depth", "col"),
            P(row, "depth", "col"),
            P("col", "depth", row),
            P(row),
            P("col", row),
            P(row, "col"),
            P(row, "col"),
        ),
        out_specs=(P(row, "depth", "col"), P("col", "depth", row)),
        check_vma=False,
    )
```

```python
import functools
import jax
import jax.numpy as jnp
from jax import lax
from jax.experimental import pallas as pl
from jax.experimental.pallas import tpu as pltpu
from jax.sharding import Mesh, PartitionSpec as P

D = 8192
DH = 128
GROUP = 8
NX = 4
NY = 4
NZ = 8
EXTRA = 16

eps_norm = 1e-05
masked_score = -1e30
bf16 = jnp.bfloat16
f32 = jnp.float32
VMEM_BYTES = 24 * 1024 * 1024
SMALL_COST = pl.CostEstimate(flops=1024, bytes_accessed=1024, transcendentals=0)


def shift(value, axis, size, by):
    return lax.ppermute(value, axis, [(i, (i + by) % size) for i in range(size)])


def in_hbm(value):
    return pltpu.with_memory_space_constraint(value, pltpu.HBM)


def swap(value):
    return shift(value, "depth", 2, 1)


def attend_kernel(where_ref, q_ref, kv_ref, out_ref):
    depth = where_ref[0]
    half = q_ref.shape[0]
    keys = jnp.concatenate([kv_ref[0, :, :DH], kv_ref[1, :, :DH]], axis=0)
    values = jnp.concatenate([kv_ref[0, :, DH:], kv_ref[1, :, DH:]], axis=0)
    rows = jnp.concatenate([q_ref[:, h * DH : (h + 1) * DH] for h in range(GROUP)], axis=0)
    scores = lax.dot_general(
        rows, keys, (((1,), (1,)), ((), ())), preferred_element_type=f32
    ) * DH ** (-0.5)
    shape = scores.shape
    position = lax.broadcasted_iota(jnp.int32, shape, 0) % half + depth * half
    allowed = lax.broadcasted_iota(jnp.int32, shape, 1) <= position
    scores = jnp.where(allowed, scores, masked_score)
    top = jnp.max(scores, axis=-1, keepdims=True)
    expo = jnp.exp(scores - top)
    totals = jnp.sum(expo, axis=-1, keepdims=True)
    mixed = jnp.dot(expo.astype(bf16), values, preferred_element_type=f32) / totals
    mixed = mixed.astype(bf16)
    for h in range(GROUP):
        out_ref[:, h * DH : (h + 1) * DH] = mixed[h * half : (h + 1) * half]


def attend(where, queries, kv):
    half, features = queries.shape
    length = 2 * half
    return pl.pallas_call(
        attend_kernel,
        in_specs=[pl.BlockSpec(memory_space=pltpu.SMEM)]
        + [pl.BlockSpec(memory_space=pltpu.VMEM)] * 2,
        out_specs=pl.BlockSpec(memory_space=pltpu.VMEM),
        out_shape=jax.ShapeDtypeStruct((half, features), bf16),
        compiler_params=pltpu.CompilerParams(vmem_limit_bytes=VMEM_BYTES),
        cost_estimate=SMALL_COST,
    )(where, queries, kv)


ANYWHERE = pl.BlockSpec(memory_space=pl.ANY)
SCALARS = pl.BlockSpec(memory_space=pltpu.SMEM)
WHOLE = pl.BlockSpec(memory_space=pltpu.VMEM)


def out_kernel(where_ref, *refs):
    own, other, w_ref, pieces = refs[:4], refs[4:8], refs[8], refs[9:12]
    out_ref, far_a_ref, far_b_ref, att_buf, w_buf, att_sem, w_sem = refs[12:]
    depth, z, x, y = (where_ref[i] for i in range(4))
    rows = own[0].shape[0]
    width = w_buf.shape[2] // 2
    first = []
    for k in range(NX):
        for i, (side, ref) in enumerate(((depth, own[k]), (1 - depth, other[k]))):
            place = pl.ds(pl.multiple_of((2 * k + side) * rows, rows), rows)
            first.append(pltpu.make_async_copy(ref, att_buf.at[place], att_sem.at[k, i]))
    columns = pl.ds(pl.multiple_of(depth * width, width), width)
    copies = []
    for j, source in enumerate([w_ref.at[:, columns], *pieces]):
        place = w_buf.at[j // 2, :, pl.ds((j % 2) * width, width)]
        copies.append(pltpu.make_async_copy(source, place, w_sem.at[j]))
    for copy in first:
        copy.start()
    for copy in copies:
        copy.start()
    for copy in first:
        copy.wait()
    for j in range(0, NY, 2):
        copies[j].wait()
        copies[j + 1].wait()
        total = jnp.dot(att_buf[...], w_buf[j // 2], preferred_element_type=f32).astype(bf16)
        for i in range(2):
            block = (y + j + i) % NY
            held = pl.ds(pl.multiple_of((block % 2) * width, width), width)
            for k in range(NX):
                place = 2 * ((x + k) % NX) + block // 2
                out_ref[place, :, held] = total[
                    2 * k * rows : 2 * (k + 1) * rows, i * width : (i + 1) * width
                ]
    far = (z + NZ // 2) % NZ
    far_a_ref[...] = out_ref[far, :rows]
    far_b_ref[...] = out_ref[far, rows:]


def out_project(where, own, other, w_out, pieces):
    rows, features = own[0].shape
    width = w_out.shape[1] // 2
    return pl.pallas_call(
        out_kernel,
        in_specs=[SCALARS] + [ANYWHERE] * 12,
        out_specs=[WHOLE] * 3,
        out_shape=[jax.ShapeDtypeStruct((NZ, 2 * rows, 2 * width), bf16)]
        + [jax.ShapeDtypeStruct((rows, 2 * width), bf16)] * 2,
        scratch_shapes=[
            pltpu.VMEM((2 * NX * rows, features), bf16),
            pltpu.VMEM((NY // 2, features, 2 * width), bf16),
            pltpu.SemaphoreType.DMA((NX, 2)),
            pltpu.SemaphoreType.DMA((NY,)),
        ],
        compiler_params=pltpu.CompilerParams(vmem_limit_bytes=VMEM_BYTES),
        cost_estimate=SMALL_COST,
    )(where, *own, *other, in_hbm(w_out), *pieces)


def put_squares(ref, row):
    rows = ref.shape[0] - EXTRA
    high = row.astype(bf16)
    rest = row - high.astype(f32)
    middle = rest.astype(bf16)
    low = (rest - middle.astype(f32)).astype(bf16)
    index = lax.broadcasted_iota(jnp.int32, row.shape, 0)
    first = jnp.where(index == 0, high.astype(f32), jnp.where(index == 1, middle.astype(f32), 0.0))
    first = jnp.where(index == 2, low.astype(f32), first)
    both = jnp.concatenate([first, jnp.zeros_like(first)], axis=0).astype(bf16)
    ref[rows:] = jnp.zeros((EXTRA, ref.shape[1]), bf16)
    ref[rows:, : row.shape[1]] = both


def get_squares(ref, count):
    held = ref[ref.shape[0] - EXTRA :, :count].astype(f32)
    return jnp.broadcast_to(jnp.sum(held, axis=0, keepdims=True), (8, count))


def gate_kernel(seqs, where_ref, *refs):
    blocks, weight_ref = refs[:NZ], refs[NZ]
    outs = refs[NZ + 1 : -4]
    w_buf, x_buf, w_sem, x_sem = refs[-4:]
    depth, z, x = (where_ref[i] for i in range(3))
    rows, pair = blocks[0].shape[0] // 2, blocks[0].shape[1]
    chunks, _, chunk = w_buf.shape

    def rows_copy(ref, i, h, side):
        place = depth if side == 0 else 1 - depth
        return pltpu.make_async_copy(
            ref.at[pl.ds(pl.multiple_of(place * rows, rows), rows)],
            x_buf.at[pl.ds((2 * i + side) * rows, rows), pl.ds(h * pair, pair)],
            x_sem.at[i, h, side],
        )

    def weight_copy(c):
        return pltpu.make_async_copy(
            weight_ref.at[:, pl.ds(c * chunk, chunk)], w_buf.at[c], w_sem.at[c]
        )

    for c in range(chunks):
        weight_copy(c).start()
    for h in range(2):
        for i, k in enumerate(seqs):
            ring = (2 * ((x + k) % NX) + h - z + NZ) % NZ
            for j in range(NZ):

                @pl.when(ring == j)
                def _():
                    rows_copy(blocks[j], i, h, 0).start()
                    rows_copy(blocks[j], i, h, 1).start()

    for h in range(2):
        for i in range(len(seqs)):
            for side in range(2):
                rows_copy(blocks[0], i, h, side).wait()
    squares = 0.0
    for n in range(0, 2 * pair, DH):
        wide = x_buf[:, n : n + DH].astype(f32)
        squares = squares + wide * wide
    column = jnp.sum(squares, axis=1, keepdims=True)
    column = jnp.broadcast_to(column, squares.shape)
    for i in range(len(seqs)):
        start = 2 * i * rows
        outs[3 * i + 1][...] = column[start : start + rows].T[:8]
        put_squares(outs[3 * i + 2], column[start + rows : start + 2 * rows].T[:8])
    for c in range(chunks):
        weight_copy(c).wait()
        total = jnp.dot(x_buf[...], w_buf[c], preferred_element_type=f32).astype(bf16)
        held = slice(c * chunk, (c + 1) * chunk)
        for i in range(len(seqs)):
            start = 2 * i * rows
            outs[3 * i][:, held] = total[start : start + rows]
            outs[3 * i + 2][:rows, held] = total[start + rows : start + 2 * rows]


def gate_products(seqs, where, blocks, weights):
    rows, pair = blocks[0].shape
    rows = rows // 2
    features, width = weights.shape
    n = len(seqs)
    chunks = 4
    results = pl.pallas_call(
        functools.partial(gate_kernel, seqs),
        in_specs=[SCALARS] + [ANYWHERE] * (NZ + 1),
        out_specs=[WHOLE] * (3 * n),
        scratch_shapes=[
            pltpu.VMEM((chunks, features, width // chunks), bf16),
            pltpu.VMEM((2 * n * rows, 2 * pair), bf16),
            pltpu.SemaphoreType.DMA((chunks,)),
            pltpu.SemaphoreType.DMA((n, 2, 2)),
        ],
        out_shape=[
            jax.ShapeDtypeStruct((rows, width), bf16),
            jax.ShapeDtypeStruct((8, rows), f32),
            jax.ShapeDtypeStruct((rows + EXTRA, width), bf16),
        ]
        * n,
        compiler_params=pltpu.CompilerParams(vmem_limit_bytes=VMEM_BYTES),
        cost_estimate=SMALL_COST,
    )(where, *blocks, in_hbm(weights))
    return [results[3 * i : 3 * i + 3] for i in range(n)]


def far_kernel(own_ref, square_ref, other_ref, out_ref):
    rows = own_ref.shape[0]
    out_ref[:rows] = (own_ref[...].astype(f32) + other_ref[:rows].astype(f32)).astype(bf16)
    put_squares(out_ref, square_ref[...] + get_squares(other_ref, rows))


def near_kernel(where_ref, far_ref, *refs):
    rows = refs[0].shape[0]
    far = far_ref[:rows].astype(f32)
    far_square = get_squares(far_ref, rows)
    for i in range(2):
        own_ref, square_ref, other_ref = refs[3 * i : 3 * i + 3]
        out_ref = refs[6 + i]
        mine = where_ref[0] == i
        total = own_ref[...].astype(f32) + other_ref[:rows].astype(f32)
        out_ref[:rows] = (total + jnp.where(mine, far, 0.0)).astype(bf16)
        squares = square_ref[...] + get_squares(other_ref, rows)
        put_squares(out_ref, squares + jnp.where(mine, far_square, 0.0))


def last_kernel(own_ref, square_ref, other_ref, left_ref, right_ref, out_ref):
    rows, width = own_ref.shape
    units = width // 2
    squares = square_ref[...]
    total = own_ref[...].astype(f32)
    for ref in (other_ref, left_ref, right_ref):
        squares = squares + get_squares(ref, rows)
        total = total + ref[:rows].astype(f32)
    squares = jnp.broadcast_to(squares[:1], (DH, rows)).T[:, :1]
    total = total * lax.rsqrt(squares / D + eps_norm)
    gate, up = total[:, :units], total[:, units:]
    out_ref[0] = (gate / (1.0 + jnp.exp(-gate)) * up).astype(bf16)


def small_call(kernel, shapes, *operands):
    first = operands[0].dtype == jnp.int32
    return pl.pallas_call(
        kernel,
        in_specs=[SCALARS] * first + [WHOLE] * (len(operands) - first),
        out_specs=[WHOLE] * len(shapes),
        out_shape=[jax.ShapeDtypeStruct(shape, bf16) for shape in shapes],
        compiler_params=pltpu.CompilerParams(vmem_limit_bytes=VMEM_BYTES),
        cost_estimate=SMALL_COST,
    )(*operands)


def ring_kernel(offset, where_ref, parts_ref, right_ref, left_ref, *refs):
    z = where_ref[1]
    buf, sem = refs[-2:]
    if offset:
        sources = (parts_ref.at[(z + offset) % NZ], parts_ref.at[(z + NZ - offset) % NZ])
    else:
        sources = (parts_ref.at[z], refs[0])
    arrived = (right_ref, left_ref)
    starts = (0, buf.shape[1] - left_ref.shape[0])
    copies = []
    for i in range(2):
        copies.append(pltpu.make_async_copy(sources[i], buf.at[i], sem.at[i]))
        place = buf.at[2 + i, pl.ds(starts[i], arrived[i].shape[0])]
        copies.append(pltpu.make_async_copy(arrived[i], place, sem.at[2 + i]))
    for copy in copies:
        copy.start()
    for copy in copies:
        copy.wait()
    if not offset:
        refs[1][...] = (
            (buf[0].astype(f32) + buf[2].astype(f32) + buf[3].astype(f32)) + buf[1].astype(f32)
        ).astype(bf16)
        return
    for i in range(2):
        rows = arrived[i].shape[0]
        held = pl.ds(starts[i], rows)
        total = buf[i, held].astype(f32) + buf[2 + i, held].astype(f32)
        refs[i][held] = total.astype(bf16)
        if rows < buf.shape[1]:
            rest = pl.ds(rows - starts[i], rows)
            refs[i][rest] = buf[i, rest]


def ring_add(offset, where, parts, right, left, residual=None):
    _, rows, width = parts.shape
    extra = [] if residual is None else [residual]
    return pl.pallas_call(
        functools.partial(ring_kernel, offset),
        in_specs=[SCALARS] + [ANYWHERE] * (3 + len(extra)),
        out_specs=[WHOLE] * (2 - len(extra)),
        scratch_shapes=[pltpu.VMEM((4, rows, width), bf16), pltpu.SemaphoreType.DMA((4,))],
        out_shape=[jax.ShapeDtypeStruct((rows, width), bf16)] * (2 - len(extra)),
        compiler_params=pltpu.CompilerParams(vmem_limit_bytes=VMEM_BYTES),
        cost_estimate=SMALL_COST,
    )(where, parts, right, left, *extra)


def reduce_scatter_z(where, parts, far_a, far_b, residual):
    right = shift(far_a, "col", NZ, 1)
    left = shift(far_b, "col", NZ, -1)
    (right, left), residual = lax.optimization_barrier(((right, left), residual))
    for offset in (3, 2, 1):
        right, left = ring_add(offset, where, parts, right, left)
        right = shift(right, "col", NZ, 1)
        left = shift(left, "col", NZ, -1)
    return ring_add(0, where, parts, right, left, residual)[0]


def all_gather_z(block):
    cut = block.shape[0] // 2
    right, left = [block], [block]
    for _ in range(3):
        got = (shift(right[-1], "col", NZ, 1), shift(left[-1], "col", NZ, -1))
        got = lax.optimization_barrier(got)
        right.append(got[0])
        left.append(got[1])
    far_a = shift(right[3][:cut], "col", NZ, 1)
    far_b = shift(left[3][cut:], "col", NZ, -1)
    far = jnp.concatenate([far_a, far_b], axis=0)
    return [block, left[1], left[2], left[3], far, right[3], right[2], right[1]]


def work_to_natural(m):
    pairs = []
    for y in range(NY):
        for z in range(NZ):
            there = 2 * (z % 2) + (m ^ (y % 2)), 2 * (z // 2) + y // 2
            pairs.append((y * NZ + z, there[0] * NZ + there[1]))
    return pairs


def in_order(depth, same, other, axis):
    return jnp.where(
        depth == 0,
        jnp.concatenate([same, other], axis=axis),
        jnp.concatenate([other, same], axis=axis),
    )


def per_device(queries, key_states, value_states, residual, gain, w_out, w_gate, w_up):
    half = queries.shape[1]
    depth, x, y, z = (lax.axis_index(name) for name in ("depth", "x", "y", "col"))
    odd = (y % 2) == 1
    where = jnp.stack([depth, z, x, y]).astype(jnp.int32)
    block = w_out.shape[1]
    width = block // 2

    wo_half = lax.dynamic_slice_in_dim(w_out, depth * width, width, 1)
    wo_next = shift(wo_half, "y", NY, -1)
    wo_last = shift(wo_half, "y", NY, 1)
    pairs = []
    for i in range(NY):
        pairs.append((i, (i - 1) % NY))
    for i in range(NY):
        pairs.append((NY + i, NY + (i + 1) % NY))
    wo_far = lax.ppermute(jnp.where(depth == 0, wo_next, wo_last), ("depth", "y"), pairs)

    kv = jnp.concatenate([key_states[0], value_states[0]], axis=1)
    kv = lax.all_gather(kv, "depth", axis=0)
    attended = attend(where, queries[0], kv)
    own = [
        attended,
        shift(attended, "x", NX, -1),
        shift(attended, "x", NX, 2),
        shift(attended, "x", NX, 1),
    ]
    last_own, wo_far = lax.optimization_barrier((own[2], wo_far))
    other = [swap(value) for value in (own[0], own[1], last_own, own[3])]

    axes = ("y", "col")
    kept, given = (
        lax.dynamic_slice_in_dim(residual, side * width, width, 2) for side in (depth, 1 - depth)
    )
    both = in_order(depth, kept, swap(given), 1)
    sent = [jnp.where(odd, both[1 - m], both[m]) for m in range(2)]
    sent, _ = lax.optimization_barrier((sent, own[1:]))
    got = [
        lax.ppermute(sent[m], axes, [(b, a) for a, b in work_to_natural(m)]) for m in range(2)
    ]
    res_work = jnp.concatenate(
        [jnp.where(odd, got[1], got[0]), jnp.where(odd, got[0], got[1])], axis=1
    )

    rows = w_gate.shape[0] // 2
    held = [
        lax.dynamic_slice_in_dim(value, depth * rows, rows, 0) for value in (w_gate, w_up, gain[:, None])
    ]
    w2_half = jnp.concatenate(
        [(weights.astype(f32) * held[2]).astype(bf16) for weights in held[:2]], axis=1
    )
    w2_half, _ = lax.optimization_barrier((w2_half, (other, wo_far, got)))
    w2 = lax.all_gather(w2_half, "y", axis=0, tiled=True)

    pieces = [wo_next, wo_far, wo_last]
    parts, far_a, far_b = out_project(where, own, other, w_out, pieces)
    stream = reduce_scatter_z(where, parts, far_a, far_b, res_work)
    blocks = all_gather_z(stream)

    ((far, far_square, sent),) = gate_products((2,), where, blocks, w2)
    payload = (half + EXTRA, w2.shape[1])
    (far,) = small_call(far_kernel, [payload], far, far_square, swap(sent))
    after_far, far = lax.optimization_barrier((where, far))
    pairs = []
    for i in range(NX):
        pairs.append((i, (i + 1) % NX))
    for i in range(NX):
        pairs.append((NX + i, NX + (i - 1) % NX))
    far = lax.ppermute(far, ("depth", "x"), pairs)
    (right, right_square, right_sent), (left, left_square, left_sent) = gate_products(
        (1, 3), after_far, blocks, w2
    )
    ((mine, mine_square, mine_sent),) = gate_products((0,), where, blocks, w2)
    near_right, near_left = small_call(
        near_kernel,
        [payload] * 2,
        where,
        far,
        right,
        right_square,
        swap(right_sent),
        left,
        left_square,
        swap(left_sent),
    )
    from_left = shift(near_right, "x", NX, 1)
    from_right = shift(near_left, "x", NX, -1)
    stream_late, _ = lax.optimization_barrier((stream, near_right))
    back = []
    for m in range(2):
        first, second = stream_late[:, :width], stream_late[:, width:]
        sent = jnp.where(odd, second, first) if m == 0 else jnp.where(odd, first, second)
        back.append(lax.ppermute(sent, axes, work_to_natural(m)))
    back = jnp.stack([jnp.where(odd, back[1], back[0]), jnp.where(odd, back[0], back[1])])
    kept, given = (
        lax.dynamic_slice_in_dim(back, side * half, half, 1) for side in (depth, 1 - depth)
    )
    stream_out = in_order(depth, kept, swap(given), 2)
    (hidden,) = small_call(
        last_kernel,
        [(1, half, w2.shape[1] // 2)],
        mine,
        mine_square,
        swap(mine_sent),
        from_left,
        from_right,
    )
    return (hidden, stream_out)


def solution(mesh):
    fine = Mesh(mesh.devices.reshape(2, NX, NY, NZ), ("depth", "x", "y", "col"))
    row = ("x", "y")
    return jax.shard_map(
        per_device,
        mesh=fine,
        in_specs=(
            P(row, "depth", "col"),
            P(row, "depth", "col"),
            P(row, "depth", "col"),
            P("col", "depth", row),
            P(row),
            P("col", row),
            P(row, "col"),
            P(row, "col"),
        ),
        out_specs=(P(row, "depth", "col"), P("col", "depth", row)),
        check_vma=False,
    )
```

```python
import functools
import jax
import jax.numpy as jnp
from jax import lax
from jax.experimental import pallas as pl
from jax.experimental.pallas import tpu as pltpu
from jax.sharding import Mesh, PartitionSpec as P

D = 8192
DH = 128
GROUP = 8
NX = 4
NY = 4
NZ = 8
EXTRA = 16

eps_norm = 1e-05
masked_score = -1e30
bf16 = jnp.bfloat16
f32 = jnp.float32
VMEM_BYTES = 24 * 1024 * 1024
SMALL_COST = pl.CostEstimate(flops=1024, bytes_accessed=1024, transcendentals=0)


def shift(value, axis, size, by):
    return lax.ppermute(value, axis, [(i, (i + by) % size) for i in range(size)])


def in_hbm(value):
    return pltpu.with_memory_space_constraint(value, pltpu.HBM)


def swap(value):
    return shift(value, "depth", 2, 1)


def attend_kernel(where_ref, q_ref, kv_ref, out_ref):
    depth = where_ref[0]
    half = q_ref.shape[0]
    keys = jnp.concatenate([kv_ref[0, :, :DH], kv_ref[1, :, :DH]], axis=0)
    values = jnp.concatenate([kv_ref[0, :, DH:], kv_ref[1, :, DH:]], axis=0)
    rows = jnp.concatenate([q_ref[:, h * DH : (h + 1) * DH] for h in range(GROUP)], axis=0)
    scores = lax.dot_general(
        rows, keys, (((1,), (1,)), ((), ())), preferred_element_type=f32
    ) * DH ** (-0.5)
    shape = scores.shape
    position = lax.broadcasted_iota(jnp.int32, shape, 0) % half + depth * half
    allowed = lax.broadcasted_iota(jnp.int32, shape, 1) <= position
    scores = jnp.where(allowed, scores, masked_score)
    top = jnp.max(scores, axis=-1, keepdims=True)
    expo = jnp.exp(scores - top)
    totals = jnp.sum(expo, axis=-1, keepdims=True)
    mixed = jnp.dot(expo.astype(bf16), values, preferred_element_type=f32) / totals
    mixed = mixed.astype(bf16)
    for h in range(GROUP):
        out_ref[:, h * DH : (h + 1) * DH] = mixed[h * half : (h + 1) * half]


def attend(where, queries, kv):
    half, features = queries.shape
    length = 2 * half
    return pl.pallas_call(
        attend_kernel,
        in_specs=[pl.BlockSpec(memory_space=pltpu.SMEM)]
        + [pl.BlockSpec(memory_space=pltpu.VMEM)] * 2,
        out_specs=pl.BlockSpec(memory_space=pltpu.VMEM),
        out_shape=jax.ShapeDtypeStruct((half, features), bf16),
        compiler_params=pltpu.CompilerParams(vmem_limit_bytes=VMEM_BYTES),
        cost_estimate=SMALL_COST,
    )(where, queries, kv)


ANYWHERE = pl.BlockSpec(memory_space=pl.ANY)
SCALARS = pl.BlockSpec(memory_space=pltpu.SMEM)
WHOLE = pl.BlockSpec(memory_space=pltpu.VMEM)


def out_kernel(where_ref, *refs):
    own, other, w_ref, pieces = refs[:4], refs[4:8], refs[8], refs[9:12]
    out_ref, far_a_ref, far_b_ref, att_buf, w_buf, att_sem, w_sem = refs[12:]
    depth, z, x, y = (where_ref[i] for i in range(4))
    rows = own[0].shape[0]
    width = w_buf.shape[2] // 2
    first = []
    for k in range(NX):
        for i, (side, ref) in enumerate(((depth, own[k]), (1 - depth, other[k]))):
            place = pl.ds(pl.multiple_of((2 * k + side) * rows, rows), rows)
            first.append(pltpu.make_async_copy(ref, att_buf.at[place], att_sem.at[k, i]))
    columns = pl.ds(pl.multiple_of(depth * width, width), width)
    copies = []
    for j, source in enumerate([w_ref.at[:, columns], *pieces]):
        place = w_buf.at[j // 2, :, pl.ds((j % 2) * width, width)]
        copies.append(pltpu.make_async_copy(source, place, w_sem.at[j]))
    for copy in first:
        copy.start()
    for copy in copies:
        copy.start()
    for copy in first:
        copy.wait()
    for j in range(0, NY, 2):
        copies[j].wait()
        copies[j + 1].wait()
        total = jnp.dot(att_buf[...], w_buf[j // 2], preferred_element_type=f32).astype(bf16)
        for i in range(2):
            block = (y + j + i) % NY
            held = pl.ds(pl.multiple_of((block % 2) * width, width), width)
            for k in range(NX):
                place = 2 * ((x + k) % NX) + block // 2
                out_ref[place, :, held] = total[
                    2 * k * rows : 2 * (k + 1) * rows, i * width : (i + 1) * width
                ]
    far = (z + NZ // 2) % NZ
    far_a_ref[...] = out_ref[far, :rows]
    far_b_ref[...] = out_ref[far, rows:]


def out_project(where, own, other, w_out, pieces):
    rows, features = own[0].shape
    width = w_out.shape[1] // 2
    return pl.pallas_call(
        out_kernel,
        in_specs=[SCALARS] + [ANYWHERE] * 12,
        out_specs=[WHOLE] * 3,
        out_shape=[jax.ShapeDtypeStruct((NZ, 2 * rows, 2 * width), bf16)]
        + [jax.ShapeDtypeStruct((rows, 2 * width), bf16)] * 2,
        scratch_shapes=[
            pltpu.VMEM((2 * NX * rows, features), bf16),
            pltpu.VMEM((NY // 2, features, 2 * width), bf16),
            pltpu.SemaphoreType.DMA((NX, 2)),
            pltpu.SemaphoreType.DMA((NY,)),
        ],
        compiler_params=pltpu.CompilerParams(vmem_limit_bytes=VMEM_BYTES),
        cost_estimate=SMALL_COST,
    )(where, *own, *other, in_hbm(w_out), *pieces)


def put_squares(ref, row):
    rows = ref.shape[0] - EXTRA
    high = row.astype(bf16)
    rest = row - high.astype(f32)
    middle = rest.astype(bf16)
    low = (rest - middle.astype(f32)).astype(bf16)
    index = lax.broadcasted_iota(jnp.int32, row.shape, 0)
    first = jnp.where(index == 0, high.astype(f32), jnp.where(index == 1, middle.astype(f32), 0.0))
    first = jnp.where(index == 2, low.astype(f32), first)
    both = jnp.concatenate([first, jnp.zeros_like(first)], axis=0).astype(bf16)
    ref[rows:] = jnp.zeros((EXTRA, ref.shape[1]), bf16)
    ref[rows:, : row.shape[1]] = both


def get_squares(ref, count):
    held = ref[ref.shape[0] - EXTRA :, :count].astype(f32)
    return jnp.broadcast_to(jnp.sum(held, axis=0, keepdims=True), (8, count))


def gate_kernel(seqs, where_ref, *refs):
    blocks, weight_ref = refs[:NZ], refs[NZ]
    outs = refs[NZ + 1 : -4]
    w_buf, x_buf, w_sem, x_sem = refs[-4:]
    depth, z, x = (where_ref[i] for i in range(3))
    rows, pair = blocks[0].shape[0] // 2, blocks[0].shape[1]
    chunks, _, chunk = w_buf.shape

    def rows_copy(ref, i, h, side):
        place = depth if side == 0 else 1 - depth
        return pltpu.make_async_copy(
            ref.at[pl.ds(pl.multiple_of(place * rows, rows), rows)],
            x_buf.at[pl.ds((2 * i + side) * rows, rows), pl.ds(h * pair, pair)],
            x_sem.at[i, h, side],
        )

    def weight_copy(c):
        return pltpu.make_async_copy(
            weight_ref.at[:, pl.ds(c * chunk, chunk)], w_buf.at[c], w_sem.at[c]
        )

    for c in range(chunks):
        weight_copy(c).start()
    for h in range(2):
        for i, k in enumerate(seqs):
            ring = (2 * ((x + k) % NX) + h - z + NZ) % NZ
            for j in range(NZ):

                @pl.when(ring == j)
                def _():
                    rows_copy(blocks[j], i, h, 0).start()
                    rows_copy(blocks[j], i, h, 1).start()

    for h in range(2):
        for i in range(len(seqs)):
            for side in range(2):
                rows_copy(blocks[0], i, h, side).wait()
    squares = 0.0
    for n in range(0, 2 * pair, DH):
        wide = x_buf[:, n : n + DH].astype(f32)
        squares = squares + wide * wide
    column = jnp.sum(squares, axis=1, keepdims=True)
    column = jnp.broadcast_to(column, squares.shape)
    for i in range(len(seqs)):
        start = 2 * i * rows
        outs[3 * i + 1][...] = column[start : start + rows].T[:8]
        put_squares(outs[3 * i + 2], column[start + rows : start + 2 * rows].T[:8])
    for c in range(chunks):
        weight_copy(c).wait()
        total = jnp.dot(x_buf[...], w_buf[c], preferred_element_type=f32).astype(bf16)
        held = slice(c * chunk, (c + 1) * chunk)
        for i in range(len(seqs)):
            start = 2 * i * rows
            outs[3 * i][:, held] = total[start : start + rows]
            outs[3 * i + 2][:rows, held] = total[start + rows : start + 2 * rows]


def gate_products(seqs, where, blocks, weights):
    rows, pair = blocks[0].shape
    rows = rows // 2
    features, width = weights.shape
    n = len(seqs)
    chunks = 4
    results = pl.pallas_call(
        functools.partial(gate_kernel, seqs),
        in_specs=[SCALARS] + [ANYWHERE] * (NZ + 1),
        out_specs=[WHOLE] * (3 * n),
        scratch_shapes=[
            pltpu.VMEM((chunks, features, width // chunks), bf16),
            pltpu.VMEM((2 * n * rows, 2 * pair), bf16),
            pltpu.SemaphoreType.DMA((chunks,)),
            pltpu.SemaphoreType.DMA((n, 2, 2)),
        ],
        out_shape=[
            jax.ShapeDtypeStruct((rows, width), bf16),
            jax.ShapeDtypeStruct((8, rows), f32),
            jax.ShapeDtypeStruct((rows + EXTRA, width), bf16),
        ]
        * n,
        compiler_params=pltpu.CompilerParams(vmem_limit_bytes=VMEM_BYTES),
        cost_estimate=SMALL_COST,
    )(where, *blocks, in_hbm(weights))
    return [results[3 * i : 3 * i + 3] for i in range(n)]


def far_kernel(own_ref, square_ref, other_ref, out_ref):
    rows = own_ref.shape[0]
    out_ref[:rows] = (own_ref[...].astype(f32) + other_ref[:rows].astype(f32)).astype(bf16)
    put_squares(out_ref, square_ref[...] + get_squares(other_ref, rows))


def near_kernel(where_ref, far_ref, *refs):
    rows = refs[0].shape[0]
    for i in range(2):
        own_ref, square_ref, other_ref = refs[3 * i : 3 * i + 3]
        out_ref = refs[6 + i]
        mine = where_ref[0] == i
        total = own_ref[...].astype(f32) + other_ref[:rows].astype(f32)
        squares = square_ref[...] + get_squares(other_ref, rows)

        @pl.when(mine)
        def _():
            out_ref[:rows] = (total + far_ref[:rows].astype(f32)).astype(bf16)
            put_squares(out_ref, squares + get_squares(far_ref, rows))

        @pl.when(jnp.logical_not(mine))
        def _():
            out_ref[:rows] = total.astype(bf16)
            put_squares(out_ref, squares)


def last_kernel(own_ref, square_ref, other_ref, left_ref, right_ref, out_ref):
    rows, width = own_ref.shape
    units = width // 2
    squares = square_ref[...]
    total = own_ref[...].astype(f32)
    for ref in (other_ref, left_ref, right_ref):
        squares = squares + get_squares(ref, rows)
        total = total + ref[:rows].astype(f32)
    squares = jnp.broadcast_to(squares[:1], (DH, rows)).T[:, :1]
    total = total * lax.rsqrt(squares / D + eps_norm)
    gate, up = total[:, :units], total[:, units:]
    out_ref[0] = (gate / (1.0 + jnp.exp(-gate)) * up).astype(bf16)


def small_call(kernel, shapes, *operands):
    first = operands[0].dtype == jnp.int32
    return pl.pallas_call(
        kernel,
        in_specs=[SCALARS] * first + [WHOLE] * (len(operands) - first),
        out_specs=[WHOLE] * len(shapes),
        out_shape=[jax.ShapeDtypeStruct(shape, bf16) for shape in shapes],
        compiler_params=pltpu.CompilerParams(vmem_limit_bytes=VMEM_BYTES),
        cost_estimate=SMALL_COST,
    )(*operands)


def ring_kernel(offset, where_ref, parts_ref, right_ref, left_ref, *refs):
    z = where_ref[1]
    buf, sem = refs[-2:]
    if offset:
        sources = (parts_ref.at[(z + offset) % NZ], parts_ref.at[(z + NZ - offset) % NZ])
    else:
        sources = (parts_ref.at[z], refs[0])
    arrived = (right_ref, left_ref)
    starts = (0, buf.shape[1] - left_ref.shape[0])
    copies = []
    for i in range(2):
        copies.append(pltpu.make_async_copy(sources[i], buf.at[i], sem.at[i]))
        place = buf.at[2 + i, pl.ds(starts[i], arrived[i].shape[0])]
        copies.append(pltpu.make_async_copy(arrived[i], place, sem.at[2 + i]))
    for copy in copies:
        copy.start()
    for copy in copies:
        copy.wait()
    if not offset:
        refs[1][...] = (
            (buf[0].astype(f32) + buf[2].astype(f32) + buf[3].astype(f32)) + buf[1].astype(f32)
        ).astype(bf16)
        return
    for i in range(2):
        rows = arrived[i].shape[0]
        held = pl.ds(starts[i], rows)
        total = buf[i, held].astype(f32) + buf[2 + i, held].astype(f32)
        refs[i][held] = total.astype(bf16)
        if rows < buf.shape[1]:
            rest = pl.ds(rows - starts[i], rows)
            refs[i][rest] = buf[i, rest]


def ring_add(offset, where, parts, right, left, residual=None):
    _, rows, width = parts.shape
    extra = [] if residual is None else [residual]
    return pl.pallas_call(
        functools.partial(ring_kernel, offset),
        in_specs=[SCALARS] + [ANYWHERE] * (3 + len(extra)),
        out_specs=[WHOLE] * (2 - len(extra)),
        scratch_shapes=[pltpu.VMEM((4, rows, width), bf16), pltpu.SemaphoreType.DMA((4,))],
        out_shape=[jax.ShapeDtypeStruct((rows, width), bf16)] * (2 - len(extra)),
        compiler_params=pltpu.CompilerParams(vmem_limit_bytes=VMEM_BYTES),
        cost_estimate=SMALL_COST,
    )(where, parts, right, left, *extra)


def reduce_scatter_z(where, parts, far_a, far_b, residual):
    right = shift(far_a, "col", NZ, 1)
    left = shift(far_b, "col", NZ, -1)
    (right, left), residual = lax.optimization_barrier(((right, left), residual))
    for offset in (3, 2, 1):
        right, left = ring_add(offset, where, parts, right, left)
        right = shift(right, "col", NZ, 1)
        left = shift(left, "col", NZ, -1)
    return ring_add(0, where, parts, right, left, residual)[0]


def all_gather_z(block):
    cut = block.shape[0] // 2
    right, left = [block], [block]
    for _ in range(3):
        got = (shift(right[-1], "col", NZ, 1), shift(left[-1], "col", NZ, -1))
        got = lax.optimization_barrier(got)
        right.append(got[0])
        left.append(got[1])
    far_a = shift(right[3][:cut], "col", NZ, 1)
    far_b = shift(left[3][cut:], "col", NZ, -1)
    far = jnp.concatenate([far_a, far_b], axis=0)
    return [block, left[1], left[2], left[3], far, right[3], right[2], right[1]]


def work_to_natural(m):
    pairs = []
    for y in range(NY):
        for z in range(NZ):
            there = 2 * (z % 2) + (m ^ (y % 2)), 2 * (z // 2) + y // 2
            pairs.append((y * NZ + z, there[0] * NZ + there[1]))
    return pairs


def in_order(depth, same, other, axis):
    return jnp.where(
        depth == 0,
        jnp.concatenate([same, other], axis=axis),
        jnp.concatenate([other, same], axis=axis),
    )


def per_device(queries, key_states, value_states, residual, gain, w_out, w_gate, w_up):
    half = queries.shape[1]
    depth, x, y, z = (lax.axis_index(name) for name in ("depth", "x", "y", "col"))
    odd = (y % 2) == 1
    where = jnp.stack([depth, z, x, y]).astype(jnp.int32)
    block = w_out.shape[1]
    width = block // 2

    wo_half = lax.dynamic_slice_in_dim(w_out, depth * width, width, 1)
    wo_next = shift(wo_half, "y", NY, -1)
    wo_last = shift(wo_half, "y", NY, 1)
    pairs = []
    for i in range(NY):
        pairs.append((i, (i - 1) % NY))
    for i in range(NY):
        pairs.append((NY + i, NY + (i + 1) % NY))
    wo_far = lax.ppermute(jnp.where(depth == 0, wo_next, wo_last), ("depth", "y"), pairs)

    kv = jnp.concatenate([key_states[0], value_states[0]], axis=1)
    kv = lax.all_gather(kv, "depth", axis=0)
    attended = attend(where, queries[0], kv)
    own = [
        attended,
        shift(attended, "x", NX, -1),
        shift(attended, "x", NX, 2),
        shift(attended, "x", NX, 1),
    ]
    last_own, wo_far = lax.optimization_barrier((own[2], wo_far))
    other = [swap(value) for value in (own[0], own[1], last_own, own[3])]

    axes = ("y", "col")
    kept, given = (
        lax.dynamic_slice_in_dim(residual, side * width, width, 2) for side in (depth, 1 - depth)
    )
    both = in_order(depth, kept, swap(given), 1)
    sent = [jnp.where(odd, both[1 - m], both[m]) for m in range(2)]
    sent, _ = lax.optimization_barrier((sent, own[1]))
    got = [
        lax.ppermute(sent[m], axes, [(b, a) for a, b in work_to_natural(m)]) for m in range(2)
    ]
    res_work = jnp.concatenate(
        [jnp.where(odd, got[1], got[0]), jnp.where(odd, got[0], got[1])], axis=1
    )

    rows = w_gate.shape[0] // 2
    held = [
        lax.dynamic_slice_in_dim(value, depth * rows, rows, 0) for value in (w_gate, w_up, gain[:, None])
    ]
    w2_half = jnp.concatenate(
        [(weights.astype(f32) * held[2]).astype(bf16) for weights in held[:2]], axis=1
    )
    w2_half, _ = lax.optimization_barrier((w2_half, (other, wo_far, got)))
    w2 = lax.all_gather(w2_half, "y", axis=0, tiled=True)

    pieces = [wo_next, wo_far, wo_last]
    parts, far_a, far_b = out_project(where, own, other, w_out, pieces)
    stream = reduce_scatter_z(where, parts, far_a, far_b, res_work)
    blocks = all_gather_z(stream)

    ((far, far_square, sent),) = gate_products((2,), where, blocks, w2)
    payload = (half + EXTRA, w2.shape[1])
    (far,) = small_call(far_kernel, [payload], far, far_square, swap(sent))
    after_far, far = lax.optimization_barrier((where, far))
    pairs = []
    for i in range(NX):
        pairs.append((i, (i + 1) % NX))
    for i in range(NX):
        pairs.append((NX + i, NX + (i - 1) % NX))
    far = lax.ppermute(far, ("depth", "x"), pairs)
    (right, right_square, right_sent), (left, left_square, left_sent) = gate_products(
        (1, 3), after_far, blocks, w2
    )
    ((mine, mine_square, mine_sent),) = gate_products((0,), where, blocks, w2)
    near_right, near_left = small_call(
        near_kernel,
        [payload] * 2,
        where,
        far,
        right,
        right_square,
        swap(right_sent),
        left,
        left_square,
        swap(left_sent),
    )
    from_left = shift(near_right, "x", NX, 1)
    from_right = shift(near_left, "x", NX, -1)
    stream_late, _ = lax.optimization_barrier((stream, near_right))
    back = []
    for m in range(2):
        first, second = stream_late[:, :width], stream_late[:, width:]
        sent = jnp.where(odd, second, first) if m == 0 else jnp.where(odd, first, second)
        back.append(lax.ppermute(sent, axes, work_to_natural(m)))
    back = jnp.stack([jnp.where(odd, back[1], back[0]), jnp.where(odd, back[0], back[1])])
    kept, given = (
        lax.dynamic_slice_in_dim(back, side * half, half, 1) for side in (depth, 1 - depth)
    )
    stream_out = in_order(depth, kept, swap(given), 2)
    (hidden,) = small_call(
        last_kernel,
        [(1, half, w2.shape[1] // 2)],
        mine,
        mine_square,
        swap(mine_sent),
        from_left,
        from_right,
    )
    return (hidden, stream_out)


def solution(mesh):
    fine = Mesh(mesh.devices.reshape(2, NX, NY, NZ), ("depth", "x", "y", "col"))
    row = ("x", "y")
    return jax.shard_map(
        per_device,
        mesh=fine,
        in_specs=(
            P(row, "depth", "col"),
            P(row, "depth", "col"),
            P(row, "depth", "col"),
            P("col", "depth", row),
            P(row),
            P("col", row),
            P(row, "col"),
            P(row, "col"),
        ),
        out_specs=(P(row, "depth", "col"), P("col", "depth", row)),
        check_vma=False,
    )
```
